32 devices in a mesh: gx: 8 (over z, x), gy: 4 (over y, core).
Axes of the slice: x: 2, y: 2, z: 4, core: 2. Of those that a mesh axis runs over, the one named last changes fastest.
Arguments:
- f_in: float32 [19, 16, 128, 512], P(None, None, 'gx', 'gy')
- rotor_place: int32 [40, 3], replicated, may hold values from 0 to 15, as said below
- marker_cell: int32 [40, 8192], replicated, may hold values from 16384 to 505663, as said below
- pitch_phase: int32 [40, 2], replicated, may hold values from 0 to 63
- blade_area: float32 [8, 4, 2, 8192], P('gx', 'gy'), may hold values from 0.3 to 1.2
- blade_twist: float32 [8, 4, 2, 8192], P('gx', 'gy'), may hold values from -0.6 to 0.6
- blade_speed: float32 [8, 4, 2, 8192], P('gx', 'gy'), may hold values from 1.5 to 3
- blade_angle: float32 [8, 4, 2, 8192], P('gx', 'gy'), may hold values from -3.14 to 3.14, as said below
- filt_in: float32 [8, 4, 2, 3, 8192], P('gx', 'gy'), may hold values from -1.5 to 1.5
Outputs:
- f_out: float32 [19, 16, 128, 512], P(None, None, 'gx', 'gy')
- loads_out: float32 [8, 4, 2, 3, 8192], P('gx', 'gy')
- filt_out: float32 [8, 4, 2, 3, 8192], P('gx', 'gy')
The draws below stay inside these ranges and needn't reach their ends.
Inputs may be any that keep to these rules, and one draw needn't show every extreme that they name: `rotor_place`: column 0 is a streamwise tile holding at most 5 rotors, some exactly 5; column 1 a plane 0 to 15; column 2 the owner's spanwise tile. Every streamwise tile holds 2 or more rotors; one owner holds at most 2 rotors, exactly 2 in every streamwise tile. `marker_cell`: all stencil cells of one rotor lie within two neighbouring spanwise tiles and within levels 0 to 15; a rotor's stencils may cover one or two tiles. `blade_angle`: azimuths in radians.
All inputs are finite; a program needn't handle non-finite values.
Results may differ from the reference program's by a relative error of at most 0.0003.
Values sent between devices are 32-bit elements; how exact they have to be, the bound alone decides.
No kernel may reach another device: no remote copies, remote signals or barrier semaphores. Data moves between devices by JAX's collectives and lax.ppermute only.
A program may use at most 128 MiB of HBM per device.

```python
import math
import jax
import jax.numpy as jnp
import numpy as np
from jax import lax

CX = 16
CY = 128
Z = 16
M = 8192
ROTORS = 40
STEPS = 2
OSLOT = 2
PHASES = 64
TX = 8
TY = 4
NX = 128
NY = 512
HALF = 48


LATTICE_DIRS = np.array([[0, 0, 0], [1, 0, 0], [-1, 0, 0], [0, 1, 0], [0, -1, 0], [0, 0, 1], [0, 0, -1], [1, 1, 0], [-1, -1, 0], [1, -1, 0], [-1, 1, 0], [1, 0, 1], [-1, 0, -1], [1, 0, -1], [-1, 0, 1], [0, 1, 1], [0, -1, -1], [0, 1, -1], [0, -1, 1]])


LATTICE_WEIGHTS = np.array([1.0 / 3.0] + [1.0 / 18.0] * 6 + [1.0 / 36.0] * 12)


def geometry(key):
    base_key = jax.random.fold_in(key, 7)
    subkeys = jax.random.split(base_key, 8)
    shuffle = jax.random.permutation(subkeys[0], ROTORS)
    street = (jnp.argsort(shuffle) % TX).astype(jnp.int32)
    rotor_ids = jnp.arange(ROTORS, dtype=jnp.int32)
    earlier = rotor_ids[None, :] < rotor_ids[:, None]
    same_row = street[:, None] == street[None, :]
    row_rank = jnp.sum((earlier & same_row).astype(jnp.int32), axis=1)
    first_owner = jax.random.randint(subkeys[1], (TX,), 0, TY)
    owner_y = ((first_owner[street] + row_rank // 2) % TY).astype(jnp.int32)
    plane_x = jax.random.randint(subkeys[2], (ROTORS,), 0, CX)
    plane_x = plane_x.at[0].set(CX - 1)
    first_tile = jax.random.randint(subkeys[3], (ROTORS,), 0, TY - 1)
    first_tile = first_tile.at[0].set(TY - 2).at[1].set(0)
    offset = jax.random.randint(subkeys[4], (ROTORS,), -(CY // 2), CY // 2 + 1)
    offset = offset.at[0].set(CY // 2).at[1].set(-(CY // 2))
    centre = (first_tile + 1) * CY + offset
    cell_y = centre[:, None] - HALF + jax.random.randint(subkeys[5], (ROTORS, M), 0, 2 * HALF - 2)
    cell_y = cell_y.at[:, 0].set(centre - HALF).at[:, 1].set(centre + HALF - 3)
    cell_z = jax.random.randint(subkeys[6], (ROTORS, M), 0, Z - 3)
    cell_z = cell_z.at[0, 1].set(Z - 4).at[1, 0].set(0)
    fractions = jax.random.randint(subkeys[7], (ROTORS, M), 0, 64)
    fractions = fractions.at[0, 1].set(63).at[1, 0].set(0)
    cell_codes = ((cell_y * Z + cell_z) * 64 + fractions).astype(jnp.int32)
    place = jnp.stack([street, plane_x.astype(jnp.int32), owner_y], axis=1)
    return (place, cell_codes)


def draw_rotor_place(key, part):
    place, cell_codes = geometry(key)
    return place


def draw_marker_cell(key, part):
    place, cell_codes = geometry(key)
    return cell_codes


def draw_blade_angle(key, part):
    subkeys = jax.random.split(jax.random.fold_in(key, 11), 3)
    side = (2 * jax.random.randint(subkeys[0], (TX, TY, OSLOT, 1), 0, 2) - 1).astype(jnp.float32)
    centre_spread = 0.4
    marker_spread = 0.5
    centre_shift = jax.random.uniform(subkeys[1], (TX, TY, OSLOT, 1), jnp.float32, -centre_spread, centre_spread)
    wobble = jax.random.uniform(subkeys[2], (TX, TY, OSLOT, M), jnp.float32, -marker_spread, marker_spread)
    return side * (0.5 * math.pi + centre_shift) + wobble


def draw_f_in(key, part):
    subkeys = jax.random.split(key, 7)
    shape = (Z, NX, NY)
    x_ids = jnp.arange(NX, dtype=jnp.int32)
    phase = jax.random.randint(subkeys[5], (), 0, 2)
    pattern = (1 - 2 * ((x_ids + phase) % 2)).astype(jnp.float32)
    density = jax.random.uniform(subkeys[0], shape, jnp.float32, 0.9, 1.1)
    plane_noise = jax.random.uniform(subkeys[6], (NX,), jnp.float32, -0.03, 0.03)
    axial_speed = 0.08 + (0.07 * pattern + plane_noise)[None, :, None] + jax.random.uniform(subkeys[1], shape, jnp.float32, -0.03, 0.03)
    span_speed = jax.random.uniform(subkeys[2], shape, jnp.float32, -0.05, 0.05)
    lift_speed = jax.random.uniform(subkeys[3], shape, jnp.float32, -0.05, 0.05)
    jitter = jax.random.uniform(subkeys[4], (19,) + shape, jnp.float32, -0.05, 0.05)
    lattice = jnp.asarray(LATTICE_DIRS, jnp.float32)
    weights = jnp.asarray(LATTICE_WEIGHTS, jnp.float32)[:, None, None, None]
    project = lattice[:, 0][:, None, None, None] * axial_speed[None] + lattice[:, 1][:, None, None, None] * span_speed[None] + lattice[:, 2][:, None, None, None] * lift_speed[None]
    speed_sq = axial_speed * axial_speed + span_speed * span_speed + lift_speed * lift_speed
    equilibrium = weights * density[None] * (1.0 + 3.0 * project + 4.5 * project * project - 1.5 * speed_sq[None])
    return equilibrium * (1.0 + jitter)


def set_ends(result, own_key, low, high):
    shape = result.shape
    spot = [jax.random.randint(jax.random.fold_in(own_key, axis), (), 0, shape[axis]) for axis in range(len(shape))]
    result = result.at[tuple(spot)].set(low)
    longest = shape.index(max(shape))
    spot[longest] = (spot[longest] + 1) % shape[longest]
    return result.at[tuple(spot)].set(high)


def block_scale(rng, extent, shards, smallest, high):
    gain = 1.0
    for axis_at, shards_of in shards:
        draws = jax.random.uniform(jax.random.fold_in(jax.random.fold_in(rng, 6), axis_at), (shards_of,), jnp.float32, smallest / len(shards), high / len(shards))
        gain = gain * jnp.repeat(jnp.exp(draws), extent[axis_at] // shards_of).reshape((-1,) + (1,) * (len(extent) - 1 - axis_at))
    return gain


def centred(stream_key, shape, scale, reach, pieces=(), kind=jnp.bfloat16):
    gain = block_scale(stream_key, shape, pieces, -0.22, 0.18) if pieces else 1.0
    drawn = jax.random.normal(stream_key, shape, jnp.float32) * scale * gain
    return jnp.minimum(jnp.maximum(drawn, -reach), reach).astype(kind)


def setup_inputs(seed: int = 0) -> dict:
    key_of = jax.random.split(jax.random.key(seed), 10)
    return {
        "f_in": draw_f_in(jax.random.fold_in(key_of[9], 71), 0),
        "rotor_place": draw_rotor_place(jax.random.fold_in(key_of[9], 71), 0),
        "marker_cell": draw_marker_cell(jax.random.fold_in(key_of[9], 71), 0),
        "pitch_phase": set_ends(jax.random.randint(key_of[3], (ROTORS, STEPS), 0, PHASES), jax.random.fold_in(key_of[3], 1), 0, PHASES - 1).astype(jnp.int32),
        "blade_area": jnp.clip(jnp.exp(math.log(1.2) - 1.3862944 * jax.random.uniform(key_of[4], (TX, TY, OSLOT, M), jnp.float32) ** block_scale(key_of[4], (TX, TY, OSLOT, M), ((0, 8), (1, 4)), -0.2, 0.2)), 0.3, 1.2),
        "blade_twist": jnp.clip(jax.random.uniform(key_of[5], (TX, TY, OSLOT, M), jnp.float32, -0.6, 0.6) * block_scale(key_of[5], (TX, TY, OSLOT, M), ((0, 8), (1, 4)), -0.4, 0.0), -0.6, 0.6),
        "blade_speed": jnp.clip(jnp.exp(math.log(3.0) - 0.6931472 * jax.random.uniform(key_of[6], (TX, TY, OSLOT, M), jnp.float32) ** block_scale(key_of[6], (TX, TY, OSLOT, M), ((0, 8), (1, 4)), -0.2, 0.2)), 1.5, 3.0),
        "blade_angle": draw_blade_angle(jax.random.fold_in(key_of[9], 71), 0),
        "filt_in": centred(key_of[8], (TX, TY, OSLOT, 3, M), 0.1, 1.5, ((0, 8), (1, 4)), jnp.float32),
    }


LATTICE_DIRS = np.array([[0, 0, 0], [1, 0, 0], [-1, 0, 0], [0, 1, 0], [0, -1, 0], [0, 0, 1], [0, 0, -1], [1, 1, 0], [-1, -1, 0], [1, -1, 0], [-1, 1, 0], [1, 0, 1], [-1, 0, -1], [1, 0, -1], [-1, 0, 1], [0, 1, 1], [0, -1, -1], [0, 1, -1], [0, -1, 1]])
OPPOSITE = [0, 2, 1, 4, 3, 6, 5, 8, 7, 10, 9, 12, 11, 14, 13, 16, 15, 18, 17]
LATTICE_WEIGHTS = np.array([1.0 / 3.0] + [1.0 / 18.0] * 6 + [1.0 / 36.0] * 12)
OMEGA = 1.0 / 0.6
SPREAD = 0.01
MIX = 0.5
PITCH_AMP = 0.2

def peskin(offsets):
    distance = jnp.abs(offsets)
    near_arg = jnp.maximum(1.0 + 4.0 * distance - 4.0 * distance * distance, 1.0)
    far_arg = jnp.maximum(-7.0 + 12.0 * distance - 4.0 * distance * distance, 1.0)
    near_part = (3.0 - 2.0 * distance + jnp.sqrt(near_arg)) / 8.0
    far_part = (5.0 - 2.0 * distance - jnp.sqrt(far_arg)) / 8.0
    return jnp.where(distance <= 1.0, near_part, far_part)

def dense_rows(anchor, weights, width, start):
    column = jnp.arange(width, dtype=jnp.int32)[None, :] + start
    gap = column - anchor[:, None]
    summed = jnp.zeros(gap.shape, jnp.float32)
    for corner in range(4):
        summed = summed + jnp.where(gap == corner, weights[corner][:, None], 0.0)
    return summed

def stencil_tables(cell_codes, levels, width, start):
    fraction_z = (cell_codes % 8).astype(jnp.float32) / 8.0
    fraction_y = (cell_codes // 8 % 8).astype(jnp.float32) / 8.0
    cell_z = (cell_codes // 64 % levels).astype(jnp.int32)
    cell_y = (cell_codes // (64 * levels)).astype(jnp.int32)
    weights_y = [peskin(corner - 1.0 - fraction_y) for corner in range(4)]
    weights_z = [peskin(corner - 1.0 - fraction_z) for corner in range(4)]
    across = dense_rows(cell_y, weights_y, width, start)
    upward = dense_rows(cell_z, weights_z, levels, jnp.int32(0))
    return (across, upward)

def sample_section(section, across, upward):
    levels = section.shape[1]
    width = section.shape[2]
    flattened = jnp.transpose(section, (2, 0, 1)).reshape(width, 3 * levels)
    partial_value = jnp.dot(across, flattened, precision=lax.Precision.HIGHEST, preferred_element_type=jnp.float32)
    partial_value = partial_value.reshape(across.shape[0], 3, levels)
    return jnp.transpose(lax.optimization_barrier(jnp.sum(partial_value * upward[:, None, :], axis=2)))

def spread_section(marker_loads, across, upward):
    markers = upward.shape[0]
    levels = upward.shape[1]
    weighted = (upward[:, None, :] * jnp.transpose(marker_loads)[:, :, None]).reshape(markers, 3 * levels)
    section = lax.dot_general(weighted, across, (((0,), (0,)), ((), ())), precision=lax.Precision.HIGHEST, preferred_element_type=jnp.float32)
    return -SPREAD * section.reshape(3, levels, across.shape[1])

def pitch_angles(phases):
    return PITCH_AMP * jnp.sin(2.0 * math.pi * phases.astype(jnp.float32) / PHASES)

def blade_loads(filtered, area, twist, speed, angle, pitch):
    axial_speed = filtered[..., 0, :]
    sin_t = jnp.sin(angle)
    cos_t = jnp.cos(angle)
    tangent = speed + sin_t * filtered[..., 1, :] - cos_t * filtered[..., 2, :]
    square = axial_speed * axial_speed + tangent * tangent
    magnitude = jnp.sqrt(square)
    sin_p = axial_speed / magnitude
    cos_p = tangent / magnitude
    blade_pitch = twist + pitch
    sin_a = sin_p * jnp.cos(blade_pitch) - cos_p * jnp.sin(blade_pitch)
    cos_a = cos_p * jnp.cos(blade_pitch) + sin_p * jnp.sin(blade_pitch)
    lift_coef = 2.0 * math.pi * sin_a * cos_a
    drag_coef = 0.02 + sin_a * sin_a
    dynamic = 0.5 * area * square
    normal = dynamic * (lift_coef * cos_p + drag_coef * sin_p)
    tangential = dynamic * (lift_coef * sin_p - drag_coef * cos_p)
    return jnp.stack([normal, -tangential * sin_t, tangential * cos_t], axis=-2)

def velocity(populations):
    lattice = jnp.asarray(LATTICE_DIRS, jnp.float32)
    density = lax.optimization_barrier(jnp.sum(populations, axis=0))
    parts = [lax.optimization_barrier(jnp.sum(populations * lattice[:, axis][:, None, None, None], axis=0)) / density for axis in range(3)]
    return jnp.stack(parts)

def collide(populations, force_field):
    lattice = jnp.asarray(LATTICE_DIRS, jnp.float32)
    weights = jnp.asarray(LATTICE_WEIGHTS, jnp.float32)[:, None, None, None]
    density = lax.optimization_barrier(jnp.sum(populations, axis=0))
    columns = [lattice[:, axis][:, None, None, None] for axis in range(3)]
    parts = [(lax.optimization_barrier(jnp.sum(populations * columns[axis], axis=0)) + 0.5 * force_field[axis]) / density for axis in range(3)]
    project = columns[0] * parts[0][None] + columns[1] * parts[1][None] + columns[2] * parts[2][None]
    force_proj = columns[0] * force_field[0][None] + columns[1] * force_field[1][None] + columns[2] * force_field[2][None]
    speed_sq = parts[0] * parts[0] + parts[1] * parts[1] + parts[2] * parts[2]
    work_rate = parts[0] * force_field[0] + parts[1] * force_field[1] + parts[2] * force_field[2]
    equilibrium = weights * density[None] * (1.0 + 3.0 * project + 4.5 * project * project - 1.5 * speed_sq[None])
    source = (1.0 - 0.5 * OMEGA) * weights * (3.0 * (force_proj - work_rate[None]) + 9.0 * project * force_proj)
    return populations - OMEGA * (populations - equilibrium) + source

def stream(padded, collided):
    x_cells = collided.shape[2]
    y_cells = collided.shape[3]
    outgoing = []
    for direction in range(19):
        shift_x = int(LATTICE_DIRS[direction, 0])
        shift_y = int(LATTICE_DIRS[direction, 1])
        shift_z = int(LATTICE_DIRS[direction, 2])
        pulled = padded[direction, :, 1 - shift_x:1 - shift_x + x_cells, 1 - shift_y:1 - shift_y + y_cells]
        mirror = collided[OPPOSITE[direction]]
        if shift_z == 1:
            pulled = jnp.concatenate([mirror[:1], pulled[:-1]], axis=0)
        elif shift_z == -1:
            pulled = jnp.concatenate([pulled[1:], mirror[-1:]], axis=0)
        outgoing.append(pulled)
    return jnp.stack(outgoing)

def reference(f_in, rotor_place, marker_cell, pitch_phase, blade_area, blade_twist, blade_speed, blade_angle, filt_in):
    street = rotor_place[:, 0]
    plane_x = rotor_place[:, 1]
    owner_y = rotor_place[:, 2]
    rotor_ids = jnp.arange(ROTORS, dtype=jnp.int32)
    earlier = rotor_ids[None, :] < rotor_ids[:, None]
    same_owner = (street[:, None] == street[None, :]) & (owner_y[:, None] == owner_y[None, :])
    owner_rank = lax.optimization_barrier(jnp.sum((earlier & same_owner).astype(jnp.int32), axis=1))
    filtered = filt_in[street, owner_y, owner_rank]
    area = blade_area[street, owner_y, owner_rank]
    twist = blade_twist[street, owner_y, owner_rank]
    speed = blade_speed[street, owner_y, owner_rank]
    angle = blade_angle[street, owner_y, owner_rank]
    pitch = pitch_angles(pitch_phase)
    lowest = lax.optimization_barrier(jnp.min(marker_cell // (64 * Z), axis=1))
    window = jnp.minimum(lowest // CY * CY, NY - 2 * CY).astype(jnp.int32)
    plane_global = (street * CX + plane_x).astype(jnp.int32)
    zero = jnp.int32(0)
    populations = f_in
    loads = jnp.zeros((ROTORS, 3, M), jnp.float32)
    for step_index in range(STEPS):
        field_speed = velocity(populations)

        def sample_one(inputs):
            cell_codes, place, start = inputs
            section = lax.dynamic_slice(field_speed, (zero, zero, place, start), (3, Z, 1, 2 * CY))[:, :, 0, :]
            across, upward = stencil_tables(cell_codes, Z, 2 * CY, start)
            return sample_section(section, across, upward)
        sampled = lax.map(sample_one, (marker_cell, plane_global, window))
        filtered = filtered + MIX * (sampled - filtered)
        loads = blade_loads(filtered, area, twist, speed, angle, pitch[:, step_index][:, None])

        def spread_one(force_field, inputs):
            cell_codes, place, start, rotor_loads = inputs
            across, upward = stencil_tables(cell_codes, Z, 2 * CY, start)
            section = spread_section(rotor_loads, across, upward)
            current = lax.dynamic_slice(force_field, (zero, zero, place, start), (3, Z, 1, 2 * CY))
            return (lax.dynamic_update_slice(force_field, current + section[:, :, None, :], (zero, zero, place, start)), None)
        force_field, unused = lax.scan(spread_one, jnp.zeros((3, Z, NX, NY), jnp.float32), (marker_cell, plane_global, window, loads))
        collided = collide(populations, force_field)
        padded = jnp.pad(collided, ((0, 0), (0, 0), (1, 1), (1, 1)), mode='wrap')
        populations = stream(padded, collided)
    loads_out = jnp.zeros((TX, TY, OSLOT, 3, M), jnp.float32).at[street, owner_y, owner_rank].set(loads)
    filt_out = jnp.zeros((TX, TY, OSLOT, 3, M), jnp.float32).at[street, owner_y, owner_rank].set(filtered)
    return (populations, loads_out, filt_out)
```

```python
import math

import jax
import jax.numpy as jnp
from jax import lax
from jax.experimental import pallas as pl
from jax.experimental.pallas import tpu as pltpu
from jax.sharding import PartitionSpec as P

PHASES = 64
PAIRS = [
    (1, 0, 0),
    (0, 1, 0),
    (0, 0, 1),
    (1, 1, 0),
    (1, -1, 0),
    (1, 0, 1),
    (1, 0, -1),
    (0, 1, 1),
    (0, 1, -1),
]
DIRS = [(0, 0, 0)]
for along in PAIRS:
    DIRS.append(along)
    DIRS.append(tuple(-part for part in along))
OPPOSITE = [0] + [q + 1 if q % 2 else q - 1 for q in range(1, 19)]
PLUS = [q for q in range(19) if DIRS[q][0] == 1]
MINUS = [q for q in range(19) if DIRS[q][0] == -1]
SIDEWAYS = [q for q in range(19) if DIRS[q][1] != 0]
OMEGA = 1.0 / 0.6
KEEP = 1.0 - OMEGA
GUO = 1.0 - 0.5 * OMEGA
SPREAD = 0.01
MIX = 0.5
PITCH_AMP = 0.2
LANES = 128
F32 = jnp.float32
BF16 = jnp.bfloat16
VMEM_LIMIT = 8 * 1024 * 1024


def iota(shape, axis):
    return lax.broadcasted_iota(jnp.int32, shape, axis)


def aligned(value, by):
    return value if isinstance(value, int) else pl.multiple_of(value, by)


def wrapped(value):
    return value % LANES if isinstance(value, int) else lax.rem(value, LANES)


def moments(f):
    sums = [f[2 * k + 1] + f[2 * k + 2] for k in range(9)]
    gaps = [f[2 * k + 1] - f[2 * k + 2] for k in range(9)]
    density = f[0]
    for part in sums:
        density = density + part
    momentum = []
    for axis in range(3):
        total = None
        for k in range(9):
            sign = PAIRS[k][axis]
            if sign == 0:
                continue
            if total is None:
                total = gaps[k]
            else:
                total = total + gaps[k] if sign > 0 else total - gaps[k]
        momentum.append(total)
    return density, momentum


def collide(f, force, wanted):
    density, momentum = moments(f)
    inverse = 1.0 / density
    v = [(momentum[a] + 0.5 * force[a]) * inverse for a in range(3)]
    relaxed = OMEGA * density
    square = v[0] * v[0] + v[1] * v[1] + v[2] * v[2]
    work = v[0] * force[0] + v[1] * force[1] + v[2] * force[2]
    base = relaxed * (1.0 - 1.5 * square) - (3.0 * GUO) * work
    drive = [relaxed * v[a] + GUO * force[a] for a in range(3)]
    bend = [(4.5 * relaxed) * v[a] + (9.0 * GUO) * force[a] for a in range(3)]
    post = {}
    if 0 in wanted:
        post[0] = KEEP * f[0] + base * (1.0 / 3.0)
    scaled = {}
    for weight in (18.0, 36.0):
        scaled[weight] = (
            base * (1.0 / weight),
            [part * (3.0 / weight) for part in drive],
            [part * (1.0 / weight) for part in bend],
        )

    def along(k, parts):
        total = None
        for axis in range(3):
            sign = PAIRS[k][axis]
            if sign == 0:
                continue
            if total is None:
                total = parts[axis]
            else:
                total = total + parts[axis] if sign > 0 else total - parts[axis]
        return total

    for k in range(9):
        if 2 * k + 1 not in wanted and 2 * k + 2 not in wanted:
            continue
        level, drives, bends = scaled[18.0 if k < 3 else 36.0]
        even = level + along(k, v) * along(k, bends)
        odd = along(k, drives)
        if 2 * k + 1 in wanted:
            post[2 * k + 1] = KEEP * f[2 * k + 1] + (even + odd)
        if 2 * k + 2 in wanted:
            post[2 * k + 2] = KEEP * f[2 * k + 2] + (even - odd)
    return post


def outside(q, levels, rows):
    if DIRS[q][2] == 1:
        return rows == 0
    if DIRS[q][2] == -1:
        return rows == levels - 1
    return None


class Shape:
    def __init__(self, f_in, rotor_place, marker_cell, pitch_phase, filt_in):
        self.levels = f_in.shape[1]
        self.xs = f_in.shape[2]
        self.rotors = rotor_place.shape[0]
        self.steps = pitch_phase.shape[1]
        self.markers = marker_cell.shape[1]
        self.slots = filt_in.shape[2]
        self.tiles = lax.axis_size("gy")
        self.groups = self.markers // LANES
        self.section = self.slots * 3 * self.levels


def in_vmem(x):
    return pltpu.with_memory_space_constraint(x, pltpu.VMEM)


def in_smem(x):
    return pltpu.with_memory_space_constraint(x, pltpu.SMEM)


VM = pl.BlockSpec(memory_space=pltpu.VMEM)
SM = pl.BlockSpec(memory_space=pltpu.SMEM)
HB = pl.BlockSpec(memory_space=pl.ANY)
PARAMS = pltpu.CompilerParams(vmem_limit_bytes=VMEM_LIMIT)


def plan_kernel(sh, place, plan, count):
    row = lax.axis_index("gx")
    me = lax.axis_index("gy")
    for k in range(sh.tiles * sh.slots + sh.slots):
        plan[k] = -1
    for k in range(sh.tiles):
        count[k] = 0

    def visit(rotor, carry):
        @pl.when(place[rotor, 0] == row)
        def _():
            owner = place[rotor, 2]
            slot = count[owner]
            count[owner] = slot + 1
            plan[owner * sh.slots + slot] = place[rotor, 1]

            @pl.when(owner == me)
            def _():
                plan[sh.tiles * sh.slots + slot] = rotor

        return carry

    lax.fori_loop(0, sh.rotors, visit, 0)


def make_plan(sh, rotor_place):
    size = sh.tiles * sh.slots + sh.slots
    return pl.pallas_call(
        lambda *refs: plan_kernel(sh, *refs),
        out_shape=pltpu.SMEM((size,), jnp.int32),
        in_specs=[SM],
        out_specs=SM,
        scratch_shapes=[pltpu.SMEM((sh.tiles,), jnp.int32)],
        name="plan",
    )(rotor_place)


def plane_of(sh, f, x, low, high):
    rows = iota((sh.levels, LANES), 0)
    planes = []
    for q in range(19):
        value = f[q, pl.ds(x, sh.levels, stride=sh.xs), :]
        if low is not None and DIRS[q][0] != 0:
            if DIRS[q][0] == 1:
                other, at = low[PLUS.index(q)], 0
            else:
                other, at = high[MINUS.index(q)], sh.xs - 1
            here = jnp.asarray(x == at)
            skip = outside(q, sh.levels, rows)
            use = here if skip is None else jnp.logical_and(here, jnp.logical_not(skip))
            value = jnp.where(use, other, value)
        planes.append(value)
    return planes


def pre_kernel(sh, has_edges, *refs):
    plan, f = refs[:2]
    low, high = refs[2:4] if has_edges else (None, None)
    outs = refs[4:] if has_edges else refs[2:]
    me = lax.axis_index("gy")
    for shift in range(sh.tiles):
        owner = lax.rem(me + shift, sh.tiles)
        for slot in range(sh.slots):
            x = plan[owner * sh.slots + slot]

            @pl.when(x >= 0)
            def _():
                planes = plane_of(sh, f, x, low, high)
                density, momentum = moments(planes)
                inverse = 1.0 / density
                for axis in range(3):
                    at = (slot * 3 + axis) * sh.levels
                    outs[shift][at : at + sh.levels, :] = momentum[axis] * inverse

            @pl.when(x < 0)
            def _():
                at = slot * 3 * sh.levels
                outs[shift][at : at + 3 * sh.levels, :] = jnp.zeros((3 * sh.levels, LANES), F32)


def make_sections(sh, plan, f, edges):
    return pl.pallas_call(
        lambda *refs: pre_kernel(sh, bool(edges), *refs),
        out_shape=[pltpu.VMEM((sh.section, LANES), F32)] * sh.tiles,
        in_specs=[SM] + [VM] * (1 + len(edges)),
        out_specs=[VM] * sh.tiles,
        compiler_params=PARAMS,
        name="sections",
    )(plan, f, *edges)


def column_kernel(sh, has_edges, *refs):
    f = refs[0]
    low, high = refs[1:3] if has_edges else (None, None)
    outs = refs[-2:]
    lanes = iota((sh.xs, LANES), 1)
    xrows = iota((sh.xs, LANES), 0)
    per = LANES // sh.levels
    groups = (19 + per - 1) // per
    for side, edge in ((0, 0), (1, LANES - 1)):
        for group in range(groups):
            total = jnp.zeros((sh.xs, LANES), F32)
            for q in range(group * per, min(19, (group + 1) * per)):
                for z in range(sh.levels):
                    tile = f[q, z * sh.xs : (z + 1) * sh.xs, :]
                    if has_edges and DIRS[q][0] != 0:
                        blocked = (DIRS[q][2] == 1 and z == 0) or (
                            DIRS[q][2] == -1 and z == sh.levels - 1
                        )
                        if not blocked:
                            if DIRS[q][0] == 1:
                                tile = jnp.where(xrows == 0, low[PLUS.index(q), z : z + 1, :], tile)
                            else:
                                tile = jnp.where(
                                    xrows == sh.xs - 1, high[MINUS.index(q), z : z + 1, :], tile
                                )
                    column = jnp.broadcast_to(tile[:, edge : edge + 1], (sh.xs, LANES))
                    total = jnp.where(lanes == (q % per) * sh.levels + z, column, total)
            outs[side][group * sh.xs : (group + 1) * sh.xs, :] = total
    zlanes = iota((sh.levels, LANES), 1)
    at = groups * sh.xs
    corners = [jnp.zeros((sh.levels, LANES), F32) for side in range(2)]
    for which, x in ((0, 0), (1, sh.xs - 1)):
        planes = plane_of(sh, f, x, low, high)
        for q in range(19):
            for side, edge in ((0, 0), (1, LANES - 1)):
                column = jnp.broadcast_to(planes[q][:, edge : edge + 1], (sh.levels, LANES))
                corners[side] = jnp.where(zlanes == 2 * q + which, column, corners[side])
    for side in range(2):
        outs[side][at : at + sh.levels, :] = corners[side]


def make_columns(sh, f, edges):
    per = LANES // sh.levels
    groups = (19 + per - 1) // per
    rows = groups * sh.xs + sh.levels
    return pl.pallas_call(
        lambda *refs: column_kernel(sh, bool(edges), *refs),
        out_shape=[pltpu.VMEM((rows, LANES), F32)] * 2,
        in_specs=[VM] * (1 + len(edges)),
        out_specs=[VM] * 2,
        compiler_params=PARAMS,
        name="columns",
    )(f, *edges)


def peskin(offsets):
    distance = jnp.abs(offsets)
    near_arg = jnp.maximum(1.0 + 4.0 * distance - 4.0 * distance * distance, 1.0)
    far_arg = jnp.maximum(-7.0 + 12.0 * distance - 4.0 * distance * distance, 1.0)
    near = distance <= 1.0
    root = jnp.sqrt(jnp.where(near, near_arg, far_arg))
    return (jnp.where(near, 3.0, 5.0) - 2.0 * distance + jnp.where(near, root, -root)) * 0.125


TABLE_CHUNK = 256


def table_kernel(sh, plan, cells, across, upward, info, codes, sem):
    ids = [plan[sh.tiles * sh.slots + slot] for slot in range(sh.slots)]
    copies = []
    for slot in range(sh.slots):
        first = pl.multiple_of(jnp.maximum(ids[slot], 0) // 8 * 8, 8)
        copy = pltpu.make_async_copy(cells.at[pl.ds(first, 8), :], codes.at[slot], sem.at[slot])
        copy.start()
        copies.append(copy)
    width = TABLE_CHUNK
    corner = iota((8, width), 0)
    spanwise = corner < 4
    place = (corner % 4).astype(F32) - 1.0
    ycells = iota((LANES, width), 0).astype(F32).astype(BF16)
    zcells = iota((sh.levels, width), 0)
    zero = jnp.zeros((LANES, width), BF16)
    for slot in range(sh.slots):
        copies[slot].wait()

        @pl.when(ids[slot] >= 0)
        def _():
            row = ids[slot] % 8
            every = codes[slot, pl.ds(row, 1), :] // (64 * sh.levels)
            lowest = jnp.min(every)
            highest = jnp.max(every)
            narrow = highest - lowest + 4 <= LANES
            start = jnp.where(narrow, lowest, lowest // LANES * LANES)
            info[2 * slot] = start
            info[2 * slot + 1] = jnp.where(narrow, 1, 2)

            def chunk(window, at):
                code = codes[slot, pl.ds(row, 1), pl.ds(at, width)]
                cell = code // (64 * sh.levels) - start - window * LANES
                level = code // 64 % sh.levels
                eighths = jnp.where(spanwise, code // 8 % 8, code % 8)
                weights = peskin(place - eighths.astype(F32) * 0.125)
                top = weights.astype(BF16)
                rest = (weights - top.astype(F32)).astype(BF16)
                tall = jnp.zeros((sh.levels, width), F32)
                for j in range(4):
                    tall = jnp.where(zcells == level + j, weights[4 + j : 5 + j, :], tall)
                upward[slot, :, pl.ds(at, width)] = tall
                wide = [zero, zero]
                for j in range(4):
                    here = ycells == (cell + j).astype(F32).astype(BF16)
                    for part, source in ((0, top), (1, rest)):
                        wide[part] = jnp.where(here, source[j : j + 1, :], wide[part])
                for part in range(2):
                    across[slot, window, part * LANES : (part + 1) * LANES, pl.ds(at, width)] = wide[
                        part
                    ]

            def sweep(window):
                def body(i, carry):
                    chunk(window, pl.multiple_of(i * width, width))
                    return carry

                lax.fori_loop(0, sh.markers // width, body, 0)

            sweep(0)

            @pl.when(jnp.logical_not(narrow))
            def _():
                sweep(1)


def make_tables(sh, plan, marker_cell):
    return pl.pallas_call(
        lambda *refs: table_kernel(sh, *refs),
        out_shape=[
            pltpu.VMEM((sh.slots, 2, 2 * LANES, sh.markers), BF16),
            pltpu.VMEM((sh.slots, sh.levels, sh.markers), F32),
            pltpu.SMEM((2 * sh.slots,), jnp.int32),
        ],
        in_specs=[SM, HB],
        out_specs=[VM, VM, SM],
        scratch_shapes=[
            pltpu.VMEM((sh.slots, 8, sh.markers), jnp.int32),
            pltpu.SemaphoreType.DMA((sh.slots,)),
        ],
        compiler_params=PARAMS,
        name="tables",
    )(plan, marker_cell)


def blade_kernel(sh, plan, phases, area, twist, speed, angle, filt, blades, filtered):
    rows = sh.slots * sh.groups

    def dense(read, write):
        for slot in range(sh.slots):
            for group in range(sh.groups):
                write(slot * sh.groups + group, read(slot, group * LANES))

    def keep(k):
        def write(row, value):
            blades[k, row : row + 1, :] = value

        return write

    for k, source in ((0, area), (1, speed), (2, angle), (3, twist)):
        dense(lambda slot, at: source[slot : slot + 1, at : at + LANES], keep(k))
    for axis in range(3):

        def write(row, value):
            filtered[axis, row : row + 1, :] = value

        dense(lambda slot, at: filt[slot, axis : axis + 1, at : at + LANES], write)
    around = blades[2]
    turned = blades[3]
    blades[2] = jnp.sin(around)
    blades[3] = jnp.cos(around)
    sin_twist = jnp.sin(turned)
    cos_twist = jnp.cos(turned)
    owner = iota((rows, LANES), 0) // sh.groups
    for step in range(sh.steps):
        phase = jnp.zeros((rows, LANES), F32)
        for slot in range(sh.slots):
            rotor = jnp.maximum(plan[sh.tiles * sh.slots + slot], 0)
            phase = jnp.where(owner == slot, phases[rotor, step].astype(F32), phase)
        pitch = PITCH_AMP * jnp.sin((2.0 * math.pi / PHASES) * phase)
        sin_pitch = jnp.sin(pitch)
        cos_pitch = jnp.cos(pitch)
        blades[4 + 2 * step] = sin_twist * cos_pitch + cos_twist * sin_pitch
        blades[5 + 2 * step] = cos_twist * cos_pitch - sin_twist * sin_pitch


def make_blades(sh, plan, phases, area, twist, speed, angle, filt):
    rows = sh.slots * sh.groups
    return pl.pallas_call(
        lambda *refs: blade_kernel(sh, *refs),
        out_shape=[
            pltpu.VMEM((4 + 2 * sh.steps, rows, LANES), F32),
            pltpu.VMEM((3, rows, LANES), F32),
        ],
        in_specs=[SM, SM] + [VM] * 5,
        out_specs=[VM, VM],
        compiler_params=PARAMS,
        name="blades",
    )(plan, phases, area, twist, speed, angle, filt)


SAMPLE_CHUNK = 512
SPREAD_CHUNK = 1024


def split(value):
    top = value.astype(BF16)
    return top, (value - top.astype(F32)).astype(BF16)


def marker_kernel(sh, step, plan, info, across, upward, blades, filt_old, *refs):
    sections = refs[: sh.tiles]
    filt_new, loads = refs[sh.tiles : sh.tiles + 2]
    forces = refs[sh.tiles + 2 : 2 * sh.tiles + 2]
    around, sampled, weighted, spread = refs[2 * sh.tiles + 2 :]
    me = lax.axis_index("gy")
    tall = 3 * sh.levels
    for shift in range(sh.tiles):
        around[lax.rem(me + sh.tiles - shift, sh.tiles)] = sections[shift][...]
    spread[...] = jnp.zeros(spread.shape, F32)

    def window_of(slot, window):
        start = info[2 * slot] + window * LANES
        tile = start // LANES
        return tile, jnp.minimum(tile + 1, sh.tiles - 1), start - tile * LANES

    def windows(slot, body):
        @pl.when(plan[sh.tiles * sh.slots + slot] >= 0)
        def _():
            body(0)

            @pl.when(info[2 * slot + 1] > 1)
            def _():
                body(1)

    for slot in range(sh.slots):
        rows = pl.ds(slot * tall, tall)

        def sample(window):
            tile, after, offset = window_of(slot, window)
            both = jnp.concatenate([around[tile, rows, :], around[after, rows, :]], axis=1)
            seen = pltpu.roll(both, lax.rem(2 * LANES - offset, 2 * LANES), 1)[:, :LANES]
            top, rest = split(seen)
            left = jnp.concatenate([top, rest], axis=0)
            left = jnp.concatenate([left, left], axis=1)

            def chunk(i, carry):
                at = pl.multiple_of(i * SAMPLE_CHUNK, SAMPLE_CHUNK)
                value = jnp.dot(
                    left,
                    across[slot, window, :, pl.ds(at, SAMPLE_CHUNK)],
                    preferred_element_type=F32,
                )
                value = value[:tall] + value[tall:]
                heights = upward[slot, :, pl.ds(at, SAMPLE_CHUNK)]
                for axis in range(3):
                    part = jnp.sum(
                        value[axis * sh.levels : (axis + 1) * sh.levels] * heights,
                        axis=0,
                        keepdims=True,
                    )
                    for group in range(SAMPLE_CHUNK // LANES):
                        row = slot * sh.groups + i * (SAMPLE_CHUNK // LANES) + group
                        piece = part[:, group * LANES : (group + 1) * LANES]
                        if window:
                            piece = piece + sampled[axis, pl.ds(row, 1), :]
                        sampled[axis, pl.ds(row, 1), :] = piece
                return carry

            lax.fori_loop(0, sh.markers // SAMPLE_CHUNK, chunk, 0)

        windows(slot, sample)

    felt = []
    for axis in range(3):
        old = filt_old[axis]
        value = old + MIX * (sampled[axis] - old)
        filt_new[axis] = value
        felt.append(value)
    sin_t = blades[2]
    cos_t = blades[3]
    tangent = blades[1] + sin_t * felt[1] - cos_t * felt[2]
    square = felt[0] * felt[0] + tangent * tangent
    inverse = 1.0 / jnp.sqrt(square)
    sin_p = felt[0] * inverse
    cos_p = tangent * inverse
    sin_b = blades[4 + 2 * step]
    cos_b = blades[5 + 2 * step]
    sin_a = sin_p * cos_b - cos_p * sin_b
    cos_a = cos_p * cos_b + sin_p * sin_b
    lift = (2.0 * math.pi) * sin_a * cos_a
    drag = 0.02 + sin_a * sin_a
    dynamic = 0.5 * blades[0] * square
    around_axis = dynamic * (lift * sin_p - drag * cos_p)
    loads[0] = dynamic * (lift * cos_p + drag * sin_p)
    loads[1] = -around_axis * sin_t
    loads[2] = around_axis * cos_t

    for slot in range(sh.slots):
        rows = pl.ds(slot * tall, tall)

        def spread_out(window):
            tile, after, offset = window_of(slot, window)

            def chunk(i, total):
                at = pl.multiple_of(i * SPREAD_CHUNK, SPREAD_CHUNK)
                for group in range(SPREAD_CHUNK // LANES):
                    heights = upward[slot, :, pl.ds(at + group * LANES, LANES)]
                    row = slot * sh.groups + i * (SPREAD_CHUNK // LANES) + group
                    parts = [heights * loads[axis, pl.ds(row, 1), :] for axis in range(3)]
                    top, rest = split(jnp.concatenate(parts, axis=0))
                    weighted[:tall, group * LANES : (group + 1) * LANES] = top
                    weighted[tall:, group * LANES : (group + 1) * LANES] = rest
                return total + lax.dot_general(
                    weighted[...],
                    across[slot, window, :, pl.ds(at, SPREAD_CHUNK)],
                    (((1,), (1,)), ((), ())),
                    preferred_element_type=F32,
                )

            total = lax.fori_loop(
                0,
                sh.markers // SPREAD_CHUNK,
                chunk,
                jnp.zeros((2 * tall, 2 * LANES), F32),
            )
            total = total[:tall] + total[tall:]
            total = -SPREAD * (total[:, :LANES] + total[:, LANES:])
            both = jnp.concatenate([total, jnp.zeros((tall, LANES), F32)], axis=1)
            both = pltpu.roll(both, offset, 1)
            spread[tile, rows, :] = spread[tile, rows, :] + both[:, :LANES]
            spread[after, rows, :] = spread[after, rows, :] + both[:, LANES:]

        windows(slot, spread_out)

    lanes = iota((sh.levels, LANES), 1)
    for shift in range(sh.tiles):
        tile = lax.rem(me + shift, sh.tiles)
        forces[shift][: sh.section, :] = spread[tile]
        before = lax.rem(tile + sh.tiles - 1, sh.tiles)
        after = lax.rem(tile + 1, sh.tiles)
        ghosts = jnp.zeros((sh.levels, LANES), F32)
        for k in range(3 * sh.slots):
            at = pl.ds(k * sh.levels, sh.levels)
            left = jnp.broadcast_to(spread[before, at, :][:, LANES - 1 :], (sh.levels, LANES))
            right = jnp.broadcast_to(spread[after, at, :][:, :1], (sh.levels, LANES))
            ghosts = jnp.where(lanes == 2 * k, left, ghosts)
            ghosts = jnp.where(lanes == 2 * k + 1, right, ghosts)
        forces[shift][sh.section :, :] = ghosts


def do_markers(sh, step, plan, info, across, upward, blades, filt, sections):
    rows = sh.slots * sh.groups
    dense = pltpu.VMEM((3, rows, LANES), F32)
    force = pltpu.VMEM((sh.section + sh.levels, LANES), F32)
    out = pl.pallas_call(
        lambda *refs: marker_kernel(sh, step, *refs),
        out_shape=[dense, dense] + [force] * sh.tiles,
        in_specs=[SM, SM] + [VM] * (4 + sh.tiles),
        out_specs=[VM] * (2 + sh.tiles),
        scratch_shapes=[
            pltpu.VMEM((sh.tiles, sh.section, LANES), F32),
            pltpu.VMEM((3, rows, LANES), F32),
            pltpu.VMEM((6 * sh.levels, SPREAD_CHUNK), BF16),
            pltpu.VMEM((sh.tiles, sh.section, LANES), F32),
        ],
        compiler_params=PARAMS,
        name="markers",
    )(plan, info, across, upward, blades, filt, *sections)
    return out[0], out[1], out[2:]


def edge_kernel(sh, has_edges, plan, f, *refs):
    low, high = refs[:2] if has_edges else (None, None)
    refs = refs[2 * has_edges :]
    left, right = refs[:2]
    forces = refs[2 : 2 + sh.tiles]
    outs = refs[2 + sh.tiles :]
    me = lax.axis_index("gy")
    lanes = iota((sh.levels, LANES), 1)
    groups = (left.shape[0] - sh.levels) // sh.xs
    corner_rows = pl.ds(groups * sh.xs, sh.levels)
    blank = jnp.zeros((sh.levels, LANES), F32)
    planes_at = (0, sh.xs - 1)
    corner = []
    from_left = left[corner_rows, :]
    from_right = right[corner_rows, :]
    for q in range(19):
        a = pltpu.roll(from_left, (LANES - 2 * q) % LANES, 1)
        b = pltpu.roll(from_right, (LANES + 2 - 2 * q) % LANES, 1)
        corner.append(jnp.where(lanes < 2, a, jnp.where(lanes < 4, b, 1.0)))
    corner_force = [blank, blank, blank]
    edge_force = [[blank, blank, blank], [blank, blank, blank]]
    for shift in range(sh.tiles):
        owner = lax.rem(me + sh.tiles - shift, sh.tiles)
        ghosts = forces[shift][sh.section :, :]
        for slot in range(sh.slots):
            x = plan[owner * sh.slots + slot]
            for axis in range(3):
                k = slot * 3 + axis
                piece = forces[shift][k * sh.levels : (k + 1) * sh.levels, :]
                for which in range(2):
                    here = jnp.asarray(x == planes_at[which])
                    edge_force[which][axis] = edge_force[which][axis] + jnp.where(here, piece, 0.0)
                    for side in range(2):
                        lane = 2 * side + which
                        moved = pltpu.roll(ghosts, (lane - 2 * k - side) % LANES, 1)
                        corner_force[axis] = corner_force[axis] + jnp.where(
                            jnp.logical_and(here, lanes == lane), moved, 0.0
                        )
    corner_post = collide(corner, corner_force, [q for q in PLUS + MINUS if DIRS[q][1]])
    for which, wanted in ((1, PLUS), (0, MINUS)):
        planes = plane_of(sh, f, planes_at[which], low, high)
        post = collide(planes, edge_force[which], wanted)
        out = outs[0] if which else outs[1]
        for k, q in enumerate(wanted):
            value = post[q]
            if DIRS[q][1] == 1:
                value = pltpu.roll(value, 1, 1)
                ghost = pltpu.roll(corner_post[q], (LANES - which) % LANES, 1)
                value = jnp.where(lanes == 0, ghost, value)
            elif DIRS[q][1] == -1:
                value = pltpu.roll(value, LANES - 1, 1)
                ghost = pltpu.roll(corner_post[q], (LANES - 1 - 2 - which) % LANES, 1)
                value = jnp.where(lanes == LANES - 1, ghost, value)
            if DIRS[q][2]:
                value = pltpu.roll(value, DIRS[q][2] % sh.levels, 0)
            out[k] = value


def make_edges(sh, plan, f, edges, columns, forces):
    return pl.pallas_call(
        lambda *refs: edge_kernel(sh, bool(edges), *refs),
        out_shape=[pltpu.VMEM((len(PLUS), sh.levels, LANES), F32)] * 2,
        in_specs=[SM] + [VM] * (3 + len(edges) + sh.tiles),
        out_specs=[VM] * 2,
        compiler_params=PARAMS,
        name="edges",
    )(plan, f, *edges, *columns, *forces)


def collide_kernel(sh, has_edges, last, plan, f, *refs):
    low, high = refs[:2] if has_edges else (None, None)
    refs = refs[2 * has_edges :]
    left, right = refs[:2]
    forces = refs[2 : 2 + sh.tiles]
    out = refs[2 + sh.tiles]
    kept = refs[3 + sh.tiles] if last else None
    field, ghost_posts = refs[-2:]
    me = lax.axis_index("gy")
    xs = sh.xs
    lanes = iota((xs, LANES), 1)
    xrows = iota((xs, LANES), 0)
    per = LANES // sh.levels
    field[...] = jnp.zeros(field.shape, F32)
    ghost_force = [jnp.zeros((xs, LANES), F32) for axis in range(3)]
    for shift in range(sh.tiles):
        owner = lax.rem(me + sh.tiles - shift, sh.tiles)
        ghosts = jnp.transpose(
            jnp.concatenate(
                [
                    forces[shift][sh.section :, :],
                    jnp.zeros((LANES - sh.levels, LANES), F32),
                ],
                axis=0,
            )
        )
        for slot in range(sh.slots):
            x = plan[owner * sh.slots + slot]

            @pl.when(x >= 0)
            def _():
                for axis in range(3):
                    k = slot * 3 + axis
                    at = pl.ds(x, sh.levels, stride=xs)
                    field[axis, at, :] = (
                        field[axis, at, :] + forces[shift][k * sh.levels : (k + 1) * sh.levels, :]
                    )

            for axis in range(3):
                k = slot * 3 + axis
                far = pltpu.roll(ghosts[2 * k + 1 : 2 * k + 2, :], sh.levels, 1)
                piece = ghosts[2 * k : 2 * k + 1, :] + far
                ghost_force[axis] = ghost_force[axis] + jnp.where(xrows == x, piece, 0.0)

    ghost = []
    for q in range(19):
        at = pl.ds(q // per * xs, xs)
        shift = (q % per) * sh.levels
        a = pltpu.roll(left[at, :], (LANES - shift) % LANES, 1)
        b = pltpu.roll(right[at, :], (LANES + sh.levels - shift) % LANES, 1)
        ghost.append(
            jnp.where(lanes < sh.levels, a, jnp.where(lanes < 2 * sh.levels, b, 1.0))
        )
    posted = collide(ghost, ghost_force, SIDEWAYS)
    for k, q in enumerate(SIDEWAYS):
        ghost_posts[k] = posted[q]

    def level(z, bottom, top):
        at = aligned(z * xs, xs)
        here = []
        for q in range(19):
            tile = f[q, pl.ds(at, xs), :]
            if has_edges and DIRS[q][0] != 0:
                blocked = (DIRS[q][2] == 1 and bottom) or (DIRS[q][2] == -1 and top)
                if not blocked:
                    if DIRS[q][0] == 1:
                        tile = jnp.where(xrows == 0, low[PLUS.index(q), pl.ds(z, 1), :], tile)
                    else:
                        tile = jnp.where(
                            xrows == xs - 1, high[MINUS.index(q), pl.ds(z, 1), :], tile
                        )
            here.append(tile)
        force = [field[axis, pl.ds(at, xs), :] for axis in range(3)]
        post = collide(here, force, range(19))
        for q in range(19):
            dx, dy, dz = DIRS[q]
            value = post[q]
            if (dz == 1 and top) or (dz == -1 and bottom):
                to, target = OPPOSITE[q], z
            else:
                to, target = q, z + dz
                if dy == 1:
                    value = pltpu.roll(value, 1, 1)
                    other = pltpu.roll(
                        ghost_posts[SIDEWAYS.index(q)], wrapped(LANES - z), 1
                    )
                    value = jnp.where(lanes == 0, other, value)
                elif dy == -1:
                    value = pltpu.roll(value, LANES - 1, 1)
                    other = pltpu.roll(
                        ghost_posts[SIDEWAYS.index(q)], LANES - 1 - sh.levels - z, 1
                    )
                    value = jnp.where(lanes == LANES - 1, other, value)
                if dx:
                    value = pltpu.roll(value, dx % xs, 0)
            row = aligned(target * xs, xs)
            out[to, pl.ds(row, xs), :] = value
            if last and DIRS[to][0] == 1:
                kept[PLUS.index(to), pl.ds(target, 1)] = value[None, :8]
            if last and DIRS[to][0] == -1:
                kept[len(PLUS) + MINUS.index(to), pl.ds(target, 1)] = value[None, xs - 8 :]

    level(0, True, False)

    def middle(z, carry):
        level(z, False, False)
        return carry

    lax.fori_loop(1, sh.levels - 1, middle, 0)
    level(sh.levels - 1, False, True)


def do_collide(sh, last, plan, f, edges, columns, forces):
    shape = (19, sh.levels * sh.xs, LANES)
    if last:
        out_shape = [
            jax.ShapeDtypeStruct(shape, F32),
            pltpu.VMEM((2 * len(PLUS), sh.levels, 8, LANES), F32),
        ]
    else:
        out_shape = [pltpu.VMEM(shape, F32)]
    return pl.pallas_call(
        lambda *refs: collide_kernel(sh, bool(edges), last, *refs),
        out_shape=out_shape,
        in_specs=[SM] + [VM] * (3 + len(edges) + sh.tiles),
        out_specs=[VM] * len(out_shape),
        scratch_shapes=[
            pltpu.VMEM((3, sh.levels * sh.xs, LANES), F32),
            pltpu.VMEM((len(SIDEWAYS), sh.xs, LANES), F32),
        ],
        compiler_params=PARAMS,
        name="collide",
    )(plan, f, *edges, *columns, *forces)


def finish_kernel(sh, kept, low, high, f_old, f, merged, sem):
    del f_old
    rows = iota((8, LANES), 0)
    copies = []
    for side, dirs, edge in ((0, PLUS, low), (1, MINUS, high)):
        at_row = 0 if side == 0 else 7
        for k, q in enumerate(dirs):
            index = side * len(PLUS) + k
            for z in range(sh.levels):
                value = kept[index, z]
                blocked = (DIRS[q][2] == 1 and z == 0) or (
                    DIRS[q][2] == -1 and z == sh.levels - 1
                )
                if not blocked:
                    value = jnp.where(rows == at_row, edge[k, z : z + 1, :], value)
                merged[index, z] = value
            first = 0 if side == 0 else sh.xs - 8
            copy = pltpu.make_async_copy(
                merged.at[index], f.at[q, :, first : first + 8, :], sem.at[index]
            )
            copy.start()
            copies.append(copy)
    for copy in copies:
        copy.wait()


def finish(sh, f, kept, edges):
    f = f.reshape(19, sh.levels, sh.xs, LANES)
    return pl.pallas_call(
        lambda *refs: finish_kernel(sh, *refs),
        out_shape=jax.ShapeDtypeStruct(f.shape, F32),
        in_specs=[VM, VM, VM, HB],
        out_specs=HB,
        scratch_shapes=[
            pltpu.VMEM((2 * len(PLUS), sh.levels, 8, LANES), F32),
            pltpu.SemaphoreType.DMA((2 * len(PLUS),)),
        ],
        input_output_aliases={3: 0},
        compiler_params=PARAMS,
        name="finish",
    )(kept, *edges, f)


def output_kernel(sh, plan, loads, filt, loads_out, filt_out):
    for slot in range(sh.slots):
        used = plan[sh.tiles * sh.slots + slot] >= 0
        for source, target in ((loads, loads_out), (filt, filt_out)):
            for axis in range(3):
                for group in range(sh.groups):
                    row = slot * sh.groups + group
                    value = jnp.where(used, source[axis, row : row + 1, :], 0.0)
                    target[slot, axis : axis + 1, group * LANES : (group + 1) * LANES] = value


def make_outputs(sh, plan, loads, filt):
    shape = jax.ShapeDtypeStruct((sh.slots, 3, sh.markers), F32)
    return pl.pallas_call(
        lambda *refs: output_kernel(sh, *refs),
        out_shape=[shape, shape],
        in_specs=[SM, VM, VM],
        out_specs=[VM, VM],
        compiler_params=PARAMS,
        name="outputs",
    )(plan, loads, filt)


def shifted(x, axis, by):
    count = lax.axis_size(axis)
    return lax.ppermute(x, axis, [(i, (i + by) % count) for i in range(count)])


def local(
    f_in,
    rotor_place,
    marker_cell,
    pitch_phase,
    blade_area,
    blade_twist,
    blade_speed,
    blade_angle,
    filt_in,
):
    sh = Shape(f_in, rotor_place, marker_cell, pitch_phase, filt_in)
    f = in_vmem(f_in.reshape(19, sh.levels * sh.xs, LANES))
    plan = in_smem(make_plan(sh, rotor_place))
    edges = ()
    filt = None
    for step in range(sh.steps):
        last = step == sh.steps - 1
        sections = make_sections(sh, plan, f, edges)
        sections = [sections[0]] + [
            shifted(sections[by], "gy", by) for by in range(1, sh.tiles)
        ]
        columns = make_columns(sh, f, edges)
        columns = (shifted(columns[1], "gy", 1), shifted(columns[0], "gy", -1))
        if step == 0:
            across, upward, info = make_tables(sh, plan, marker_cell)
            across, upward, info = in_vmem(across), in_vmem(upward), in_smem(info)
            blades, filt = make_blades(
                sh,
                plan,
                pitch_phase,
                blade_area[0, 0],
                blade_twist[0, 0],
                blade_speed[0, 0],
                blade_angle[0, 0],
                filt_in[0, 0],
            )
            blades = in_vmem(blades)
        filt, loads, forces = do_markers(
            sh,
            step,
            plan,
            info,
            across,
            upward,
            blades,
            in_vmem(filt),
            [in_vmem(section) for section in sections],
        )
        forces = [forces[0]] + [shifted(forces[by], "gy", by) for by in range(1, sh.tiles)]
        forces = [in_vmem(force) for force in forces]
        columns = [in_vmem(column) for column in columns]
        sent = make_edges(sh, plan, f, edges, columns, forces)
        new_edges = (shifted(sent[0], "gx", 1), shifted(sent[1], "gx", -1))
        done = do_collide(sh, last, plan, f, edges, columns, forces)
        edges = tuple(in_vmem(edge) for edge in new_edges)
        if last:
            f = finish(sh, done[0], in_vmem(done[1]), edges)
        else:
            f = in_vmem(done[0])
    loads_out, filt_out = make_outputs(sh, plan, in_vmem(loads), in_vmem(filt))
    return f, loads_out[None, None], filt_out[None, None]


def solution(mesh):
    in_specs = (
        P(None, None, "gx", "gy"),
        P(),
        P(),
        P(),
        P("gx", "gy", None, None),
        P("gx", "gy", None, None),
        P("gx", "gy", None, None),
        P("gx", "gy", None, None),
        P("gx", "gy", None, None, None),
    )
    out_specs = (
        P(None, None, "gx", "gy"),
        P("gx", "gy", None, None, None),
        P("gx", "gy", None, None, None),
    )
    return jax.shard_map(local, mesh=mesh, in_specs=in_specs, out_specs=out_specs, check_vma=False)
```

```python
import math

import jax
import jax.numpy as jnp
from jax import lax
from jax.experimental import pallas as pl
from jax.experimental.pallas import tpu as pltpu
from jax.sharding import PartitionSpec as P

PHASES = 64
PAIRS = [
    (1, 0, 0),
    (0, 1, 0),
    (0, 0, 1),
    (1, 1, 0),
    (1, -1, 0),
    (1, 0, 1),
    (1, 0, -1),
    (0, 1, 1),
    (0, 1, -1),
]
DIRS = [(0, 0, 0)]
for along in PAIRS:
    DIRS.append(along)
    DIRS.append(tuple(-part for part in along))
OPPOSITE = [0] + [q + 1 if q % 2 else q - 1 for q in range(1, 19)]
PLUS = [q for q in range(19) if DIRS[q][0] == 1]
MINUS = [q for q in range(19) if DIRS[q][0] == -1]
SIDEWAYS = [q for q in range(19) if DIRS[q][1] != 0]
OMEGA = 1.0 / 0.6
KEEP = 1.0 - OMEGA
GUO = 1.0 - 0.5 * OMEGA
SPREAD = 0.01
MIX = 0.5
PITCH_AMP = 0.2
LANES = 128
F32 = jnp.float32
BF16 = jnp.bfloat16
VMEM_LIMIT = 8 * 1024 * 1024


def iota(shape, axis):
    return lax.broadcasted_iota(jnp.int32, shape, axis)


def aligned(value, by):
    return value if isinstance(value, int) else pl.multiple_of(value, by)


def wrapped(value):
    return value % LANES if isinstance(value, int) else lax.rem(value, LANES)


def moments(f):
    sums = [f[2 * k + 1] + f[2 * k + 2] for k in range(9)]
    gaps = [f[2 * k + 1] - f[2 * k + 2] for k in range(9)]
    density = f[0]
    for part in sums:
        density = density + part
    momentum = []
    for axis in range(3):
        total = None
        for k in range(9):
            sign = PAIRS[k][axis]
            if sign == 0:
                continue
            if total is None:
                total = gaps[k]
            else:
                total = total + gaps[k] if sign > 0 else total - gaps[k]
        momentum.append(total)
    return density, momentum


def collide(f, force, wanted):
    density, momentum = moments(f)
    inverse = 1.0 / density
    relaxed = OMEGA * density
    if force is None:
        v = [momentum[a] * inverse for a in range(3)]
        square = v[0] * v[0] + v[1] * v[1] + v[2] * v[2]
        base = relaxed * (1.0 - 1.5 * square)
        drive = [OMEGA * momentum[a] for a in range(3)]
        bend = [4.5 * part for part in drive]
    else:
        v = [(momentum[a] + 0.5 * force[a]) * inverse for a in range(3)]
        square = v[0] * v[0] + v[1] * v[1] + v[2] * v[2]
        work = v[0] * force[0] + v[1] * force[1] + v[2] * force[2]
        base = relaxed * (1.0 - 1.5 * square) - (3.0 * GUO) * work
        drive = [relaxed * v[a] + GUO * force[a] for a in range(3)]
        bend = [(4.5 * relaxed) * v[a] + (9.0 * GUO) * force[a] for a in range(3)]
    post = {}
    if 0 in wanted:
        post[0] = KEEP * f[0] + base * (1.0 / 3.0)
    scaled = {}
    for weight in (18.0, 36.0):
        scaled[weight] = (
            base * (1.0 / weight),
            [part * (3.0 / weight) for part in drive],
            [part * (1.0 / weight) for part in bend],
        )

    def along(k, parts):
        total = None
        for axis in range(3):
            sign = PAIRS[k][axis]
            if sign == 0:
                continue
            if total is None:
                total = parts[axis]
            else:
                total = total + parts[axis] if sign > 0 else total - parts[axis]
        return total

    for k in range(9):
        if 2 * k + 1 not in wanted and 2 * k + 2 not in wanted:
            continue
        level, drives, bends = scaled[18.0 if k < 3 else 36.0]
        even = level + along(k, v) * along(k, bends)
        odd = along(k, drives)
        if 2 * k + 1 in wanted:
            post[2 * k + 1] = KEEP * f[2 * k + 1] + (even + odd)
        if 2 * k + 2 in wanted:
            post[2 * k + 2] = KEEP * f[2 * k + 2] + (even - odd)
    return post


def outside(q, levels, rows):
    if DIRS[q][2] == 1:
        return rows == 0
    if DIRS[q][2] == -1:
        return rows == levels - 1
    return None


class Shape:
    def __init__(self, f_in, rotor_place, marker_cell, pitch_phase, filt_in):
        self.levels = f_in.shape[1]
        self.xs = f_in.shape[2]
        self.rotors = rotor_place.shape[0]
        self.steps = pitch_phase.shape[1]
        self.markers = marker_cell.shape[1]
        self.slots = filt_in.shape[2]
        self.tiles = lax.axis_size("gy")
        self.groups = self.markers // LANES
        self.section = self.slots * 3 * self.levels


def in_vmem(x):
    return pltpu.with_memory_space_constraint(x, pltpu.VMEM)


def in_smem(x):
    return pltpu.with_memory_space_constraint(x, pltpu.SMEM)


VM = pl.BlockSpec(memory_space=pltpu.VMEM)
SM = pl.BlockSpec(memory_space=pltpu.SMEM)
HB = pl.BlockSpec(memory_space=pl.ANY)
PARAMS = pltpu.CompilerParams(vmem_limit_bytes=VMEM_LIMIT)


def write_plan(sh, place, plan):
    row = lax.axis_index("gx")
    shape = (sh.tiles, sh.rotors)
    mine = jnp.logical_and(place[2:3, :] == iota(shape, 0), place[0:1, :] == row)
    keys = iota(shape, 1) * sh.xs + place[1:2, :]
    none = sh.rotors * sh.xs
    last = jnp.full((sh.tiles, 1), -1, jnp.int32)
    for slot in range(sh.slots):
        left = jnp.logical_and(mine, keys > last)
        last = jnp.min(jnp.where(left, keys, none), axis=1, keepdims=True)
        for owner in range(sh.tiles):
            key = last[owner, 0]
            plan[owner * sh.slots + slot] = jnp.where(key < none, key, -1)


def plane_at(sh, plan, owner, slot):
    key = plan[owner * sh.slots + slot]
    return jnp.where(key < 0, -1, lax.rem(key, sh.xs))


def rotor_at(sh, plan, slot):
    key = plan[lax.axis_index("gy") * sh.slots + slot]
    return jnp.where(key < 0, -1, lax.div(key, sh.xs))


def plane_of(sh, f, x, low, high):
    rows = iota((sh.levels, LANES), 0)
    planes = []
    for q in range(19):
        value = f[q, pl.ds(x, sh.levels, stride=sh.xs), :]
        if low is not None and DIRS[q][0] != 0:
            if DIRS[q][0] == 1:
                other, at = low[PLUS.index(q)], 0
            else:
                other, at = high[MINUS.index(q)], sh.xs - 1
            here = jnp.asarray(x == at)
            skip = outside(q, sh.levels, rows)
            use = here if skip is None else jnp.logical_and(here, jnp.logical_not(skip))
            value = jnp.where(use, other, value)
        planes.append(value)
    return planes


def write_sections(sh, plan, f, low, high, outs):
    me = lax.axis_index("gy")
    for shift in range(sh.tiles):
        owner = lax.rem(me + shift, sh.tiles)
        for slot in range(sh.slots):
            x = plane_at(sh, plan, owner, slot)

            @pl.when(x >= 0)
            def _():
                planes = plane_of(sh, f, x, low, high)
                density, momentum = moments(planes)
                inverse = 1.0 / density
                for axis in range(3):
                    at = (slot * 3 + axis) * sh.levels
                    outs[shift][at : at + sh.levels, :] = momentum[axis] * inverse

            @pl.when(x < 0)
            def _():
                at = slot * 3 * sh.levels
                outs[shift][at : at + 3 * sh.levels, :] = jnp.zeros((3 * sh.levels, LANES), F32)


def start_kernel(sh, place, f_in, plan, f, *refs):
    outs, sem = refs[:-1], refs[-1]
    copy = pltpu.make_async_copy(f_in, f, sem)
    copy.start()
    write_plan(sh, place, plan)
    copy.wait()
    write_sections(sh, plan, f, None, None, outs)


def start(sh, rotor_place, f_in):
    out = pl.pallas_call(
        lambda *refs: start_kernel(sh, *refs),
        out_shape=[
            pltpu.SMEM((sh.tiles * sh.slots,), jnp.int32),
            pltpu.VMEM((19, sh.levels * sh.xs, LANES), F32),
        ]
        + [pltpu.VMEM((sh.section, LANES), F32)] * sh.tiles,
        in_specs=[VM, HB],
        out_specs=[SM] + [VM] * (1 + sh.tiles),
        scratch_shapes=[pltpu.SemaphoreType.DMA],
        compiler_params=PARAMS,
        name="start",
    )(jnp.transpose(rotor_place), f_in.reshape(19, sh.levels * sh.xs, LANES))
    return in_smem(out[0]), in_vmem(out[1]), out[2:]


def make_sections(sh, plan, f, edges):
    return pl.pallas_call(
        lambda plan, f, low, high, *outs: write_sections(sh, plan, f, low, high, outs),
        out_shape=[pltpu.VMEM((sh.section, LANES), F32)] * sh.tiles,
        in_specs=[SM] + [VM] * 3,
        out_specs=[VM] * sh.tiles,
        compiler_params=PARAMS,
        name="sections",
    )(plan, f, *edges)


def column_kernel(sh, has_edges, *refs):
    f = refs[0]
    low, high = refs[1:3] if has_edges else (None, None)
    outs = refs[-2:]
    lanes = iota((sh.xs, LANES), 1)
    xrows = iota((sh.xs, LANES), 0)
    per = LANES // sh.levels
    groups = (19 + per - 1) // per
    for side, edge in ((0, 0), (1, LANES - 1)):
        for group in range(groups):
            total = jnp.zeros((sh.xs, LANES), F32)
            for q in range(group * per, min(19, (group + 1) * per)):
                for z in range(sh.levels):
                    tile = f[q, z * sh.xs : (z + 1) * sh.xs, :]
                    if has_edges and DIRS[q][0] != 0:
                        blocked = (DIRS[q][2] == 1 and z == 0) or (
                            DIRS[q][2] == -1 and z == sh.levels - 1
                        )
                        if not blocked:
                            if DIRS[q][0] == 1:
                                tile = jnp.where(xrows == 0, low[PLUS.index(q), z : z + 1, :], tile)
                            else:
                                tile = jnp.where(
                                    xrows == sh.xs - 1, high[MINUS.index(q), z : z + 1, :], tile
                                )
                    column = jnp.broadcast_to(tile[:, edge : edge + 1], (sh.xs, LANES))
                    total = jnp.where(lanes == (q % per) * sh.levels + z, column, total)
            outs[side][group * sh.xs : (group + 1) * sh.xs, :] = total
    zlanes = iota((sh.levels, LANES), 1)
    at = groups * sh.xs
    corners = [jnp.zeros((sh.levels, LANES), F32) for side in range(2)]
    for which, x in ((0, 0), (1, sh.xs - 1)):
        planes = plane_of(sh, f, x, low, high)
        for q in range(19):
            for side, edge in ((0, 0), (1, LANES - 1)):
                column = jnp.broadcast_to(planes[q][:, edge : edge + 1], (sh.levels, LANES))
                corners[side] = jnp.where(zlanes == 2 * q + which, column, corners[side])
    for side in range(2):
        outs[side][at : at + sh.levels, :] = corners[side]


def make_columns(sh, f, edges):
    per = LANES // sh.levels
    groups = (19 + per - 1) // per
    rows = groups * sh.xs + sh.levels
    return pl.pallas_call(
        lambda *refs: column_kernel(sh, bool(edges), *refs),
        out_shape=[pltpu.VMEM((rows, LANES), F32)] * 2,
        in_specs=[VM] * (1 + len(edges)),
        out_specs=[VM] * 2,
        compiler_params=PARAMS,
        name="columns",
    )(f, *edges)


def peskin(offsets):
    distance = jnp.abs(offsets)
    near_arg = jnp.maximum(1.0 + 4.0 * distance - 4.0 * distance * distance, 1.0)
    far_arg = jnp.maximum(-7.0 + 12.0 * distance - 4.0 * distance * distance, 1.0)
    near = distance <= 1.0
    root = jnp.sqrt(jnp.where(near, near_arg, far_arg))
    return (jnp.where(near, 3.0, 5.0) - 2.0 * distance + jnp.where(near, root, -root)) * 0.125


TABLE_CHUNK = 1024


def table_kernel(sh, plan, cells, after, across, upward, info, codes, sem):
    del after
    ids = [rotor_at(sh, plan, slot) for slot in range(sh.slots)]
    copies = []
    for slot in range(sh.slots):
        first = pl.multiple_of(jnp.maximum(ids[slot], 0) // 8 * 8, 8)
        copy = pltpu.make_async_copy(cells.at[pl.ds(first, 8), :], codes.at[slot], sem.at[slot])
        copy.start()
        copies.append(copy)
    width = min(TABLE_CHUNK, sh.markers)
    corner = iota((8, width), 0)
    spanwise = corner < 4
    place = (corner % 4).astype(F32) - 1.0
    ycells = iota((LANES, LANES), 0).astype(F32).astype(BF16)
    zcells = iota((sh.levels, LANES), 0)
    for slot in range(sh.slots):
        copies[slot].wait()

        @pl.when(ids[slot] >= 0)
        def _():
            row = ids[slot] % 8
            every = codes[slot, pl.ds(row, 1), :] // (64 * sh.levels)
            lowest = jnp.min(every)
            highest = jnp.max(every)
            narrow = highest - lowest + 4 <= LANES
            start = jnp.where(narrow, lowest, lowest // LANES * LANES)
            info[2 * slot] = start
            info[2 * slot + 1] = jnp.where(narrow, 1, 2)

            def chunk(window, at):
                code = codes[slot, pl.ds(row, 1), pl.ds(at, width)]
                cells_y = code // (64 * sh.levels) - start - window * LANES
                levels = code // 64 % sh.levels
                eighths = jnp.where(spanwise, code // 8 % 8, code % 8)
                weights = peskin(place - eighths.astype(F32) * 0.125)
                top = weights.astype(BF16)
                rest = (weights - top.astype(F32)).astype(BF16)
                cells_y = cells_y.astype(F32)
                for group in range(width // LANES):
                    lanes = slice(group * LANES, (group + 1) * LANES)
                    to = pl.ds(at + group * LANES, LANES)
                    tall = jnp.zeros((sh.levels, LANES), F32)
                    for j in range(4):
                        tall = jnp.where(
                            zcells == levels[:, lanes] + j, weights[4 + j : 5 + j, lanes], tall
                        )
                    upward[slot, :, to] = tall
                    wide = [jnp.zeros((LANES, LANES), BF16)] * 2
                    for j in range(4):
                        here = ycells == (cells_y[:, lanes] + float(j)).astype(BF16)
                        for part, source in ((0, top), (1, rest)):
                            wide[part] = jnp.where(here, source[j : j + 1, lanes], wide[part])
                    for part in range(2):
                        across[slot, window, part * LANES : (part + 1) * LANES, to] = wide[part]

            def sweep(window):
                def body(i, carry):
                    chunk(window, pl.multiple_of(i * width, width))
                    return carry

                lax.fori_loop(0, sh.markers // width, body, 0)

            sweep(0)

            @pl.when(jnp.logical_not(narrow))
            def _():
                sweep(1)


def make_tables(sh, plan, marker_cell, after):
    across, upward, info = pl.pallas_call(
        lambda *refs: table_kernel(sh, *refs),
        out_shape=[
            pltpu.VMEM((sh.slots, 2, 2 * LANES, sh.markers), BF16),
            pltpu.VMEM((sh.slots, sh.levels, sh.markers), F32),
            pltpu.SMEM((2 * sh.slots,), jnp.int32),
        ],
        in_specs=[SM, HB, VM],
        out_specs=[VM, VM, SM],
        scratch_shapes=[
            pltpu.VMEM((sh.slots, 8, sh.markers), jnp.int32),
            pltpu.SemaphoreType.DMA((sh.slots,)),
        ],
        compiler_params=PARAMS,
        name="tables",
    )(plan, marker_cell, after)
    return in_vmem(across), in_vmem(upward), in_smem(info)


def blade_kernel(sh, plan, phases, twist, angle, after, blades):
    del after
    blades[0] = jnp.sin(angle[...])
    blades[1] = jnp.cos(angle[...])
    sin_twist = jnp.sin(twist[...])
    cos_twist = jnp.cos(twist[...])
    owner = iota((1, LANES), 1)
    rows = iota((sh.slots * sh.groups, LANES), 0) % sh.slots
    phase = jnp.zeros((1, LANES), F32)
    for step in range(sh.steps):
        for slot in range(sh.slots):
            rotor = jnp.maximum(rotor_at(sh, plan, slot), 0)
            here = owner == step * sh.slots + slot
            phase = jnp.where(here, phases[step, rotor].astype(F32), phase)
    pitch = PITCH_AMP * jnp.sin((2.0 * math.pi / PHASES) * phase)
    sin_pitch = jnp.sin(pitch)
    cos_pitch = jnp.cos(pitch)
    for step in range(sh.steps):
        parts = []
        for part in (sin_pitch, cos_pitch):
            total = jnp.zeros((sh.slots * sh.groups, LANES), F32)
            for slot in range(sh.slots):
                lane = step * sh.slots + slot
                total = jnp.where(rows == slot, part[:, lane : lane + 1], total)
            parts.append(total)
        blades[2 + 2 * step] = sin_twist * parts[1] + cos_twist * parts[0]
        blades[3 + 2 * step] = cos_twist * parts[1] - sin_twist * parts[0]


def make_blades(sh, plan, phases, twist, angle, after):
    rows = sh.slots * sh.groups
    return pl.pallas_call(
        lambda *refs: blade_kernel(sh, *refs),
        out_shape=pltpu.VMEM((2 + 2 * sh.steps, rows, LANES), F32),
        in_specs=[SM, SM, VM, VM, VM],
        out_specs=VM,
        compiler_params=PARAMS,
        name="blades",
    )(plan, jnp.transpose(phases), twist, angle, after)


SAMPLE_CHUNK = 4096
SPREAD_CHUNK = 4096


def split(value):
    top = value.astype(BF16)
    return top, (value - top.astype(F32)).astype(BF16)


def marker_kernel(
    sh, step, plan, info, across, upward, area, speed, blades, filt_old, west, east, *refs
):
    sections = refs[: sh.tiles]
    filt_new, loads = refs[sh.tiles : sh.tiles + 2]
    forces = refs[sh.tiles + 2 : 2 * sh.tiles + 2]
    around, sampled, weighted, spread = refs[2 * sh.tiles + 2 :]
    me = lax.axis_index("gy")
    tall = 3 * sh.levels
    for shift in range(sh.tiles):
        around[lax.rem(me + sh.tiles - shift, sh.tiles)] = sections[shift][...]
    spread[...] = jnp.zeros(spread.shape, F32)

    def window_of(slot, window):
        start = info[2 * slot] + window * LANES
        tile = start // LANES
        return tile, jnp.minimum(tile + 1, sh.tiles - 1), start - tile * LANES

    def windows(slot, body):
        @pl.when(rotor_at(sh, plan, slot) >= 0)
        def _():
            body(0)

            @pl.when(info[2 * slot + 1] > 1)
            def _():
                body(1)

    for slot in range(sh.slots):
        rows = pl.ds(slot * tall, tall)

        def sample(window):
            tile, after, offset = window_of(slot, window)
            both = jnp.concatenate([around[tile, rows, :], around[after, rows, :]], axis=1)
            seen = pltpu.roll(both, lax.rem(2 * LANES - offset, 2 * LANES), 1)[:, :LANES]
            top, rest = split(seen)
            left = jnp.concatenate([top, rest], axis=0)
            left = jnp.concatenate([left, left], axis=1)

            def chunk(i, carry):
                at = pl.multiple_of(i * SAMPLE_CHUNK, SAMPLE_CHUNK)
                value = jnp.dot(
                    left,
                    across[slot, window, :, pl.ds(at, SAMPLE_CHUNK)],
                    preferred_element_type=F32,
                )
                value = value[:tall] + value[tall:]
                heights = upward[slot, :, pl.ds(at, SAMPLE_CHUNK)]
                for axis in range(3):
                    part = jnp.sum(
                        value[axis * sh.levels : (axis + 1) * sh.levels] * heights,
                        axis=0,
                        keepdims=True,
                    )
                    for group in range(SAMPLE_CHUNK // LANES):
                        row = (i * (SAMPLE_CHUNK // LANES) + group) * sh.slots + slot
                        piece = part[:, group * LANES : (group + 1) * LANES]
                        if window:
                            piece = piece + sampled[axis, pl.ds(row, 1), :]
                        sampled[axis, pl.ds(row, 1), :] = piece
                return carry

            lax.fori_loop(0, sh.markers // SAMPLE_CHUNK, chunk, 0)

        windows(slot, sample)

    felt = []
    for axis in range(3):
        old = filt_old[axis]
        value = old + MIX * (sampled[axis] - old)
        filt_new[axis] = value
        felt.append(value)
    sin_t = blades[0]
    cos_t = blades[1]
    tangent = speed[...] + sin_t * felt[1] - cos_t * felt[2]
    square = felt[0] * felt[0] + tangent * tangent
    inverse = 1.0 / jnp.sqrt(square)
    sin_p = felt[0] * inverse
    cos_p = tangent * inverse
    sin_b = blades[2 + 2 * step]
    cos_b = blades[3 + 2 * step]
    sin_a = sin_p * cos_b - cos_p * sin_b
    cos_a = cos_p * cos_b + sin_p * sin_b
    lift = (2.0 * math.pi) * sin_a * cos_a
    drag = 0.02 + sin_a * sin_a
    dynamic = 0.5 * area[...] * square
    around_axis = dynamic * (lift * sin_p - drag * cos_p)
    loads[0] = dynamic * (lift * cos_p + drag * sin_p)
    loads[1] = -around_axis * sin_t
    loads[2] = around_axis * cos_t

    for slot in range(sh.slots):
        rows = pl.ds(slot * tall, tall)

        def spread_out(window):
            tile, after, offset = window_of(slot, window)

            def chunk(i, total):
                at = pl.multiple_of(i * SPREAD_CHUNK, SPREAD_CHUNK)
                for group in range(SPREAD_CHUNK // LANES):
                    heights = upward[slot, :, pl.ds(at + group * LANES, LANES)]
                    row = (i * (SPREAD_CHUNK // LANES) + group) * sh.slots + slot
                    parts = [heights * loads[axis, pl.ds(row, 1), :] for axis in range(3)]
                    top, rest = split(jnp.concatenate(parts, axis=0))
                    weighted[:tall, group * LANES : (group + 1) * LANES] = top
                    weighted[tall:, group * LANES : (group + 1) * LANES] = rest
                return total + lax.dot_general(
                    weighted[...],
                    across[slot, window, :, pl.ds(at, SPREAD_CHUNK)],
                    (((1,), (1,)), ((), ())),
                    preferred_element_type=F32,
                )

            total = lax.fori_loop(
                0,
                sh.markers // SPREAD_CHUNK,
                chunk,
                jnp.zeros((2 * tall, 2 * LANES), F32),
            )
            total = total[:tall] + total[tall:]
            total = -SPREAD * (total[:, :LANES] + total[:, LANES:])
            both = jnp.concatenate([total, jnp.zeros((tall, LANES), F32)], axis=1)
            both = pltpu.roll(both, offset, 1)
            spread[tile, rows, :] = spread[tile, rows, :] + both[:, :LANES]
            spread[after, rows, :] = spread[after, rows, :] + both[:, LANES:]

        windows(slot, spread_out)

    lanes = iota((sh.levels, LANES), 1)
    for shift in range(sh.tiles):
        tile = lax.rem(me + shift, sh.tiles)
        forces[shift][: sh.section, :] = spread[tile]
        before = lax.rem(tile + sh.tiles - 1, sh.tiles)
        after = lax.rem(tile + 1, sh.tiles)
        ghosts = jnp.zeros((sh.levels, LANES), F32)
        for k in range(3 * sh.slots):
            at = pl.ds(k * sh.levels, sh.levels)
            left = jnp.broadcast_to(spread[before, at, :][:, LANES - 1 :], (sh.levels, LANES))
            right = jnp.broadcast_to(spread[after, at, :][:, :1], (sh.levels, LANES))
            ghosts = jnp.where(lanes == 2 * k, left, ghosts)
            ghosts = jnp.where(lanes == 2 * k + 1, right, ghosts)
        forces[shift][sh.section : sh.section + sh.levels, :] = ghosts
    forces[1][sh.section + sh.levels :, :] = east[...]
    forces[sh.tiles - 1][sh.section + sh.levels :, :] = west[...]


def do_markers(sh, step, plan, tables, fixed, blades, filt, columns, sections):
    across, upward, info = tables
    rows = sh.slots * sh.groups
    dense = pltpu.VMEM((3, rows, LANES), F32)
    plain = sh.section + sh.levels
    extra = columns[0].shape[0]
    forces = [
        pltpu.VMEM((plain + (extra if by in (1, sh.tiles - 1) else 0), LANES), F32)
        for by in range(sh.tiles)
    ]
    out = pl.pallas_call(
        lambda *refs: marker_kernel(sh, step, *refs),
        out_shape=[dense, dense] + forces,
        in_specs=[SM, SM] + [VM] * (8 + sh.tiles),
        out_specs=[VM] * (2 + sh.tiles),
        scratch_shapes=[
            pltpu.VMEM((sh.tiles, sh.section, LANES), F32),
            pltpu.VMEM((3, rows, LANES), F32),
            pltpu.VMEM((6 * sh.levels, SPREAD_CHUNK), BF16),
            pltpu.VMEM((sh.tiles, sh.section, LANES), F32),
        ],
        compiler_params=PARAMS,
        name="markers",
    )(plan, info, across, upward, *fixed, blades, filt, *columns, *sections)
    return in_vmem(out[0]), in_vmem(out[1]), out[2:]


def edge_kernel(sh, has_edges, plan, f, *refs):
    low, high = refs[:2] if has_edges else (None, None)
    refs = refs[2 * has_edges :]
    forces = refs[: sh.tiles]
    outs = refs[sh.tiles + 1 :]
    first = sh.section + sh.levels
    me = lax.axis_index("gy")
    lanes = iota((sh.levels, LANES), 1)
    per = LANES // sh.levels
    corner_rows = pl.ds(first + (19 + per - 1) // per * sh.xs, sh.levels)
    blank = jnp.zeros((sh.levels, LANES), F32)
    planes_at = (0, sh.xs - 1)
    corner = []
    from_left = forces[1][corner_rows, :]
    from_right = forces[sh.tiles - 1][corner_rows, :]
    for q in range(19):
        a = pltpu.roll(from_left, (LANES - 2 * q) % LANES, 1)
        b = pltpu.roll(from_right, (LANES + 2 - 2 * q) % LANES, 1)
        corner.append(jnp.where(lanes < 2, a, jnp.where(lanes < 4, b, 1.0)))
    corner_force = [blank, blank, blank]
    edge_force = [[blank, blank, blank], [blank, blank, blank]]
    for shift in range(sh.tiles):
        owner = lax.rem(me + sh.tiles - shift, sh.tiles)
        ghosts = forces[shift][sh.section : sh.section + sh.levels, :]
        for slot in range(sh.slots):
            x = plane_at(sh, plan, owner, slot)
            for axis in range(3):
                k = slot * 3 + axis
                piece = forces[shift][k * sh.levels : (k + 1) * sh.levels, :]
                for which in range(2):
                    here = jnp.asarray(x == planes_at[which])
                    edge_force[which][axis] = edge_force[which][axis] + jnp.where(here, piece, 0.0)
                    for side in range(2):
                        lane = 2 * side + which
                        moved = pltpu.roll(ghosts, (lane - 2 * k - side) % LANES, 1)
                        corner_force[axis] = corner_force[axis] + jnp.where(
                            jnp.logical_and(here, lanes == lane), moved, 0.0
                        )
    corner_post = collide(corner, corner_force, [q for q in PLUS + MINUS if DIRS[q][1]])
    for which, wanted in ((1, PLUS), (0, MINUS)):
        planes = plane_of(sh, f, planes_at[which], low, high)
        post = collide(planes, edge_force[which], wanted)
        out = outs[0] if which else outs[1]
        for k, q in enumerate(wanted):
            value = post[q]
            if DIRS[q][1] == 1:
                value = pltpu.roll(value, 1, 1)
                ghost = pltpu.roll(corner_post[q], (LANES - which) % LANES, 1)
                value = jnp.where(lanes == 0, ghost, value)
            elif DIRS[q][1] == -1:
                value = pltpu.roll(value, LANES - 1, 1)
                ghost = pltpu.roll(corner_post[q], (LANES - 1 - 2 - which) % LANES, 1)
                value = jnp.where(lanes == LANES - 1, ghost, value)
            if DIRS[q][2]:
                value = pltpu.roll(value, DIRS[q][2] % sh.levels, 0)
            out[k] = value


def make_edges(sh, plan, f, edges, forces, after):
    return pl.pallas_call(
        lambda *refs: edge_kernel(sh, bool(edges), *refs),
        out_shape=[pltpu.VMEM((len(PLUS), sh.levels, LANES), F32)] * 2,
        in_specs=[SM] + [VM] * (2 + len(edges) + sh.tiles),
        out_specs=[VM] * 2,
        compiler_params=PARAMS,
        name="edges",
    )(plan, f, *edges, *forces, after)


def bulk_kernel(sh, has_edges, last, plan, f, *refs):
    low, high = refs[:2] if has_edges else (None, None)
    refs = refs[2 * has_edges :]
    loads, filt, out = refs[:3]
    xs = sh.xs
    xrows = iota((xs, LANES), 0)
    if last:
        rows = iota((sh.slots * sh.groups, LANES), 0) % sh.slots
        used = jnp.zeros((sh.slots * sh.groups, LANES), jnp.int32)
        for slot in range(sh.slots):
            there = (rotor_at(sh, plan, slot) >= 0).astype(jnp.int32)
            used = jnp.where(rows == slot, there, used)
        for source, target in ((loads, refs[3]), (filt, refs[4])):
            for axis in range(3):
                target[axis] = jnp.where(used > 0, source[axis], 0.0)

    def level(z, bottom, top):
        at = aligned(z * xs, xs)
        here = []
        for q in range(19):
            tile = f[q, pl.ds(at, xs), :]
            if has_edges and DIRS[q][0] != 0:
                blocked = (DIRS[q][2] == 1 and bottom) or (DIRS[q][2] == -1 and top)
                if not blocked:
                    if DIRS[q][0] == 1:
                        tile = jnp.where(xrows == 0, low[PLUS.index(q), pl.ds(z, 1), :], tile)
                    else:
                        tile = jnp.where(
                            xrows == xs - 1, high[MINUS.index(q), pl.ds(z, 1), :], tile
                        )
            here.append(tile)
        post = collide(here, None, range(19))
        for q in range(19):
            dx, dy, dz = DIRS[q]
            value = post[q]
            if (dz == 1 and top) or (dz == -1 and bottom):
                to, target = OPPOSITE[q], z
            else:
                to, target = q, z + dz
                if dy:
                    value = pltpu.roll(value, dy % LANES, 1)
                if dx:
                    value = pltpu.roll(value, dx % xs, 0)
            out[to, pl.ds(aligned(target * xs, xs), xs), :] = value

    level(0, True, False)

    def middle(z, carry):
        level(z, False, False)
        return carry

    lax.fori_loop(1, sh.levels - 1, middle, 0)
    level(sh.levels - 1, False, True)


def do_bulk(sh, last, plan, f, edges, loads, filt):
    out_shape = [pltpu.VMEM((19, sh.levels * sh.xs, LANES), F32)]
    if last:
        out_shape += [jax.ShapeDtypeStruct(loads.shape, F32)] * 2
    return pl.pallas_call(
        lambda *refs: bulk_kernel(sh, bool(edges), last, *refs),
        out_shape=out_shape,
        in_specs=[SM] + [VM] * (3 + len(edges)),
        out_specs=[VM] * len(out_shape),
        compiler_params=PARAMS,
        name="bulk",
    )(plan, f, *edges, loads, filt)


def patch_kernel(sh, has_edges, last, plan, f, *refs):
    low, high = refs[:2] if has_edges else (None, None)
    refs = refs[2 * has_edges :]
    forces = refs[: sh.tiles]
    out = refs[sh.tiles + 1]
    field, ghost_posts = refs[-3:-1]
    sem = refs[-1]
    me = lax.axis_index("gy")
    xs = sh.xs
    lanes = iota((xs, LANES), 1)
    xrows = iota((xs, LANES), 0)
    per = LANES // sh.levels
    field[...] = jnp.zeros(field.shape, F32)
    ghost_force = [jnp.zeros((xs, LANES), F32) for axis in range(3)]
    for shift in range(sh.tiles):
        owner = lax.rem(me + sh.tiles - shift, sh.tiles)
        ghosts = jnp.transpose(
            jnp.concatenate(
                [
                    forces[shift][sh.section : sh.section + sh.levels, :],
                    jnp.zeros((LANES - sh.levels, LANES), F32),
                ],
                axis=0,
            )
        )
        for slot in range(sh.slots):
            x = plane_at(sh, plan, owner, slot)

            @pl.when(x >= 0)
            def _():
                for axis in range(3):
                    k = slot * 3 + axis
                    at = pl.ds(x, sh.levels, stride=xs)
                    field[axis, at, :] = (
                        field[axis, at, :] + forces[shift][k * sh.levels : (k + 1) * sh.levels, :]
                    )

            for axis in range(3):
                k = slot * 3 + axis
                far = pltpu.roll(ghosts[2 * k + 1 : 2 * k + 2, :], sh.levels, 1)
                piece = ghosts[2 * k : 2 * k + 1, :] + far
                ghost_force[axis] = ghost_force[axis] + jnp.where(xrows == x, piece, 0.0)

    ghost = []
    left, right = forces[1], forces[sh.tiles - 1]
    for q in range(19):
        at = pl.ds(sh.section + sh.levels + q // per * xs, xs)
        shift = (q % per) * sh.levels
        a = pltpu.roll(left[at, :], (LANES - shift) % LANES, 1)
        b = pltpu.roll(right[at, :], (LANES + sh.levels - shift) % LANES, 1)
        ghost.append(jnp.where(lanes < sh.levels, a, jnp.where(lanes < 2 * sh.levels, b, 1.0)))
    posted = collide(ghost, ghost_force, SIDEWAYS)
    for k, q in enumerate(SIDEWAYS):
        value = posted[q]
        if DIRS[q][0]:
            value = pltpu.roll(value, DIRS[q][0] % xs, 0)
        ghost_posts[k] = value

    def plane(k, carry):
        key = plan[k]

        @pl.when(key >= 0)
        def _():
            x = lax.rem(key, xs)
            here = plane_of(sh, f, x, low, high)
            force = [field[axis, pl.ds(x, sh.levels, stride=xs), :] for axis in range(3)]
            post = collide(here, force, range(19))
            rows = sh.levels - 1
            for q in range(19):
                dx, dy, dz = DIRS[q]
                value = post[q]
                moved = pltpu.roll(value, dy % LANES, 1) if dy else value

                def put(dx=dx, dz=dz, q=q, moved=moved):
                    if dz == 0:
                        out[q, pl.ds(x + dx, sh.levels, stride=xs), :] = moved
                    elif dz == 1:
                        out[q, pl.ds(x + dx + xs, rows, stride=xs), :] = moved[:rows]
                    else:
                        out[q, pl.ds(x + dx, rows, stride=xs), :] = moved[1:]

                if dx:
                    pl.when(x != (xs - 1 if dx == 1 else 0))(put)
                else:
                    put()
                if dz == 1:
                    out[OPPOSITE[q], pl.ds(x + rows * xs, 1), :] = value[rows:]
                elif dz == -1:
                    out[OPPOSITE[q], pl.ds(x, 1), :] = value[:1]

        return carry

    lax.fori_loop(0, sh.tiles * sh.slots, plane, 0)

    for k, q in enumerate(SIDEWAYS):
        dy, dz = DIRS[q][1:]
        for z in range(sh.levels):
            if not 0 <= z - dz < sh.levels:
                continue
            at = pl.ds(z * xs, xs)
            value = out[q, at, :]
            if dy == 1:
                other = pltpu.roll(ghost_posts[k], (LANES - z + dz) % LANES, 1)
                value = jnp.where(lanes == 0, other, value)
            else:
                other = pltpu.roll(ghost_posts[k], LANES - 1 - sh.levels - z + dz, 1)
                value = jnp.where(lanes == LANES - 1, other, value)
            out[q, at, :] = value
    if last:
        copy = pltpu.make_async_copy(out, refs[sh.tiles + 2], sem)
        copy.start()
        copy.wait()


def do_patch(sh, last, plan, f, edges, forces, bulk):
    out_shape = [pltpu.VMEM(bulk.shape, F32)]
    if last:
        out_shape.append(jax.ShapeDtypeStruct(bulk.shape, F32))
    return pl.pallas_call(
        lambda *refs: patch_kernel(sh, bool(edges), last, *refs),
        out_shape=out_shape,
        in_specs=[SM] + [VM] * (2 + len(edges) + sh.tiles),
        out_specs=[VM] + [HB] * last,
        scratch_shapes=[
            pltpu.VMEM((3, sh.levels * sh.xs, LANES), F32),
            pltpu.VMEM((len(SIDEWAYS), sh.xs, LANES), F32),
            pltpu.SemaphoreType.DMA,
        ],
        input_output_aliases={2 + len(edges) + sh.tiles: 0},
        compiler_params=PARAMS,
        name="patch",
    )(plan, f, *edges, *forces, bulk)


def finish_kernel(sh, held, low, high, f_old, f, merged, sem):
    del f_old
    rows = iota((8, LANES), 0)
    copies = []
    for side, dirs, edge in ((0, PLUS, low), (1, MINUS, high)):
        at_row = 0 if side == 0 else 7
        first = 0 if side == 0 else sh.xs - 8
        for k, q in enumerate(dirs):
            index = side * len(PLUS) + k
            for z in range(sh.levels):
                value = held[q, z * sh.xs + first : z * sh.xs + first + 8, :]
                blocked = (DIRS[q][2] == 1 and z == 0) or (
                    DIRS[q][2] == -1 and z == sh.levels - 1
                )
                if not blocked:
                    value = jnp.where(rows == at_row, edge[k, z : z + 1, :], value)
                merged[index, z] = value
            copy = pltpu.make_async_copy(
                merged.at[index], f.at[q, :, first : first + 8, :], sem.at[index]
            )
            copy.start()
            copies.append(copy)
    for copy in copies:
        copy.wait()


def finish(sh, held, f, edges):
    f = f.reshape(19, sh.levels, sh.xs, LANES)
    return pl.pallas_call(
        lambda *refs: finish_kernel(sh, *refs),
        out_shape=jax.ShapeDtypeStruct(f.shape, F32),
        in_specs=[VM, VM, VM, HB],
        out_specs=HB,
        scratch_shapes=[
            pltpu.VMEM((2 * len(PLUS), sh.levels, 8, LANES), F32),
            pltpu.SemaphoreType.DMA((2 * len(PLUS),)),
        ],
        input_output_aliases={3: 0},
        compiler_params=PARAMS,
        name="finish",
    )(held, *edges, f)


def by_group(sh, x):
    head = x.shape[:-2]
    x = x.reshape(*head, sh.slots, sh.groups, LANES)
    return jnp.swapaxes(x, -3, -2).reshape(*head, sh.slots * sh.groups, LANES)


def by_slot(sh, x):
    head = x.shape[:-2]
    x = x.reshape(*head, sh.groups, sh.slots, LANES)
    return jnp.swapaxes(x, -3, -2).reshape(*head, sh.slots, sh.markers)


def shifted(x, axis, by):
    count = lax.axis_size(axis)
    return lax.ppermute(x, axis, [(i, (i + by) % count) for i in range(count)])


def local(
    f_in,
    rotor_place,
    marker_cell,
    pitch_phase,
    blade_area,
    blade_twist,
    blade_speed,
    blade_angle,
    filt_in,
):
    sh = Shape(f_in, rotor_place, marker_cell, pitch_phase, filt_in)
    plan, f, sections = start(sh, rotor_place, f_in)
    area, twist, speed, angle = [
        by_group(sh, x[0, 0]) for x in (blade_area, blade_twist, blade_speed, blade_angle)
    ]
    filt = by_group(sh, jnp.swapaxes(filt_in[0, 0], 0, 1))
    edges = ()
    for step in range(sh.steps):
        last = step == sh.steps - 1
        if step:
            sections = make_sections(sh, plan, f, edges)
        sections = [sections[0]] + [
            shifted(sections[by], "gy", by) for by in range(1, sh.tiles)
        ]
        columns = [in_vmem(column) for column in make_columns(sh, f, edges)]
        if step == 0:
            blades = in_vmem(make_blades(sh, plan, pitch_phase, twist, angle, columns[0]))
            tables = make_tables(sh, plan, marker_cell, blades)
        filt, loads, forces = do_markers(
            sh,
            step,
            plan,
            tables,
            (area, speed),
            blades,
            filt,
            columns,
            [in_vmem(section) for section in sections],
        )
        forces = [forces[0]] + [shifted(forces[by], "gy", by) for by in range(1, sh.tiles)]
        forces = [in_vmem(force) for force in forces]
        bulk = do_bulk(sh, last, plan, f, edges, loads, filt)
        if last:
            loads_out, filt_out = bulk[1:]
        bulk = in_vmem(bulk[0])
        sent = make_edges(sh, plan, f, edges, forces, bulk)
        arrived = [shifted(sent[0], "gx", 1), shifted(sent[1], "gx", -1)]
        done = do_patch(sh, last, plan, f, edges, forces, bulk)
        edges = tuple(in_vmem(edge) for edge in arrived)
        f = in_vmem(done[0])
    f = finish(sh, f, done[1], edges)
    loads_out, filt_out = [
        jnp.swapaxes(by_slot(sh, x), 0, 1)[None, None] for x in (loads_out, filt_out)
    ]
    return f, loads_out, filt_out


def solution(mesh):
    in_specs = (
        P(None, None, "gx", "gy"),
        P(),
        P(),
        P(),
        P("gx", "gy", None, None),
        P("gx", "gy", None, None),
        P("gx", "gy", None, None),
        P("gx", "gy", None, None),
        P("gx", "gy", None, None, None),
    )
    out_specs = (
        P(None, None, "gx", "gy"),
        P("gx", "gy", None, None, None),
        P("gx", "gy", None, None, None),
    )
    return jax.shard_map(local, mesh=mesh, in_specs=in_specs, out_specs=out_specs, check_vma=False)
```

```python
import math

import jax
import jax.numpy as jnp
from jax import lax
from jax.experimental import pallas as pl
from jax.experimental.pallas import tpu as pltpu
from jax.sharding import PartitionSpec as P

PHASES = 64
PAIRS = [
    (1, 0, 0),
    (0, 1, 0),
    (0, 0, 1),
    (1, 1, 0),
    (1, -1, 0),
    (1, 0, 1),
    (1, 0, -1),
    (0, 1, 1),
    (0, 1, -1),
]
DIRS = [(0, 0, 0)]
for along in PAIRS:
    DIRS.append(along)
    DIRS.append(tuple(-part for part in along))
OPPOSITE = [0] + [q + 1 if q % 2 else q - 1 for q in range(1, 19)]
PLUS = [q for q in range(19) if DIRS[q][0] == 1]
MINUS = [q for q in range(19) if DIRS[q][0] == -1]
SIDEWAYS = [q for q in range(19) if DIRS[q][1] != 0]
OMEGA = 1.0 / 0.6
KEEP = 1.0 - OMEGA
GUO = 1.0 - 0.5 * OMEGA
SPREAD = 0.01
MIX = 0.5
PITCH_AMP = 0.2
LANES = 128
F32 = jnp.float32
BF16 = jnp.bfloat16
VMEM_LIMIT = 8 * 1024 * 1024


def iota(shape, axis):
    return lax.broadcasted_iota(jnp.int32, shape, axis)


def aligned(value, by):
    return value if isinstance(value, int) else pl.multiple_of(value, by)


def wrapped(value):
    return value % LANES if isinstance(value, int) else lax.rem(value, LANES)


def moments(f):
    sums = [f[2 * k + 1] + f[2 * k + 2] for k in range(9)]
    gaps = [f[2 * k + 1] - f[2 * k + 2] for k in range(9)]
    density = f[0]
    for part in sums:
        density = density + part
    momentum = []
    for axis in range(3):
        total = None
        for k in range(9):
            sign = PAIRS[k][axis]
            if sign == 0:
                continue
            if total is None:
                total = gaps[k]
            else:
                total = total + gaps[k] if sign > 0 else total - gaps[k]
        momentum.append(total)
    return density, momentum


def collide(f, force, wanted):
    density, momentum = moments(f)
    inverse = 1.0 / density
    relaxed = OMEGA * density
    if force is None:
        v = [momentum[a] * inverse for a in range(3)]
        square = v[0] * v[0] + v[1] * v[1] + v[2] * v[2]
        base = relaxed * (1.0 - 1.5 * square)
        drive = [OMEGA * momentum[a] for a in range(3)]
        bend = [4.5 * part for part in drive]
    else:
        v = [(momentum[a] + 0.5 * force[a]) * inverse for a in range(3)]
        square = v[0] * v[0] + v[1] * v[1] + v[2] * v[2]
        work = v[0] * force[0] + v[1] * force[1] + v[2] * force[2]
        base = relaxed * (1.0 - 1.5 * square) - (3.0 * GUO) * work
        drive = [relaxed * v[a] + GUO * force[a] for a in range(3)]
        bend = [(4.5 * relaxed) * v[a] + (9.0 * GUO) * force[a] for a in range(3)]
    post = {}
    if 0 in wanted:
        post[0] = KEEP * f[0] + base * (1.0 / 3.0)
    scaled = {}
    for weight in (18.0, 36.0):
        scaled[weight] = (
            base * (1.0 / weight),
            [part * (3.0 / weight) for part in drive],
            [part * (1.0 / weight) for part in bend],
        )

    def along(k, parts):
        total = None
        for axis in range(3):
            sign = PAIRS[k][axis]
            if sign == 0:
                continue
            if total is None:
                total = parts[axis]
            else:
                total = total + parts[axis] if sign > 0 else total - parts[axis]
        return total

    for k in range(9):
        if 2 * k + 1 not in wanted and 2 * k + 2 not in wanted:
            continue
        level, drives, bends = scaled[18.0 if k < 3 else 36.0]
        even = level + along(k, v) * along(k, bends)
        odd = along(k, drives)
        if 2 * k + 1 in wanted:
            post[2 * k + 1] = KEEP * f[2 * k + 1] + (even + odd)
        if 2 * k + 2 in wanted:
            post[2 * k + 2] = KEEP * f[2 * k + 2] + (even - odd)
    return post


def outside(q, levels, rows):
    if DIRS[q][2] == 1:
        return rows == 0
    if DIRS[q][2] == -1:
        return rows == levels - 1
    return None


class Shape:
    def __init__(self, f_in, rotor_place, marker_cell, pitch_phase, filt_in):
        self.levels = f_in.shape[1]
        self.xs = f_in.shape[2]
        self.rotors = rotor_place.shape[0]
        self.steps = pitch_phase.shape[1]
        self.markers = marker_cell.shape[1]
        self.slots = filt_in.shape[2]
        self.tiles = lax.axis_size("gy")
        self.groups = self.markers // LANES
        self.section = self.slots * 3 * self.levels


def in_vmem(x):
    return pltpu.with_memory_space_constraint(x, pltpu.VMEM)


def in_hbm(x):
    return pltpu.with_memory_space_constraint(x, pltpu.HBM)


def in_smem(x):
    return pltpu.with_memory_space_constraint(x, pltpu.SMEM)


VM = pl.BlockSpec(memory_space=pltpu.VMEM)
SM = pl.BlockSpec(memory_space=pltpu.SMEM)
HB = pl.BlockSpec(memory_space=pl.ANY)
PARAMS = pltpu.CompilerParams(vmem_limit_bytes=VMEM_LIMIT)


def write_plan(sh, place, plan):
    row = lax.axis_index("gx")
    shape = (sh.tiles, sh.rotors)
    mine = jnp.logical_and(place[2:3, :] == iota(shape, 0), place[0:1, :] == row)
    keys = iota(shape, 1) * sh.xs + place[1:2, :]
    none = sh.rotors * sh.xs
    last = jnp.full((sh.tiles, 1), -1, jnp.int32)
    for slot in range(sh.slots):
        left = jnp.logical_and(mine, keys > last)
        last = jnp.min(jnp.where(left, keys, none), axis=1, keepdims=True)
        for owner in range(sh.tiles):
            key = last[owner, 0]
            plan[owner * sh.slots + slot] = jnp.where(key < none, key, -1)


def plane_at(sh, plan, owner, slot):
    key = plan[owner * sh.slots + slot]
    return jnp.where(key < 0, -1, lax.rem(key, sh.xs))


def rotor_at(sh, plan, slot):
    key = plan[lax.axis_index("gy") * sh.slots + slot]
    return jnp.where(key < 0, -1, lax.div(key, sh.xs))


def plane_of(sh, f, x, low, high):
    rows = iota((sh.levels, LANES), 0)
    planes = []
    for q in range(19):
        value = f[q, pl.ds(x, sh.levels, stride=sh.xs), :]
        if low is not None and DIRS[q][0] != 0:
            if DIRS[q][0] == 1:
                other, at = low[PLUS.index(q)], 0
            else:
                other, at = high[MINUS.index(q)], sh.xs - 1
            here = jnp.asarray(x == at)
            skip = outside(q, sh.levels, rows)
            use = here if skip is None else jnp.logical_and(here, jnp.logical_not(skip))
            value = jnp.where(use, other, value)
        planes.append(value)
    return planes


def write_sections(sh, plan, f, low, high, outs):
    me = lax.axis_index("gy")
    for shift in range(sh.tiles):
        owner = lax.rem(me + shift, sh.tiles)
        for slot in range(sh.slots):
            x = plane_at(sh, plan, owner, slot)

            @pl.when(x >= 0)
            def _():
                planes = plane_of(sh, f, x, low, high)
                density, momentum = moments(planes)
                inverse = 1.0 / density
                for axis in range(3):
                    at = (slot * 3 + axis) * sh.levels
                    outs[shift][at : at + sh.levels, :] = momentum[axis] * inverse

            @pl.when(x < 0)
            def _():
                at = slot * 3 * sh.levels
                outs[shift][at : at + 3 * sh.levels, :] = jnp.zeros((3 * sh.levels, LANES), F32)


def sincos(x):
    turns = jnp.floor(x * (2.0 / math.pi) + 0.5)
    r = x - turns * 1.5703125
    r = r - turns * 4.837512969970703125e-4
    r = r - turns * 7.549789954891882e-8
    r2 = r * r
    sin_r = r + r * r2 * (
        -1.0 / 6 + r2 * (1.0 / 120 + r2 * (-1.0 / 5040 + r2 * (1.0 / 362880)))
    )
    cos_r = (
        1.0
        - 0.5 * r2
        + r2
        * r2
        * (1.0 / 24 + r2 * (-1.0 / 720 + r2 * (1.0 / 40320 - r2 * (1.0 / 3628800))))
    )
    quarter = turns.astype(jnp.int32)
    swap = (quarter & 1) == 1
    sin_x = jnp.where(swap, cos_r, sin_r)
    cos_x = jnp.where(swap, sin_r, cos_r)
    sin_x = jnp.where((quarter & 2) == 2, -sin_x, sin_x)
    cos_x = jnp.where(((quarter + 1) & 2) == 2, -cos_x, cos_x)
    return sin_x, cos_x


def write_blades(sh, plan, phases, twist, angle, blades):
    blades[0], blades[1] = sincos(angle[...])
    sin_twist, cos_twist = sincos(twist[...])
    owner = iota((1, LANES), 1)
    rows = iota((sh.slots * sh.groups, LANES), 0) % sh.slots
    phase = jnp.zeros((1, LANES), F32)
    for step in range(sh.steps):
        for slot in range(sh.slots):
            rotor = jnp.maximum(rotor_at(sh, plan, slot), 0)
            here = owner == step * sh.slots + slot
            phase = jnp.where(here, phases[step, rotor].astype(F32), phase)
    pitch = PITCH_AMP * sincos((2.0 * math.pi / PHASES) * phase)[0]
    pitched = sincos(pitch)
    for step in range(sh.steps):
        parts = []
        for part in pitched:
            total = jnp.zeros((sh.slots * sh.groups, LANES), F32)
            for slot in range(sh.slots):
                lane = step * sh.slots + slot
                total = jnp.where(rows == slot, part[:, lane : lane + 1], total)
            parts.append(total)
        blades[2 + 2 * step] = sin_twist * parts[1] + cos_twist * parts[0]
        blades[3 + 2 * step] = cos_twist * parts[1] - sin_twist * parts[0]


def start_kernel(
    sh, place_in, phases_in, twist_in, angle_in, plan, blades, place, phases, twist, angle, sems
):
    pairs = ((place_in, place), (phases_in, phases), (angle_in, angle), (twist_in, twist))
    copies = [pltpu.make_async_copy(*pair, sems.at[k]) for k, pair in enumerate(pairs)]
    for copy in copies:
        copy.start()
    for copy in copies:
        copy.wait()
    write_plan(sh, place, plan)
    write_blades(sh, plan, phases, twist, angle, blades)


def start(sh, rotor_place, phases, twist, angle):
    rows = sh.slots * sh.groups
    plan, blades = pl.pallas_call(
        lambda *refs: start_kernel(sh, *refs),
        out_shape=[
            pltpu.SMEM((sh.tiles * sh.slots,), jnp.int32),
            pltpu.VMEM((2 + 2 * sh.steps, rows, LANES), F32),
        ],
        in_specs=[HB] * 4,
        out_specs=[SM, VM],
        scratch_shapes=[
            pltpu.VMEM((3, sh.rotors), jnp.int32),
            pltpu.SMEM((sh.steps, sh.rotors), jnp.int32),
            pltpu.VMEM((rows, LANES), F32),
            pltpu.VMEM((rows, LANES), F32),
            pltpu.SemaphoreType.DMA((4,)),
        ],
        compiler_params=PARAMS,
        name="start",
    )(
        in_hbm(jnp.transpose(rotor_place)),
        in_hbm(jnp.transpose(phases)),
        in_hbm(twist),
        in_hbm(angle),
    )
    return in_smem(plan), in_vmem(blades)


def section_kernel(sh, has_edges, plan, f, *refs):
    low, high = refs[:2] if has_edges else (None, None)
    write_sections(sh, plan, f, low, high, refs[-sh.tiles :])


def make_sections(sh, plan, f, edges, after):
    return pl.pallas_call(
        lambda *refs: section_kernel(sh, bool(edges), *refs),
        out_shape=[pltpu.VMEM((sh.section, LANES), F32)] * sh.tiles,
        in_specs=[SM] + [VM] * (1 + len(edges) + len(after)),
        out_specs=[VM] * sh.tiles,
        compiler_params=PARAMS,
        name="sections",
    )(plan, f, *edges, *after)


def column_kernel(sh, has_edges, *refs):
    f = refs[1]
    low, high = refs[2:4] if has_edges else (None, None)
    out = refs[-1]
    pairs = iota((sh.xs, LANES), 1) // 2
    xrows = iota((sh.xs, LANES), 0)
    per = LANES // (2 * sh.levels)
    groups = (19 + per - 1) // per
    for group in range(groups):
        total = jnp.ones((sh.xs, LANES), F32)
        for q in range(group * per, min(19, (group + 1) * per)):
            for z in range(sh.levels):
                tile = f[q, z * sh.xs : (z + 1) * sh.xs, :]
                if has_edges and DIRS[q][0] != 0:
                    blocked = (DIRS[q][2] == 1 and z == 0) or (
                        DIRS[q][2] == -1 and z == sh.levels - 1
                    )
                    if not blocked:
                        if DIRS[q][0] == 1:
                            tile = jnp.where(xrows == 0, low[PLUS.index(q), z : z + 1, :], tile)
                        else:
                            tile = jnp.where(
                                xrows == sh.xs - 1, high[MINUS.index(q), z : z + 1, :], tile
                            )
                pair = (q % per) * sh.levels + z
                total = jnp.where(
                    pairs == pair, pltpu.roll(tile, (2 * pair + 1) % LANES, 1), total
                )
        out[group * sh.xs : (group + 1) * sh.xs, :] = total
    zpairs = iota((sh.levels, LANES), 1) // 2
    corners = jnp.ones((sh.levels, LANES), F32)
    for which, x in ((0, 0), (1, sh.xs - 1)):
        planes = plane_of(sh, f, x, low, high)
        for q in range(19):
            pair = 2 * q + which
            corners = jnp.where(zpairs == pair, pltpu.roll(planes[q], 2 * pair + 1, 1), corners)
    out[groups * sh.xs :, :] = corners


def column_rows(sh):
    per = LANES // (2 * sh.levels)
    return (19 + per - 1) // per * sh.xs


def make_columns(sh, plan, f, edges):
    return pl.pallas_call(
        lambda *refs: column_kernel(sh, bool(edges), *refs),
        out_shape=pltpu.VMEM((column_rows(sh) + sh.levels, LANES), F32),
        in_specs=[SM] + [VM] * (1 + len(edges)),
        out_specs=VM,
        compiler_params=PARAMS,
        name="columns",
    )(plan, f, *edges)


def peskin(offsets):
    distance = jnp.abs(offsets)
    near_arg = jnp.maximum(1.0 + 4.0 * distance - 4.0 * distance * distance, 1.0)
    far_arg = jnp.maximum(-7.0 + 12.0 * distance - 4.0 * distance * distance, 1.0)
    near = distance <= 1.0
    root = jnp.sqrt(jnp.where(near, near_arg, far_arg))
    return (jnp.where(near, 3.0, 5.0) - 2.0 * distance + jnp.where(near, root, -root)) * 0.125


TABLE_CHUNK = 1024


def table_kernel(sh, plan, cells, after, across, upward, info, codes, lines, sem):
    del after
    ids = [rotor_at(sh, plan, slot) for slot in range(sh.slots)]
    copies = []
    for slot in range(sh.slots):
        first = pl.multiple_of(jnp.maximum(ids[slot], 0) // 8 * 8, 8)
        copy = pltpu.make_async_copy(cells.at[pl.ds(first, 8), :], codes.at[slot], sem.at[slot])
        copy.start()
        copies.append(copy)
    width = min(TABLE_CHUNK, sh.markers)
    part = iota((8, width), 0)
    spanwise = part < 4
    cell_bits = 6 + sh.levels.bit_length() - 1
    quarter = LANES // 4
    packed = 16
    ycells = [
        (iota((packed, LANES), 0) + first).astype(F32).astype(BF16)
        for first in range(0, quarter, packed)
    ]
    zcells = iota((sh.levels, LANES), 0)
    for slot in range(sh.slots):
        copies[slot].wait()

        @pl.when(ids[slot] >= 0)
        def _():
            line = ids[slot] % 8
            every = codes[slot, pl.ds(line, 1), :] >> cell_bits
            lowest = jnp.min(every)
            highest = jnp.max(every)
            narrow = highest - lowest + 4 <= LANES
            start = jnp.where(narrow, lowest, lowest // LANES * LANES)
            info[2 * slot] = start
            info[2 * slot + 1] = jnp.where(narrow, 1, 2)

            def chunk(window, at):
                code = codes[slot, pl.ds(line, 1), pl.ds(at, width)]
                cells = (code >> cell_bits) - (start + window * LANES)
                levels = (code >> 6) & (sh.levels - 1)
                eighths = jnp.where(spanwise, code >> 3, code) & 7
                corner = jnp.where(spanwise, (part - cells) & 3, part - 4)
                weights = peskin(corner.astype(F32) - 1.0 - eighths.astype(F32) * 0.125)
                places = ((cells + corner - part) >> 2).astype(F32)
                top = weights.astype(BF16).astype(F32)
                rest = weights - top
                lines[0] = places
                lines[1] = top
                lines[2] = rest
                lines[3] = weights
                for group in range(width // LANES):
                    lanes = slice(group * LANES, (group + 1) * LANES)
                    to = pl.ds(at + group * LANES, LANES)
                    tall = jnp.zeros((sh.levels, LANES), F32)
                    for j in range(4):
                        tall = jnp.where(
                            zcells == levels[:, lanes] + j, lines[3, 4 + j : 5 + j, lanes], tall
                        )
                    upward[slot, :, to] = tall

                    def spread_line(k, kind):
                        line = lines[k, kind : kind + 1, lanes]
                        return jnp.broadcast_to(line, (packed, LANES)).astype(BF16)

                    for kind in range(4):
                        spot, high, low = [spread_line(k, kind) for k in range(3)]
                        for k, cell in enumerate(ycells):
                            here = cell == spot
                            for half, source in ((0, high), (1, low)):
                                row = half * LANES + kind * quarter + k * packed
                                across[slot, window, row : row + packed, to] = jnp.where(
                                    here, source, jnp.zeros((), BF16)
                                )

            def sweep(window):
                def body(i, carry):
                    chunk(window, pl.multiple_of(i * width, width))
                    return carry

                lax.fori_loop(0, sh.markers // width, body, 0)

            sweep(0)

            @pl.when(jnp.logical_not(narrow))
            def _():
                sweep(1)


def make_tables(sh, plan, marker_cell, after):
    across, upward, info = pl.pallas_call(
        lambda *refs: table_kernel(sh, *refs),
        out_shape=[
            pltpu.VMEM((sh.slots, 2, 2 * LANES, sh.markers), BF16),
            pltpu.VMEM((sh.slots, sh.levels, sh.markers), F32),
            pltpu.SMEM((2 * sh.slots,), jnp.int32),
        ],
        in_specs=[SM, HB, VM],
        out_specs=[VM, VM, SM],
        scratch_shapes=[
            pltpu.VMEM((sh.slots, 8, sh.markers), jnp.int32),
            pltpu.VMEM((4, 8, min(TABLE_CHUNK, sh.markers)), F32),
            pltpu.SemaphoreType.DMA((sh.slots,)),
        ],
        compiler_params=PARAMS,
        name="tables",
    )(plan, marker_cell, after)
    return in_vmem(across), in_vmem(upward), in_smem(info)


SAMPLE_CHUNK = 8192
SPREAD_CHUNK = 8192


def split(value):
    top = value.astype(BF16)
    return top, (value - top.astype(F32)).astype(BF16)


def marker_kernel(
    sh, step, plan, info, across, upward, area, speed, blades, filt_old, columns, *refs
):
    sections = refs[: sh.tiles]
    filt_new, loads = refs[sh.tiles : sh.tiles + 2]
    forces = refs[sh.tiles + 2 : 2 * sh.tiles + 2]
    around, sampled, weighted, spread = refs[2 * sh.tiles + 2 :]
    me = lax.axis_index("gy")
    tall = 3 * sh.levels
    quarter = LANES // 4
    rows = iota((LANES, LANES), 0)
    kinds = iota((LANES, LANES), 1)
    by_class = (rows == kinds % quarter * 4 + kinds // quarter).astype(F32).astype(BF16)
    from_class = (kinds == rows % quarter * 4 + rows // quarter).astype(F32).astype(BF16)
    for shift in range(sh.tiles):
        around[lax.rem(me + sh.tiles - shift, sh.tiles)] = sections[shift][...]
    spread[...] = jnp.zeros(spread.shape, F32)

    def window_of(slot, window):
        start = info[2 * slot] + window * LANES
        tile = start // LANES
        return tile, jnp.minimum(tile + 1, sh.tiles - 1), start - tile * LANES

    def windows(slot, body):
        @pl.when(rotor_at(sh, plan, slot) >= 0)
        def _():
            body(0)

            @pl.when(info[2 * slot + 1] > 1)
            def _():
                body(1)

    for slot in range(sh.slots):
        rows = pl.ds(slot * tall, tall)

        def sample(window):
            tile, after, offset = window_of(slot, window)
            both = jnp.concatenate([around[tile, rows, :], around[after, rows, :]], axis=1)
            seen = pltpu.roll(both, lax.rem(2 * LANES - offset, 2 * LANES), 1)[:, :LANES]
            top, rest = split(seen)
            left = jnp.concatenate([top, rest], axis=0)
            left = jnp.dot(left, by_class, preferred_element_type=F32).astype(BF16)
            left = jnp.concatenate([left, left], axis=1)

            def chunk(i, carry):
                at = pl.multiple_of(i * SAMPLE_CHUNK, SAMPLE_CHUNK)
                value = jnp.dot(
                    left,
                    across[slot, window, :, pl.ds(at, SAMPLE_CHUNK)],
                    preferred_element_type=F32,
                )
                value = value[:tall] + value[tall:]
                heights = upward[slot, :, pl.ds(at, SAMPLE_CHUNK)]
                for axis in range(3):
                    part = jnp.sum(
                        value[axis * sh.levels : (axis + 1) * sh.levels] * heights,
                        axis=0,
                        keepdims=True,
                    )
                    for group in range(SAMPLE_CHUNK // LANES):
                        row = (i * (SAMPLE_CHUNK // LANES) + group) * sh.slots + slot
                        piece = part[:, group * LANES : (group + 1) * LANES]
                        if window:
                            piece = piece + sampled[axis, pl.ds(row, 1), :]
                        sampled[axis, pl.ds(row, 1), :] = piece
                return carry

            lax.fori_loop(0, sh.markers // SAMPLE_CHUNK, chunk, 0)

        windows(slot, sample)

    felt = []
    for axis in range(3):
        old = filt_old[axis]
        value = old + MIX * (sampled[axis] - old)
        filt_new[axis] = value
        felt.append(value)
    sin_t = blades[0]
    cos_t = blades[1]
    tangent = speed[...] + sin_t * felt[1] - cos_t * felt[2]
    square = felt[0] * felt[0] + tangent * tangent
    inverse = 1.0 / jnp.sqrt(square)
    sin_p = felt[0] * inverse
    cos_p = tangent * inverse
    sin_b = blades[2 + 2 * step]
    cos_b = blades[3 + 2 * step]
    sin_a = sin_p * cos_b - cos_p * sin_b
    cos_a = cos_p * cos_b + sin_p * sin_b
    lift = (2.0 * math.pi) * sin_a * cos_a
    drag = 0.02 + sin_a * sin_a
    dynamic = 0.5 * area[...] * square
    around_axis = dynamic * (lift * sin_p - drag * cos_p)
    loads[0] = dynamic * (lift * cos_p + drag * sin_p)
    loads[1] = -around_axis * sin_t
    loads[2] = around_axis * cos_t

    for slot in range(sh.slots):
        rows = pl.ds(slot * tall, tall)

        def spread_out(window):
            tile, after, offset = window_of(slot, window)

            def chunk(i, total):
                at = pl.multiple_of(i * SPREAD_CHUNK, SPREAD_CHUNK)
                for group in range(SPREAD_CHUNK // LANES):
                    heights = upward[slot, :, pl.ds(at + group * LANES, LANES)]
                    row = (i * (SPREAD_CHUNK // LANES) + group) * sh.slots + slot
                    parts = [heights * loads[axis, pl.ds(row, 1), :] for axis in range(3)]
                    top, rest = split(jnp.concatenate(parts, axis=0))
                    weighted[:tall, group * LANES : (group + 1) * LANES] = top
                    weighted[tall:, group * LANES : (group + 1) * LANES] = rest
                return total + lax.dot_general(
                    across[slot, window, :, pl.ds(at, SPREAD_CHUNK)],
                    weighted[...],
                    (((1,), (1,)), ((), ())),
                    preferred_element_type=F32,
                )

            total = lax.fori_loop(
                0,
                sh.markers // SPREAD_CHUNK,
                chunk,
                jnp.zeros((2 * LANES, 2 * tall), F32),
            )
            total = jnp.transpose(total)
            total = total[:tall] + total[tall:]
            total = -SPREAD * (total[:, :LANES] + total[:, LANES:])
            pieces = []
            for _ in range(3):
                pieces.append(total.astype(BF16))
                total = total - pieces[-1].astype(F32)
            pieces = jnp.dot(
                jnp.concatenate(pieces, axis=0), from_class, preferred_element_type=F32
            )
            total = pieces[:tall] + pieces[tall : 2 * tall] + pieces[2 * tall :]
            both = jnp.concatenate([total, jnp.zeros((tall, LANES), F32)], axis=1)
            both = pltpu.roll(both, offset, 1)
            spread[tile, rows, :] = spread[tile, rows, :] + both[:, :LANES]
            spread[after, rows, :] = spread[after, rows, :] + both[:, LANES:]

        windows(slot, spread_out)

    lanes = iota((sh.levels, LANES), 1)
    for shift in range(sh.tiles):
        tile = lax.rem(me + shift, sh.tiles)
        forces[shift][: sh.section, :] = spread[tile]
        before = lax.rem(tile + sh.tiles - 1, sh.tiles)
        after = lax.rem(tile + 1, sh.tiles)
        beyond = [jnp.zeros((sh.levels, LANES), F32)] * 2
        for k in range(3 * sh.slots):
            at = pl.ds(k * sh.levels, sh.levels)
            left = jnp.broadcast_to(spread[before, at, :][:, LANES - 1 :], (sh.levels, LANES))
            right = jnp.broadcast_to(spread[after, at, :][:, :1], (sh.levels, LANES))
            beyond[0] = jnp.where(lanes == k, left, beyond[0])
            beyond[1] = jnp.where(lanes == k, right, beyond[1])
        for side in range(2):
            forces[shift][pl.ds(sh.section + side, sh.levels, stride=2), :] = beyond[side]
    for shift in {1, sh.tiles - 1}:
        forces[shift][sh.section + 2 * sh.levels :, :] = columns[...]


def do_markers(sh, step, plan, tables, fixed, blades, filt, columns, sections):
    across, upward, info = tables
    rows = sh.slots * sh.groups
    dense = pltpu.VMEM((3, rows, LANES), F32)
    plain = sh.section + 2 * sh.levels
    extra = columns.shape[0]
    forces = [
        pltpu.VMEM((plain + (extra if by in (1, sh.tiles - 1) else 0), LANES), F32)
        for by in range(sh.tiles)
    ]
    out = pl.pallas_call(
        lambda *refs: marker_kernel(sh, step, *refs),
        out_shape=[dense, dense] + forces,
        in_specs=[SM, SM] + [VM] * (7 + sh.tiles),
        out_specs=[VM] * (2 + sh.tiles),
        scratch_shapes=[
            pltpu.VMEM((sh.tiles, sh.section, LANES), F32),
            pltpu.VMEM((3, rows, LANES), F32),
            pltpu.VMEM((6 * sh.levels, SPREAD_CHUNK), BF16),
            pltpu.VMEM((sh.tiles, sh.section, LANES), F32),
        ],
        compiler_params=PARAMS,
        name="markers",
    )(plan, info, across, upward, *fixed, blades, filt, columns, *sections)
    return in_vmem(out[0]), in_vmem(out[1]), out[2:]


def edge_kernel(sh, has_edges, plan, f, *refs):
    low, high = refs[:2] if has_edges else (None, None)
    refs = refs[2 * has_edges :]
    forces = refs[: sh.tiles]
    outs = refs[sh.tiles + 1 :]
    me = lax.axis_index("gy")
    lanes = iota((sh.levels, LANES), 1)
    corner_rows = pl.ds(sh.section + 2 * sh.levels + column_rows(sh), sh.levels)
    blank = jnp.zeros((sh.levels, LANES), F32)
    planes_at = (0, sh.xs - 1)
    beyond = jnp.where(
        lanes % 2 == 0, forces[1][corner_rows, :], forces[sh.tiles - 1][corner_rows, :]
    )
    corner = [pltpu.roll(beyond, (LANES - 4 * q) % LANES, 1) for q in range(19)]
    corner_force = [blank, blank, blank]
    edge_force = [[blank, blank, blank], [blank, blank, blank]]
    for shift in range(sh.tiles):
        owner = lax.rem(me + sh.tiles - shift, sh.tiles)
        ghosts = [
            forces[shift][pl.ds(sh.section + side, sh.levels, stride=2), :] for side in range(2)
        ]
        for slot in range(sh.slots):
            x = plane_at(sh, plan, owner, slot)
            for axis in range(3):
                k = slot * 3 + axis
                piece = forces[shift][k * sh.levels : (k + 1) * sh.levels, :]
                for which in range(2):
                    here = jnp.asarray(x == planes_at[which])
                    edge_force[which][axis] = edge_force[which][axis] + jnp.where(here, piece, 0.0)
                    for side in range(2):
                        lane = 2 * which + side
                        moved = pltpu.roll(ghosts[side], (lane - k) % LANES, 1)
                        corner_force[axis] = corner_force[axis] + jnp.where(
                            jnp.logical_and(here, lanes == lane), moved, 0.0
                        )
    corner_post = collide(corner, corner_force, [q for q in PLUS + MINUS if DIRS[q][1]])
    for which, wanted in ((1, PLUS), (0, MINUS)):
        planes = plane_of(sh, f, planes_at[which], low, high)
        post = collide(planes, edge_force[which], wanted)
        out = outs[0] if which else outs[1]
        for k, q in enumerate(wanted):
            value = post[q]
            if DIRS[q][1] == 1:
                value = pltpu.roll(value, 1, 1)
                ghost = pltpu.roll(corner_post[q], (LANES - 2 * which) % LANES, 1)
                value = jnp.where(lanes == 0, ghost, value)
            elif DIRS[q][1] == -1:
                value = pltpu.roll(value, LANES - 1, 1)
                ghost = pltpu.roll(corner_post[q], LANES - 2 - 2 * which, 1)
                value = jnp.where(lanes == LANES - 1, ghost, value)
            if DIRS[q][2]:
                value = pltpu.roll(value, DIRS[q][2] % sh.levels, 0)
            out[k] = value


def make_edges(sh, plan, f, edges, forces, after):
    return pl.pallas_call(
        lambda *refs: edge_kernel(sh, bool(edges), *refs),
        out_shape=[pltpu.VMEM((len(PLUS), sh.levels, LANES), F32)] * 2,
        in_specs=[SM] + [VM] * (2 + len(edges) + sh.tiles),
        out_specs=[VM] * 2,
        compiler_params=PARAMS,
        name="edges",
    )(plan, f, *edges, *forces, after)


def bulk_kernel(sh, has_edges, last, plan, f, *refs):
    low, high = refs[:2] if has_edges else (None, None)
    refs = refs[2 * has_edges :]
    loads, filt, out = refs[:3]
    xs = sh.xs
    xrows = iota((xs, LANES), 0)
    if last:
        rows = iota((sh.slots * sh.groups, LANES), 0) % sh.slots
        used = jnp.zeros((sh.slots * sh.groups, LANES), jnp.int32)
        for slot in range(sh.slots):
            there = (rotor_at(sh, plan, slot) >= 0).astype(jnp.int32)
            used = jnp.where(rows == slot, there, used)
        for source, target in ((loads, refs[3]), (filt, refs[4])):
            for axis in range(3):
                target[axis] = jnp.where(used > 0, source[axis], 0.0)

    def level(z, bottom, top):
        at = aligned(z * xs, xs)
        here = []
        for q in range(19):
            tile = f[q, pl.ds(at, xs), :]
            if has_edges and DIRS[q][0] != 0:
                blocked = (DIRS[q][2] == 1 and bottom) or (DIRS[q][2] == -1 and top)
                if not blocked:
                    if DIRS[q][0] == 1:
                        tile = jnp.where(xrows == 0, low[PLUS.index(q), pl.ds(z, 1), :], tile)
                    else:
                        tile = jnp.where(
                            xrows == xs - 1, high[MINUS.index(q), pl.ds(z, 1), :], tile
                        )
            here.append(tile)
        post = collide(here, None, range(19))
        for q in range(19):
            dx, dy, dz = DIRS[q]
            value = post[q]
            if (dz == 1 and top) or (dz == -1 and bottom):
                to, target = OPPOSITE[q], z
            else:
                to, target = q, z + dz
                if dy:
                    value = pltpu.roll(value, dy % LANES, 1)
                if dx:
                    value = pltpu.roll(value, dx % xs, 0)
            out[to, pl.ds(aligned(target * xs, xs), xs), :] = value

    level(0, True, False)

    def middle(z, carry):
        level(z, False, False)
        return carry

    lax.fori_loop(1, sh.levels - 1, middle, 0)
    level(sh.levels - 1, False, True)


def do_bulk(sh, last, plan, f, edges, loads, filt):
    out_shape = [pltpu.VMEM((19, sh.levels * sh.xs, LANES), F32)]
    if last:
        out_shape += [jax.ShapeDtypeStruct(loads.shape, F32)] * 2
    return pl.pallas_call(
        lambda *refs: bulk_kernel(sh, bool(edges), last, *refs),
        out_shape=out_shape,
        in_specs=[SM] + [VM] * (3 + len(edges)),
        out_specs=[VM] * len(out_shape),
        compiler_params=PARAMS,
        name="bulk",
    )(plan, f, *edges, loads, filt)


def patch_kernel(sh, has_edges, last, plan, f, *refs):
    low, high = refs[:2] if has_edges else (None, None)
    refs = refs[2 * has_edges :]
    forces = refs[: sh.tiles]
    out = refs[sh.tiles + 1]
    sems = refs[-1]
    me = lax.axis_index("gy")
    xs = sh.xs
    lanes = iota((xs, LANES), 1)
    xrows = iota((xs, LANES), 0)
    per = LANES // (2 * sh.levels)
    copies = []

    def send(q):
        if last:
            copy = pltpu.make_async_copy(out.at[q], refs[sh.tiles + 2].at[q], sems.at[q])
            copy.start()
            copies.append(copy)

    rotors = []
    for shift in range(sh.tiles):
        owner = lax.rem(me + sh.tiles - shift, sh.tiles)
        for slot in range(sh.slots):
            rotors.append((plane_at(sh, plan, owner, slot), forces[shift], slot * 3))

    for x, _, _ in rotors:

        @pl.when(x >= 0)
        def _():
            here = plane_of(sh, f, x, low, high)
            force = [jnp.zeros((sh.levels, LANES), F32)] * 3
            for other, source, first in rotors:
                same = (other == x).astype(F32)
                for axis in range(3):
                    at = (first + axis) * sh.levels
                    force[axis] = force[axis] + same * source[at : at + sh.levels, :]
            post = collide(here, force, range(19))
            rows = sh.levels - 1
            for q in range(19):
                dx, dy, dz = DIRS[q]
                value = post[q]
                moved = pltpu.roll(value, dy % LANES, 1) if dy else value
                to = x + dx

                def put(dz=dz, q=q, moved=moved, to=to):
                    if dz == 0:
                        out[q, pl.ds(to, sh.levels, stride=xs), :] = moved
                    elif dz == 1:
                        out[q, pl.ds(to + xs, rows, stride=xs), :] = moved[:rows]
                    else:
                        out[q, pl.ds(to, rows, stride=xs), :] = moved[1:]

                if dx:
                    pl.when(x != (xs - 1 if dx == 1 else 0))(put)
                else:
                    put()
                if dz == 1:
                    out[OPPOSITE[q], pl.ds(x + rows * xs, 1), :] = value[rows:]
                elif dz == -1:
                    out[OPPOSITE[q], pl.ds(x, 1), :] = value[:1]

    for q in range(19):
        if q not in SIDEWAYS:
            send(q)

    ghost_force = [jnp.zeros((xs, LANES), F32) for axis in range(3)]
    tall = 2 * sh.levels
    for shift in range(sh.tiles):
        ghosts = jnp.transpose(
            jnp.concatenate(
                [
                    forces[shift][sh.section : sh.section + tall, :],
                    jnp.zeros((LANES - tall, LANES), F32),
                ],
                axis=0,
            )
        )
        for x, _, first in rotors[shift * sh.slots : (shift + 1) * sh.slots]:
            for axis in range(3):
                k = first + axis
                ghost_force[axis] = ghost_force[axis] + jnp.where(
                    xrows == x, ghosts[k : k + 1, :], 0.0
                )
    left, right = forces[1], forces[sh.tiles - 1]
    beyond = []
    for group in range(column_rows(sh) // xs):
        at = pl.ds(sh.section + tall + group * xs, xs)
        beyond.append(jnp.where(lanes % 2 == 0, left[at, :], right[at, :]))
    ghost = [
        pltpu.roll(beyond[q // per], (LANES - (q % per) * tall) % LANES, 1) for q in range(19)
    ]
    posted = collide(ghost, ghost_force, SIDEWAYS)
    for k, q in enumerate(SIDEWAYS):
        dx, dy, dz = DIRS[q]
        value = posted[q]
        if dx:
            value = pltpu.roll(value, dx % xs, 0)
        for z in range(sh.levels):
            if not 0 <= z - dz < sh.levels:
                continue
            at = pl.ds(z * xs, xs)
            here = out[q, at, :]
            if dy == 1:
                other = pltpu.roll(value, (LANES - 2 * (z - dz)) % LANES, 1)
                here = jnp.where(lanes == 0, other, here)
            else:
                other = pltpu.roll(value, LANES - 2 - 2 * (z - dz), 1)
                here = jnp.where(lanes == LANES - 1, other, here)
            out[q, at, :] = here
        send(q)
    for copy in copies:
        copy.wait()


def do_patch(sh, last, plan, f, edges, forces, bulk):
    out_shape = [pltpu.VMEM(bulk.shape, F32)]
    if last:
        out_shape.append(jax.ShapeDtypeStruct(bulk.shape, F32))
    return pl.pallas_call(
        lambda *refs: patch_kernel(sh, bool(edges), last, *refs),
        out_shape=out_shape,
        in_specs=[SM] + [VM] * (2 + len(edges) + sh.tiles),
        out_specs=[VM] + [HB] * last,
        scratch_shapes=[
            pltpu.SemaphoreType.DMA((19,)),
        ],
        input_output_aliases={2 + len(edges) + sh.tiles: 0},
        compiler_params=PARAMS,
        name="patch",
    )(plan, f, *edges, *forces, bulk)


def finish_kernel(sh, held, low, high, f_old, f, merged, sem):
    del f_old
    rows = iota((8, LANES), 0)
    copies = []
    for side, dirs, edge in ((0, PLUS, low), (1, MINUS, high)):
        at_row = 0 if side == 0 else 7
        first = 0 if side == 0 else sh.xs - 8
        for k, q in enumerate(dirs):
            index = side * len(PLUS) + k
            for z in range(sh.levels):
                value = held[q, z * sh.xs + first : z * sh.xs + first + 8, :]
                blocked = (DIRS[q][2] == 1 and z == 0) or (
                    DIRS[q][2] == -1 and z == sh.levels - 1
                )
                if not blocked:
                    value = jnp.where(rows == at_row, edge[k, z : z + 1, :], value)
                merged[index, z] = value
            copy = pltpu.make_async_copy(
                merged.at[index], f.at[q, :, first : first + 8, :], sem.at[index]
            )
            copy.start()
            copies.append(copy)
    for copy in copies:
        copy.wait()


def finish(sh, held, f, edges):
    f = f.reshape(19, sh.levels, sh.xs, LANES)
    return pl.pallas_call(
        lambda *refs: finish_kernel(sh, *refs),
        out_shape=jax.ShapeDtypeStruct(f.shape, F32),
        in_specs=[VM, VM, VM, HB],
        out_specs=HB,
        scratch_shapes=[
            pltpu.VMEM((2 * len(PLUS), sh.levels, 8, LANES), F32),
            pltpu.SemaphoreType.DMA((2 * len(PLUS),)),
        ],
        input_output_aliases={3: 0},
        compiler_params=PARAMS,
        name="finish",
    )(held, *edges, f)


def by_group(sh, x):
    head = x.shape[:-2]
    x = x.reshape(*head, sh.slots, sh.groups, LANES)
    return jnp.swapaxes(x, -3, -2).reshape(*head, sh.slots * sh.groups, LANES)


def by_slot(sh, x):
    head = x.shape[:-2]
    x = x.reshape(*head, sh.groups, sh.slots, LANES)
    return jnp.swapaxes(x, -3, -2).reshape(*head, sh.slots, sh.markers)


def shifted(x, axis, by):
    count = lax.axis_size(axis)
    return lax.ppermute(x, axis, [(i, (i + by) % count) for i in range(count)])


def local(
    f_in,
    rotor_place,
    marker_cell,
    pitch_phase,
    blade_area,
    blade_twist,
    blade_speed,
    blade_angle,
    filt_in,
):
    sh = Shape(f_in, rotor_place, marker_cell, pitch_phase, filt_in)
    area, twist, speed, angle = [
        by_group(sh, x[0, 0]) for x in (blade_area, blade_twist, blade_speed, blade_angle)
    ]
    filt = by_group(sh, jnp.swapaxes(filt_in[0, 0], 0, 1))
    f = in_vmem(f_in.reshape(19, sh.levels * sh.xs, LANES))
    plan, blades = start(sh, rotor_place, pitch_phase, twist, angle)
    edges = ()
    for step in range(sh.steps):
        last = step == sh.steps - 1
        if step == 0:
            columns = in_vmem(make_columns(sh, plan, f, edges))
            sections = make_sections(sh, plan, f, edges, (columns,))
            tables = make_tables(sh, plan, marker_cell, in_vmem(sections[0]))
        else:
            sections = make_sections(sh, plan, f, edges, ())
            columns = in_vmem(make_columns(sh, plan, f, edges))
        sections = [sections[0]] + [
            shifted(sections[by], "gy", by) for by in range(1, sh.tiles)
        ]
        filt, loads, forces = do_markers(
            sh,
            step,
            plan,
            tables,
            (area, speed),
            blades,
            filt,
            columns,
            [in_vmem(section) for section in sections],
        )
        forces = [forces[0]] + [shifted(forces[by], "gy", by) for by in range(1, sh.tiles)]
        forces = [in_vmem(force) for force in forces]
        bulk = do_bulk(sh, last, plan, f, edges, loads, filt)
        if last:
            loads_out, filt_out = bulk[1:]
        bulk = in_vmem(bulk[0])
        sent = make_edges(sh, plan, f, edges, forces, bulk)
        arrived = [shifted(sent[0], "gx", 1), shifted(sent[1], "gx", -1)]
        done = do_patch(sh, last, plan, f, edges, forces, bulk)
        edges = tuple(in_vmem(edge) for edge in arrived)
        f = in_vmem(done[0])
    f = finish(sh, f, done[1], edges)
    loads_out, filt_out = [
        jnp.swapaxes(by_slot(sh, x), 0, 1)[None, None] for x in (loads_out, filt_out)
    ]
    return f, loads_out, filt_out


def solution(mesh):
    in_specs = (
        P(None, None, "gx", "gy"),
        P(),
        P(),
        P(),
        P("gx", "gy", None, None),
        P("gx", "gy", None, None),
        P("gx", "gy", None, None),
        P("gx", "gy", None, None),
        P("gx", "gy", None, None, None),
    )
    out_specs = (
        P(None, None, "gx", "gy"),
        P("gx", "gy", None, None, None),
        P("gx", "gy", None, None, None),
    )
    return jax.shard_map(local, mesh=mesh, in_specs=in_specs, out_specs=out_specs, check_vma=False)
```

```python
import math

import jax
import jax.numpy as jnp
from jax import lax
from jax.experimental import pallas as pl
from jax.experimental.pallas import tpu as pltpu
from jax.sharding import PartitionSpec as P

PHASES = 64
PAIRS = [
    (1, 0, 0),
    (0, 1, 0),
    (0, 0, 1),
    (1, 1, 0),
    (1, -1, 0),
    (1, 0, 1),
    (1, 0, -1),
    (0, 1, 1),
    (0, 1, -1),
]
DIRS = [(0, 0, 0)]
for along in PAIRS:
    DIRS.append(along)
    DIRS.append(tuple(-part for part in along))
OPPOSITE = [0] + [q + 1 if q % 2 else q - 1 for q in range(1, 19)]
PLUS = [q for q in range(19) if DIRS[q][0] == 1]
MINUS = [q for q in range(19) if DIRS[q][0] == -1]
SIDEWAYS = [q for q in range(19) if DIRS[q][1] != 0]
OMEGA = 1.0 / 0.6
KEEP = 1.0 - OMEGA
GUO = 1.0 - 0.5 * OMEGA
SPREAD = 0.01
MIX = 0.5
PITCH_AMP = 0.2
LANES = 128
F32 = jnp.float32
BF16 = jnp.bfloat16
VMEM_LIMIT = 8 * 1024 * 1024


def iota(shape, axis):
    return lax.broadcasted_iota(jnp.int32, shape, axis)


def aligned(value, by):
    return value if isinstance(value, int) else pl.multiple_of(value, by)


def wrapped(value):
    return value % LANES if isinstance(value, int) else lax.rem(value, LANES)


def moments(f):
    sums = [f[2 * k + 1] + f[2 * k + 2] for k in range(9)]
    gaps = [f[2 * k + 1] - f[2 * k + 2] for k in range(9)]
    density = f[0]
    for part in sums:
        density = density + part
    momentum = []
    for axis in range(3):
        total = None
        for k in range(9):
            sign = PAIRS[k][axis]
            if sign == 0:
                continue
            if total is None:
                total = gaps[k]
            else:
                total = total + gaps[k] if sign > 0 else total - gaps[k]
        momentum.append(total)
    return density, momentum


def collide(f, force, wanted):
    density, momentum = moments(f)
    inverse = 1.0 / density
    relaxed = OMEGA * density
    if force is None:
        v = [momentum[a] * inverse for a in range(3)]
        square = v[0] * v[0] + v[1] * v[1] + v[2] * v[2]
        base = relaxed * (1.0 - 1.5 * square)
        drive = [OMEGA * momentum[a] for a in range(3)]
        bend = [4.5 * part for part in drive]
    else:
        v = [(momentum[a] + 0.5 * force[a]) * inverse for a in range(3)]
        square = v[0] * v[0] + v[1] * v[1] + v[2] * v[2]
        work = v[0] * force[0] + v[1] * force[1] + v[2] * force[2]
        base = relaxed * (1.0 - 1.5 * square) - (3.0 * GUO) * work
        drive = [relaxed * v[a] + GUO * force[a] for a in range(3)]
        bend = [(4.5 * relaxed) * v[a] + (9.0 * GUO) * force[a] for a in range(3)]
    post = {}
    if 0 in wanted:
        post[0] = KEEP * f[0] + base * (1.0 / 3.0)
    scaled = {}
    for weight in (18.0, 36.0):
        scaled[weight] = (
            base * (1.0 / weight),
            [part * (3.0 / weight) for part in drive],
            [part * (1.0 / weight) for part in bend],
        )

    def along(k, parts):
        total = None
        for axis in range(3):
            sign = PAIRS[k][axis]
            if sign == 0:
                continue
            if total is None:
                total = parts[axis]
            else:
                total = total + parts[axis] if sign > 0 else total - parts[axis]
        return total

    for k in range(9):
        if 2 * k + 1 not in wanted and 2 * k + 2 not in wanted:
            continue
        level, drives, bends = scaled[18.0 if k < 3 else 36.0]
        even = level + along(k, v) * along(k, bends)
        odd = along(k, drives)
        if 2 * k + 1 in wanted:
            post[2 * k + 1] = KEEP * f[2 * k + 1] + (even + odd)
        if 2 * k + 2 in wanted:
            post[2 * k + 2] = KEEP * f[2 * k + 2] + (even - odd)
    return post


def outside(q, levels, rows):
    if DIRS[q][2] == 1:
        return rows == 0
    if DIRS[q][2] == -1:
        return rows == levels - 1
    return None


class Shape:
    def __init__(self, f_in, rotor_place, marker_cell, pitch_phase, filt_in):
        self.levels = f_in.shape[1]
        self.xs = f_in.shape[2]
        self.rotors = rotor_place.shape[0]
        self.steps = pitch_phase.shape[1]
        self.markers = marker_cell.shape[1]
        self.slots = filt_in.shape[2]
        self.tiles = lax.axis_size("gy")
        self.groups = self.markers // LANES
        self.section = self.slots * 3 * self.levels


def in_vmem(x):
    return pltpu.with_memory_space_constraint(x, pltpu.VMEM)


def in_hbm(x):
    return pltpu.with_memory_space_constraint(x, pltpu.HBM)


def in_smem(x):
    return pltpu.with_memory_space_constraint(x, pltpu.SMEM)


VM = pl.BlockSpec(memory_space=pltpu.VMEM)
SM = pl.BlockSpec(memory_space=pltpu.SMEM)
HB = pl.BlockSpec(memory_space=pl.ANY)
PARAMS = pltpu.CompilerParams(vmem_limit_bytes=VMEM_LIMIT)


def write_plan(sh, place, plan):
    row = lax.axis_index("gx")
    shape = (sh.tiles, sh.rotors)
    mine = jnp.logical_and(place[2:3, :] == iota(shape, 0), place[0:1, :] == row)
    keys = iota(shape, 1) * sh.xs + place[1:2, :]
    none = sh.rotors * sh.xs
    last = jnp.full((sh.tiles, 1), -1, jnp.int32)
    for slot in range(sh.slots):
        left = jnp.logical_and(mine, keys > last)
        last = jnp.min(jnp.where(left, keys, none), axis=1, keepdims=True)
        for owner in range(sh.tiles):
            key = last[owner, 0]
            plan[owner * sh.slots + slot] = jnp.where(key < none, key, -1)


def plane_at(sh, plan, owner, slot):
    key = plan[owner * sh.slots + slot]
    return jnp.where(key < 0, -1, lax.rem(key, sh.xs))


def rotor_at(sh, plan, slot):
    key = plan[lax.axis_index("gy") * sh.slots + slot]
    return jnp.where(key < 0, -1, lax.div(key, sh.xs))


def plane_of(sh, f, x, low, high):
    rows = iota((sh.levels, LANES), 0)
    planes = []
    for q in range(19):
        value = f[q, pl.ds(x, sh.levels, stride=sh.xs), :]
        if low is not None and DIRS[q][0] != 0:
            if DIRS[q][0] == 1:
                other, at = low[PLUS.index(q)], 0
            else:
                other, at = high[MINUS.index(q)], sh.xs - 1
            here = jnp.asarray(x == at)
            skip = outside(q, sh.levels, rows)
            use = here if skip is None else jnp.logical_and(here, jnp.logical_not(skip))
            value = jnp.where(use, other, value)
        planes.append(value)
    return planes


def write_sections(sh, plan, f, low, high, outs):
    me = lax.axis_index("gy")
    for shift in range(sh.tiles):
        owner = lax.rem(me + shift, sh.tiles)
        for slot in range(sh.slots):
            x = plane_at(sh, plan, owner, slot)

            @pl.when(x >= 0)
            def _():
                planes = plane_of(sh, f, x, low, high)
                density, momentum = moments(planes)
                inverse = 1.0 / density
                for axis in range(3):
                    at = (slot * 3 + axis) * sh.levels
                    outs[shift][at : at + sh.levels, :] = momentum[axis] * inverse

            @pl.when(x < 0)
            def _():
                at = slot * 3 * sh.levels
                outs[shift][at : at + 3 * sh.levels, :] = jnp.zeros((3 * sh.levels, LANES), F32)


def sincos(x):
    turns = jnp.floor(x * (2.0 / math.pi) + 0.5)
    r = x - turns * 1.5703125
    r = r - turns * 4.837512969970703125e-4
    r = r - turns * 7.549789954891882e-8
    r2 = r * r
    sin_r = r + r * r2 * (
        -1.0 / 6 + r2 * (1.0 / 120 + r2 * (-1.0 / 5040 + r2 * (1.0 / 362880)))
    )
    cos_r = (
        1.0
        - 0.5 * r2
        + r2
        * r2
        * (1.0 / 24 + r2 * (-1.0 / 720 + r2 * (1.0 / 40320 - r2 * (1.0 / 3628800))))
    )
    quarter = turns.astype(jnp.int32)
    swap = (quarter & 1) == 1
    sin_x = jnp.where(swap, cos_r, sin_r)
    cos_x = jnp.where(swap, sin_r, cos_r)
    sin_x = jnp.where((quarter & 2) == 2, -sin_x, sin_x)
    cos_x = jnp.where(((quarter + 1) & 2) == 2, -cos_x, cos_x)
    return sin_x, cos_x


def write_blades(sh, plan, phases, twist, angle, blades):
    blades[0], blades[1] = sincos(angle[...])
    sin_twist, cos_twist = sincos(twist[...])
    owner = iota((1, LANES), 1)
    rows = iota((sh.slots * sh.groups, LANES), 0) % sh.slots
    phase = jnp.zeros((1, LANES), F32)
    for step in range(sh.steps):
        for slot in range(sh.slots):
            rotor = jnp.maximum(rotor_at(sh, plan, slot), 0)
            here = owner == step * sh.slots + slot
            phase = jnp.where(here, phases[step, rotor].astype(F32), phase)
    pitch = PITCH_AMP * sincos((2.0 * math.pi / PHASES) * phase)[0]
    pitched = sincos(pitch)
    for step in range(sh.steps):
        parts = []
        for part in pitched:
            total = jnp.zeros((sh.slots * sh.groups, LANES), F32)
            for slot in range(sh.slots):
                lane = step * sh.slots + slot
                total = jnp.where(rows == slot, part[:, lane : lane + 1], total)
            parts.append(total)
        blades[2 + 2 * step] = sin_twist * parts[1] + cos_twist * parts[0]
        blades[3 + 2 * step] = cos_twist * parts[1] - sin_twist * parts[0]


def start_kernel(
    sh, place_in, phases_in, twist_in, angle_in, f_in, plan, blades, f, place, phases, twist, angle, sems
):
    pairs = ((place_in, place), (phases_in, phases), (angle_in, angle), (twist_in, twist))
    copies = [pltpu.make_async_copy(*pair, sems.at[k]) for k, pair in enumerate(pairs)]
    whole = pltpu.make_async_copy(f_in, f, sems.at[4])
    for copy in copies:
        copy.start()
    whole.start()
    for copy in copies:
        copy.wait()
    write_plan(sh, place, plan)
    write_blades(sh, plan, phases, twist, angle, blades)
    whole.wait()


def start(sh, rotor_place, phases, twist, angle, f_in):
    rows = sh.slots * sh.groups
    plan, blades, f = pl.pallas_call(
        lambda *refs: start_kernel(sh, *refs),
        out_shape=[
            pltpu.SMEM((sh.tiles * sh.slots,), jnp.int32),
            pltpu.VMEM((2 + 2 * sh.steps, rows, LANES), F32),
            pltpu.VMEM((19, sh.levels * sh.xs, LANES), F32),
        ],
        in_specs=[HB] * 5,
        out_specs=[SM, VM, VM],
        scratch_shapes=[
            pltpu.VMEM((3, sh.rotors), jnp.int32),
            pltpu.SMEM((sh.steps, sh.rotors), jnp.int32),
            pltpu.VMEM((rows, LANES), F32),
            pltpu.VMEM((rows, LANES), F32),
            pltpu.SemaphoreType.DMA((5,)),
        ],
        compiler_params=PARAMS,
        name="start",
    )(
        in_hbm(jnp.transpose(rotor_place)),
        in_hbm(jnp.transpose(phases)),
        in_hbm(twist),
        in_hbm(angle),
        in_hbm(f_in.reshape(19, sh.levels * sh.xs, LANES)),
    )
    return in_smem(plan), in_vmem(blades), in_vmem(f)


def section_kernel(sh, has_edges, plan, f, *refs):
    low, high = refs[:2] if has_edges else (None, None)
    write_sections(sh, plan, f, low, high, refs[-sh.tiles :])


def make_sections(sh, plan, f, edges, after):
    return pl.pallas_call(
        lambda *refs: section_kernel(sh, bool(edges), *refs),
        out_shape=[pltpu.VMEM((sh.section, LANES), F32)] * sh.tiles,
        in_specs=[SM] + [VM] * (1 + len(edges) + len(after)),
        out_specs=[VM] * sh.tiles,
        compiler_params=PARAMS,
        name="sections",
    )(plan, f, *edges, *after)


def column_kernel(sh, has_edges, *refs):
    f = refs[1]
    low, high = refs[2:4] if has_edges else (None, None)
    east, west = refs[-2:]
    packed = []
    pairs = iota((sh.xs, LANES), 1) // 2
    xrows = iota((sh.xs, LANES), 0)
    per = LANES // (2 * sh.levels)
    groups = (19 + per - 1) // per
    for group in range(groups):
        total = jnp.ones((sh.xs, LANES), F32)
        for q in range(group * per, min(19, (group + 1) * per)):
            for z in range(sh.levels):
                tile = f[q, z * sh.xs : (z + 1) * sh.xs, :]
                if has_edges and DIRS[q][0] != 0:
                    blocked = (DIRS[q][2] == 1 and z == 0) or (
                        DIRS[q][2] == -1 and z == sh.levels - 1
                    )
                    if not blocked:
                        if DIRS[q][0] == 1:
                            tile = jnp.where(xrows == 0, low[PLUS.index(q), z : z + 1, :], tile)
                        else:
                            tile = jnp.where(
                                xrows == sh.xs - 1, high[MINUS.index(q), z : z + 1, :], tile
                            )
                pair = (q % per) * sh.levels + z
                total = jnp.where(
                    pairs == pair, pltpu.roll(tile, (2 * pair + 1) % LANES, 1), total
                )
        packed.append(total)
    zpairs = iota((sh.levels, LANES), 1) // 2
    corners = jnp.ones((sh.levels, LANES), F32)
    for which, x in ((0, 0), (1, sh.xs - 1)):
        planes = plane_of(sh, f, x, low, high)
        for q in range(19):
            pair = 2 * q + which
            corners = jnp.where(zpairs == pair, pltpu.roll(planes[q], 2 * pair + 1, 1), corners)
    packed.append(corners)
    even = iota((sh.xs, LANES), 1) % 2 == 0
    for k in range(len(packed) // 2):
        first, second = packed[2 * k], packed[2 * k + 1]
        rows = slice(k * sh.xs, (k + 1) * sh.xs)
        east[rows, :] = jnp.where(even, first, pltpu.roll(second, 1, 1))
        west[rows, :] = jnp.where(even, pltpu.roll(first, LANES - 1, 1), second)


def packed_columns(sh):
    per = LANES // (2 * sh.levels)
    return (19 + per - 1) // per + 1


def unpack_columns(sh, left, right, first):
    even = iota((sh.xs, LANES), 1) % 2 == 0
    groups = []
    for k in range(packed_columns(sh) // 2):
        rows = pl.ds(first + k * sh.xs, sh.xs)
        a, b = left[rows, :], right[rows, :]
        groups.append(jnp.where(even, a, pltpu.roll(b, 1, 1)))
        groups.append(jnp.where(even, pltpu.roll(a, LANES - 1, 1), b))
    return groups


def make_columns(sh, plan, f, edges):
    shape = (packed_columns(sh) // 2 * sh.xs, LANES)
    out = pl.pallas_call(
        lambda *refs: column_kernel(sh, bool(edges), *refs),
        out_shape=[pltpu.VMEM(shape, F32)] * 2,
        in_specs=[SM] + [VM] * (1 + len(edges)),
        out_specs=[VM] * 2,
        compiler_params=PARAMS,
        name="columns",
    )(plan, f, *edges)
    return [in_vmem(x) for x in out]


def peskin(offsets):
    distance = jnp.abs(offsets)
    near_arg = jnp.maximum(1.0 + 4.0 * distance - 4.0 * distance * distance, 1.0)
    far_arg = jnp.maximum(-7.0 + 12.0 * distance - 4.0 * distance * distance, 1.0)
    near = distance <= 1.0
    root = jnp.sqrt(jnp.where(near, near_arg, far_arg))
    return (jnp.where(near, 3.0, 5.0) - 2.0 * distance + jnp.where(near, root, -root)) * 0.125


TABLE_CHUNK = 1024


def table_kernel(sh, plan, cells, after, across, upward, info, codes, lines, sem):
    del after
    ids = [rotor_at(sh, plan, slot) for slot in range(sh.slots)]
    copies = []
    for slot in range(sh.slots):
        first = pl.multiple_of(jnp.maximum(ids[slot], 0) // 8 * 8, 8)
        copy = pltpu.make_async_copy(cells.at[pl.ds(first, 8), :], codes.at[slot], sem.at[slot])
        copy.start()
        copies.append(copy)
    width = min(TABLE_CHUNK, sh.markers)
    part = iota((8, width), 0)
    spanwise = part < 4
    cell_bits = 6 + sh.levels.bit_length() - 1
    quarter = LANES // 4
    packed = 16
    ycells = [
        (iota((packed, LANES), 0) + first).astype(F32).astype(BF16)
        for first in range(0, quarter, packed)
    ]
    zcells = iota((sh.levels, LANES), 0)
    for slot in range(sh.slots):
        copies[slot].wait()

        @pl.when(ids[slot] >= 0)
        def _():
            line = ids[slot] % 8
            every = codes[slot, pl.ds(line, 1), :] >> cell_bits
            lowest = jnp.min(every)
            highest = jnp.max(every)
            narrow = highest - lowest + 4 <= LANES
            start = jnp.where(narrow, lowest, lowest // LANES * LANES)
            info[2 * slot] = start
            info[2 * slot + 1] = jnp.where(narrow, 1, 2)

            def chunk(window, at):
                code = codes[slot, pl.ds(line, 1), pl.ds(at, width)]
                cells = (code >> cell_bits) - (start + window * LANES)
                levels = (code >> 6) & (sh.levels - 1)
                eighths = jnp.where(spanwise, code >> 3, code) & 7
                corner = jnp.where(spanwise, (part - cells) & 3, part - 4)
                weights = peskin(corner.astype(F32) - 1.0 - eighths.astype(F32) * 0.125)
                places = ((cells + corner - part) >> 2).astype(F32)
                top = weights.astype(BF16).astype(F32)
                rest = weights - top
                lines[0] = places
                lines[1] = top
                lines[2] = rest
                lines[3] = weights
                for group in range(width // LANES):
                    lanes = slice(group * LANES, (group + 1) * LANES)
                    to = pl.ds(at + group * LANES, LANES)
                    tall = jnp.zeros((sh.levels, LANES), F32)
                    for j in range(4):
                        tall = jnp.where(
                            zcells == levels[:, lanes] + j, lines[3, 4 + j : 5 + j, lanes], tall
                        )
                    upward[slot, :, to] = tall

                    def spread_line(k, kind):
                        line = lines[k, kind : kind + 1, lanes]
                        return jnp.broadcast_to(line, (packed, LANES)).astype(BF16)

                    for kind in range(4):
                        spot, high, low = [spread_line(k, kind) for k in range(3)]
                        for k, cell in enumerate(ycells):
                            here = cell == spot
                            for half, source in ((0, high), (1, low)):
                                row = half * LANES + kind * quarter + k * packed
                                across[slot, window, row : row + packed, to] = jnp.where(
                                    here, source, jnp.zeros((), BF16)
                                )

            def sweep(window):
                def body(i, carry):
                    chunk(window, pl.multiple_of(i * width, width))
                    return carry

                lax.fori_loop(0, sh.markers // width, body, 0)

            sweep(0)

            @pl.when(jnp.logical_not(narrow))
            def _():
                sweep(1)


def make_tables(sh, plan, marker_cell, after):
    across, upward, info = pl.pallas_call(
        lambda *refs: table_kernel(sh, *refs),
        out_shape=[
            pltpu.VMEM((sh.slots, 2, 2 * LANES, sh.markers), BF16),
            pltpu.VMEM((sh.slots, sh.levels, sh.markers), F32),
            pltpu.SMEM((2 * sh.slots,), jnp.int32),
        ],
        in_specs=[SM, HB, VM],
        out_specs=[VM, VM, SM],
        scratch_shapes=[
            pltpu.VMEM((sh.slots, 8, sh.markers), jnp.int32),
            pltpu.VMEM((4, 8, min(TABLE_CHUNK, sh.markers)), F32),
            pltpu.SemaphoreType.DMA((sh.slots,)),
        ],
        compiler_params=PARAMS,
        name="tables",
    )(plan, marker_cell, after)
    return in_vmem(across), in_vmem(upward), in_smem(info)


GHOST_LANES = 32
SAMPLE_CHUNK = 8192
SPREAD_CHUNK = 8192


def split(value):
    top = value.astype(BF16)
    return top, (value - top.astype(F32)).astype(BF16)


def marker_kernel(
    sh, step, plan, info, across, upward, area, speed, blades, filt_old, east, west, *refs
):
    sections = refs[: sh.tiles]
    filt_new, loads = refs[sh.tiles : sh.tiles + 2]
    forces = refs[sh.tiles + 2 : 2 * sh.tiles + 2]
    around, sampled, weighted, spread, turning = refs[2 * sh.tiles + 2 :]
    me = lax.axis_index("gy")
    tall = 3 * sh.levels
    quarter = LANES // 4
    rows = iota((LANES, LANES), 0)
    kinds = iota((LANES, LANES), 1)
    by_class = (rows == kinds % quarter * 4 + kinds // quarter).astype(F32).astype(BF16)
    from_class = (kinds == rows % quarter * 4 + rows // quarter).astype(F32).astype(BF16)
    for shift in range(sh.tiles):
        around[lax.rem(me + sh.tiles - shift, sh.tiles)] = sections[shift][...]
    spread[...] = jnp.zeros(spread.shape, F32)

    def window_of(slot, window):
        start = info[2 * slot] + window * LANES
        tile = start // LANES
        return tile, jnp.minimum(tile + 1, sh.tiles - 1), start - tile * LANES

    def windows(slot, body):
        @pl.when(rotor_at(sh, plan, slot) >= 0)
        def _():
            body(0)

            @pl.when(info[2 * slot + 1] > 1)
            def _():
                body(1)

    for slot in range(sh.slots):
        rows = pl.ds(slot * tall, tall)

        def sample(window):
            tile, after, offset = window_of(slot, window)
            both = jnp.concatenate([around[tile, rows, :], around[after, rows, :]], axis=1)
            seen = pltpu.roll(both, lax.rem(2 * LANES - offset, 2 * LANES), 1)[:, :LANES]
            top, rest = split(seen)
            left = jnp.concatenate([top, rest], axis=0)
            left = jnp.dot(left, by_class, preferred_element_type=F32).astype(BF16)
            left = jnp.concatenate([left, left], axis=1)

            def chunk(i, carry):
                at = pl.multiple_of(i * SAMPLE_CHUNK, SAMPLE_CHUNK)
                value = jnp.dot(
                    left,
                    across[slot, window, :, pl.ds(at, SAMPLE_CHUNK)],
                    preferred_element_type=F32,
                )
                value = value[:tall] + value[tall:]
                heights = upward[slot, :, pl.ds(at, SAMPLE_CHUNK)]
                for axis in range(3):
                    part = jnp.sum(
                        value[axis * sh.levels : (axis + 1) * sh.levels] * heights,
                        axis=0,
                        keepdims=True,
                    )
                    for group in range(SAMPLE_CHUNK // LANES):
                        row = (i * (SAMPLE_CHUNK // LANES) + group) * sh.slots + slot
                        piece = part[:, group * LANES : (group + 1) * LANES]
                        if window:
                            piece = piece + sampled[axis, pl.ds(row, 1), :]
                        sampled[axis, pl.ds(row, 1), :] = piece
                return carry

            lax.fori_loop(0, sh.markers // SAMPLE_CHUNK, chunk, 0)

        windows(slot, sample)

    felt = []
    for axis in range(3):
        old = filt_old[axis]
        value = old + MIX * (sampled[axis] - old)
        filt_new[axis] = value
        felt.append(value)
    sin_t = blades[0]
    cos_t = blades[1]
    tangent = speed[...] + sin_t * felt[1] - cos_t * felt[2]
    square = felt[0] * felt[0] + tangent * tangent
    inverse = 1.0 / jnp.sqrt(square)
    sin_p = felt[0] * inverse
    cos_p = tangent * inverse
    sin_b = blades[2 + 2 * step]
    cos_b = blades[3 + 2 * step]
    sin_a = sin_p * cos_b - cos_p * sin_b
    cos_a = cos_p * cos_b + sin_p * sin_b
    lift = (2.0 * math.pi) * sin_a * cos_a
    drag = 0.02 + sin_a * sin_a
    dynamic = 0.5 * area[...] * square
    around_axis = dynamic * (lift * sin_p - drag * cos_p)
    loads[0] = dynamic * (lift * cos_p + drag * sin_p)
    loads[1] = -around_axis * sin_t
    loads[2] = around_axis * cos_t

    for slot in range(sh.slots):
        rows = pl.ds(slot * tall, tall)

        def spread_out(window):
            tile, after, offset = window_of(slot, window)

            def chunk(i, total):
                at = pl.multiple_of(i * SPREAD_CHUNK, SPREAD_CHUNK)
                for group in range(SPREAD_CHUNK // LANES):
                    heights = upward[slot, :, pl.ds(at + group * LANES, LANES)]
                    row = (i * (SPREAD_CHUNK // LANES) + group) * sh.slots + slot
                    parts = [heights * loads[axis, pl.ds(row, 1), :] for axis in range(3)]
                    top, rest = split(jnp.concatenate(parts, axis=0))
                    weighted[:tall, group * LANES : (group + 1) * LANES] = top
                    weighted[tall:, group * LANES : (group + 1) * LANES] = rest
                return total + lax.dot_general(
                    across[slot, window, :, pl.ds(at, SPREAD_CHUNK)],
                    weighted[...],
                    (((1,), (1,)), ((), ())),
                    preferred_element_type=F32,
                )

            total = lax.fori_loop(
                0,
                sh.markers // SPREAD_CHUNK,
                chunk,
                jnp.zeros((2 * LANES, 2 * tall), F32),
            )
            total = jnp.transpose(total)
            total = total[:tall] + total[tall:]
            total = -SPREAD * (total[:, :LANES] + total[:, LANES:])
            pieces = []
            for _ in range(3):
                pieces.append(total.astype(BF16))
                total = total - pieces[-1].astype(F32)
            pieces = jnp.dot(
                jnp.concatenate(pieces, axis=0), from_class, preferred_element_type=F32
            )
            total = pieces[:tall] + pieces[tall : 2 * tall] + pieces[2 * tall :]
            both = jnp.concatenate([total, jnp.zeros((tall, LANES), F32)], axis=1)
            both = pltpu.roll(both, offset, 1)
            spread[tile, rows, :] = spread[tile, rows, :] + both[:, :LANES]
            spread[after, rows, :] = spread[after, rows, :] + both[:, LANES:]

        windows(slot, spread_out)

    lanes = iota((sh.levels, LANES), 1)
    for shift in range(sh.tiles):
        tile = lax.rem(me + shift, sh.tiles)
        forces[shift][: sh.section, :] = spread[tile]
        before = lax.rem(tile + sh.tiles - 1, sh.tiles)
        after = lax.rem(tile + 1, sh.tiles)
        beyond = [jnp.zeros((sh.levels, LANES), F32)] * 2
        for k in range(3 * sh.slots):
            at = pl.ds(k * sh.levels, sh.levels)
            left = jnp.broadcast_to(spread[before, at, :][:, LANES - 1 :], (sh.levels, LANES))
            right = jnp.broadcast_to(spread[after, at, :][:, :1], (sh.levels, LANES))
            beyond[0] = jnp.where(lanes == k, left, beyond[0])
            beyond[1] = jnp.where(lanes == k, right, beyond[1])
        at = shift * GHOST_LANES
        for side in range(2):
            turning[pl.ds(at + side, sh.levels, stride=2), :] = beyond[side]
        forces[shift][sh.section + 8 : sh.section + 8 + sh.levels, :] = jnp.where(
            lanes < 8, beyond[0], pltpu.roll(beyond[1], 8, 1)
        )
    each = LANES // GHOST_LANES
    for first in range(0, sh.tiles, each):
        rows = jnp.transpose(turning[first * GHOST_LANES : (first + each) * GHOST_LANES, :])[:8]
        for k in range(each):
            forces[first + k][sh.section : sh.section + 8, :] = pltpu.roll(
                rows, (LANES - k * GHOST_LANES) % LANES, 1
            )
    forces[1][sh.section + 8 + sh.levels :, :] = east[...]
    forces[sh.tiles - 1][sh.section + 8 + sh.levels :, :] = west[...]


def do_markers(sh, step, plan, tables, fixed, blades, filt, columns, sections):
    across, upward, info = tables
    rows = sh.slots * sh.groups
    dense = pltpu.VMEM((3, rows, LANES), F32)
    plain = sh.section + 8 + sh.levels
    extra = columns[0].shape[0]
    forces = [
        pltpu.VMEM((plain + (extra if by in (1, sh.tiles - 1) else 0), LANES), F32)
        for by in range(sh.tiles)
    ]
    out = pl.pallas_call(
        lambda *refs: marker_kernel(sh, step, *refs),
        out_shape=[dense, dense] + forces,
        in_specs=[SM, SM] + [VM] * (8 + sh.tiles),
        out_specs=[VM] * (2 + sh.tiles),
        scratch_shapes=[
            pltpu.VMEM((sh.tiles, sh.section, LANES), F32),
            pltpu.VMEM((3, rows, LANES), F32),
            pltpu.VMEM((6 * sh.levels, SPREAD_CHUNK), BF16),
            pltpu.VMEM((sh.tiles, sh.section, LANES), F32),
            pltpu.VMEM((sh.tiles * GHOST_LANES, LANES), F32),
        ],
        compiler_params=PARAMS,
        name="markers",
    )(plan, info, across, upward, *fixed, blades, filt, *columns, *sections)
    return in_vmem(out[0]), in_vmem(out[1]), out[2:]


def edge_kernel(sh, has_edges, plan, f, *refs):
    low, high = refs[:2] if has_edges else (None, None)
    refs = refs[2 * has_edges :]
    forces = refs[: sh.tiles]
    outs = refs[sh.tiles + 1 :]
    me = lax.axis_index("gy")
    lanes = iota((sh.levels, LANES), 1)
    blank = jnp.zeros((sh.levels, LANES), F32)
    planes_at = (0, sh.xs - 1)
    even = lax.rem(lax.axis_index("gx"), 2) == 0
    beyond = unpack_columns(sh, forces[1], forces[sh.tiles - 1], sh.section + 8 + sh.levels)[-1]
    corner = [pltpu.roll(beyond, (LANES - 4 * q) % LANES, 1) for q in range(19)]
    corner_force = [blank, blank, blank]
    edge_force = [[blank, blank, blank], [blank, blank, blank]]
    for shift in range(sh.tiles):
        owner = lax.rem(me + sh.tiles - shift, sh.tiles)
        ghosts = forces[shift][sh.section + 8 : sh.section + 8 + sh.levels, :]
        for slot in range(sh.slots):
            x = plane_at(sh, plan, owner, slot)
            for axis in range(3):
                k = slot * 3 + axis
                piece = forces[shift][k * sh.levels : (k + 1) * sh.levels, :]
                for which in range(2):
                    here = jnp.asarray(x == planes_at[which])
                    edge_force[which][axis] = edge_force[which][axis] + jnp.where(here, piece, 0.0)
                    for side in range(2):
                        lane = 2 * which + side
                        moved = pltpu.roll(ghosts, (lane - side * 8 - k) % LANES, 1)
                        corner_force[axis] = corner_force[axis] + jnp.where(
                            jnp.logical_and(here, lanes == lane), moved, 0.0
                        )
    corner_post = collide(corner, corner_force, [q for q in PLUS + MINUS if DIRS[q][1]])
    leaving = ([], [])
    for which, wanted in ((1, PLUS), (0, MINUS)):
        planes = plane_of(sh, f, planes_at[which], low, high)
        post = collide(planes, edge_force[which], wanted)
        for k, q in enumerate(wanted):
            value = post[q]
            if DIRS[q][1] == 1:
                value = pltpu.roll(value, 1, 1)
                ghost = pltpu.roll(corner_post[q], (LANES - 2 * which) % LANES, 1)
                value = jnp.where(lanes == 0, ghost, value)
            elif DIRS[q][1] == -1:
                value = pltpu.roll(value, LANES - 1, 1)
                ghost = pltpu.roll(corner_post[q], LANES - 2 - 2 * which, 1)
                value = jnp.where(lanes == LANES - 1, ghost, value)
            if DIRS[q][2]:
                value = pltpu.roll(value, DIRS[q][2] % sh.levels, 0)
            leaving[which].append(value)
    for k, (down, up) in enumerate(zip(*leaving)):
        outs[0][k] = jnp.where(even, up, down)
        outs[1][k] = jnp.where(even, down, up)


def make_edges(sh, plan, f, edges, forces, after):
    return pl.pallas_call(
        lambda *refs: edge_kernel(sh, bool(edges), *refs),
        out_shape=[pltpu.VMEM((len(PLUS), sh.levels, LANES), F32)] * 2,
        in_specs=[SM] + [VM] * (2 + len(edges) + sh.tiles),
        out_specs=[VM] * 2,
        compiler_params=PARAMS,
        name="edges",
    )(plan, f, *edges, *forces, after)


def bulk_kernel(sh, has_edges, last, plan, f, *refs):
    low, high = refs[:2] if has_edges else (None, None)
    refs = refs[2 * has_edges :]
    loads, filt, out, planes = refs[:4]
    xs = sh.xs
    for k in range(sh.tiles * sh.slots):

        @pl.when(plan[k] >= 0)
        def _():
            for q, value in enumerate(plane_of(sh, f, lax.rem(plan[k], xs), low, high)):
                planes[k, q] = value

    xrows = iota((xs, LANES), 0)
    if last:
        rows = iota((sh.slots * sh.groups, LANES), 0) % sh.slots
        used = jnp.zeros((sh.slots * sh.groups, LANES), jnp.int32)
        for slot in range(sh.slots):
            there = (rotor_at(sh, plan, slot) >= 0).astype(jnp.int32)
            used = jnp.where(rows == slot, there, used)
        for source, target in ((loads, refs[4]), (filt, refs[5])):
            for axis in range(3):
                target[axis] = jnp.where(used > 0, source[axis], 0.0)

    def level(z, bottom, top):
        at = aligned(z * xs, xs)
        here = []
        for q in range(19):
            tile = f[q, pl.ds(at, xs), :]
            if has_edges and DIRS[q][0] != 0:
                blocked = (DIRS[q][2] == 1 and bottom) or (DIRS[q][2] == -1 and top)
                if not blocked:
                    if DIRS[q][0] == 1:
                        tile = jnp.where(xrows == 0, low[PLUS.index(q), pl.ds(z, 1), :], tile)
                    else:
                        tile = jnp.where(
                            xrows == xs - 1, high[MINUS.index(q), pl.ds(z, 1), :], tile
                        )
            here.append(tile)
        post = collide(here, None, range(19))
        for q in range(19):
            dx, dy, dz = DIRS[q]
            value = post[q]
            if (dz == 1 and top) or (dz == -1 and bottom):
                to, target = OPPOSITE[q], z
            else:
                to, target = q, z + dz
                if dy:
                    value = pltpu.roll(value, dy % LANES, 1)
                if dx:
                    value = pltpu.roll(value, dx % xs, 0)
            out[to, pl.ds(aligned(target * xs, xs), xs), :] = value

    level(0, True, False)

    def middle(z, carry):
        level(z, False, False)
        return carry

    lax.fori_loop(1, sh.levels - 1, middle, 0)
    level(sh.levels - 1, False, True)


def do_bulk(sh, last, plan, f, edges, loads, filt):
    out_shape = [
        pltpu.VMEM((19, sh.levels * sh.xs, LANES), F32),
        pltpu.VMEM((sh.tiles * sh.slots, 19, sh.levels, LANES), F32),
    ]
    if last:
        out_shape += [jax.ShapeDtypeStruct(loads.shape, F32)] * 2
    return pl.pallas_call(
        lambda *refs: bulk_kernel(sh, bool(edges), last, *refs),
        out_shape=out_shape,
        in_specs=[SM] + [VM] * (3 + len(edges)),
        out_specs=[VM] * len(out_shape),
        compiler_params=PARAMS,
        name="bulk",
    )(plan, f, *edges, loads, filt)


def patch_kernel(sh, last, plan, planes, *refs):
    forces = refs[: sh.tiles]
    out = refs[sh.tiles + 1]
    sems = refs[-1]
    me = lax.axis_index("gy")
    xs = sh.xs
    lanes = iota((xs, LANES), 1)
    xrows = iota((xs, LANES), 0)
    per = LANES // (2 * sh.levels)
    copies = []

    def send(q):
        if last:
            copy = pltpu.make_async_copy(out.at[q], refs[sh.tiles + 2].at[q], sems.at[q])
            copy.start()
            copies.append(copy)

    rotors = []
    for shift in range(sh.tiles):
        owner = lax.rem(me + sh.tiles - shift, sh.tiles)
        for slot in range(sh.slots):
            rotors.append(
                (plane_at(sh, plan, owner, slot), forces[shift], slot * 3, owner * sh.slots + slot)
            )

    for x, _, _, index in rotors:

        @pl.when(x >= 0)
        def _():
            here = [planes[index, q] for q in range(19)]
            force = [jnp.zeros((sh.levels, LANES), F32)] * 3
            for other, source, first, _ in rotors:
                same = (other == x).astype(F32)
                for axis in range(3):
                    at = (first + axis) * sh.levels
                    force[axis] = force[axis] + same * source[at : at + sh.levels, :]
            post = collide(here, force, range(19))
            rows = sh.levels - 1
            for q in range(19):
                dx, dy, dz = DIRS[q]
                value = post[q]
                moved = pltpu.roll(value, dy % LANES, 1) if dy else value
                to = lax.rem(x + (dx + xs), xs) if dx else x
                if dz == 0:
                    out[q, pl.ds(to, sh.levels, stride=xs), :] = moved
                elif dz == 1:
                    out[q, pl.ds(to + xs, rows, stride=xs), :] = moved[:rows]
                else:
                    out[q, pl.ds(to, rows, stride=xs), :] = moved[1:]
                if dz == 1:
                    out[OPPOSITE[q], pl.ds(x + rows * xs, 1), :] = value[rows:]
                elif dz == -1:
                    out[OPPOSITE[q], pl.ds(x, 1), :] = value[:1]

    for q in range(19):
        if q not in SIDEWAYS:
            send(q)

    ghost_force = [jnp.zeros((xs, LANES), F32) for axis in range(3)]
    tall = 2 * sh.levels
    for x, source, first, _ in rotors:
        ghosts = source[sh.section : sh.section + 8, :]
        for axis in range(3):
            k = first + axis
            ghost_force[axis] = ghost_force[axis] + jnp.where(
                xrows == x, ghosts[k : k + 1, :], 0.0
            )
    beyond = unpack_columns(sh, forces[1], forces[sh.tiles - 1], sh.section + 8 + sh.levels)
    ghost = [
        pltpu.roll(beyond[q // per], (LANES - (q % per) * tall) % LANES, 1) for q in range(19)
    ]
    posted = collide(ghost, ghost_force, SIDEWAYS)
    for k, q in enumerate(SIDEWAYS):
        dx, dy, dz = DIRS[q]
        value = posted[q]
        if dx:
            value = pltpu.roll(value, dx % xs, 0)
        for z in range(sh.levels):
            if not 0 <= z - dz < sh.levels:
                continue
            at = pl.ds(z * xs, xs)
            here = out[q, at, :]
            if dy == 1:
                other = pltpu.roll(value, (LANES - 2 * (z - dz)) % LANES, 1)
                here = jnp.where(lanes == 0, other, here)
            else:
                other = pltpu.roll(value, LANES - 2 - 2 * (z - dz), 1)
                here = jnp.where(lanes == LANES - 1, other, here)
            out[q, at, :] = here
        send(q)
    for copy in copies:
        copy.wait()


def do_patch(sh, last, plan, planes, forces, bulk):
    out_shape = [pltpu.VMEM(bulk.shape, F32)]
    if last:
        out_shape.append(jax.ShapeDtypeStruct(bulk.shape, F32))
    return pl.pallas_call(
        lambda *refs: patch_kernel(sh, last, *refs),
        out_shape=out_shape,
        in_specs=[SM] + [VM] * (2 + sh.tiles),
        out_specs=[VM] + [HB] * last,
        scratch_shapes=[
            pltpu.SemaphoreType.DMA((19,)),
        ],
        input_output_aliases={2 + sh.tiles: 0},
        compiler_params=PARAMS,
        name="patch",
    )(plan, planes, *forces, bulk)


def finish_kernel(sh, held, low, high, f_old, f, merged, sem):
    del f_old
    rows = iota((8, LANES), 0)
    copies = []
    for side, dirs, edge in ((0, PLUS, low), (1, MINUS, high)):
        at_row = 0 if side == 0 else 7
        first = 0 if side == 0 else sh.xs - 8
        for k, q in enumerate(dirs):
            index = side * len(PLUS) + k
            for z in range(sh.levels):
                value = held[q, z * sh.xs + first : z * sh.xs + first + 8, :]
                blocked = (DIRS[q][2] == 1 and z == 0) or (
                    DIRS[q][2] == -1 and z == sh.levels - 1
                )
                if not blocked:
                    value = jnp.where(rows == at_row, edge[k, z : z + 1, :], value)
                merged[index, z] = value
            copy = pltpu.make_async_copy(
                merged.at[index], f.at[q, :, first : first + 8, :], sem.at[index]
            )
            copy.start()
            copies.append(copy)
    for copy in copies:
        copy.wait()


def finish(sh, held, f, edges):
    f = f.reshape(19, sh.levels, sh.xs, LANES)
    return pl.pallas_call(
        lambda *refs: finish_kernel(sh, *refs),
        out_shape=jax.ShapeDtypeStruct(f.shape, F32),
        in_specs=[VM, VM, VM, HB],
        out_specs=HB,
        scratch_shapes=[
            pltpu.VMEM((2 * len(PLUS), sh.levels, 8, LANES), F32),
            pltpu.SemaphoreType.DMA((2 * len(PLUS),)),
        ],
        input_output_aliases={3: 0},
        compiler_params=PARAMS,
        name="finish",
    )(held, *edges, f)


def by_group(sh, x):
    head = x.shape[:-2]
    x = x.reshape(*head, sh.slots, sh.groups, LANES)
    return jnp.swapaxes(x, -3, -2).reshape(*head, sh.slots * sh.groups, LANES)


def by_slot(sh, x):
    head = x.shape[:-2]
    x = x.reshape(*head, sh.groups, sh.slots, LANES)
    return jnp.swapaxes(x, -3, -2).reshape(*head, sh.slots, sh.markers)


def shifted(x, axis, by):
    count = lax.axis_size(axis)
    return lax.ppermute(x, axis, [(i, (i + by) % count) for i in range(count)])


def swapped(x, axis, first):
    count = lax.axis_size(axis)
    pairs = [(i, (i + 1) % count) for i in range(first, count, 2)]
    return lax.ppermute(x, axis, pairs + [(b, a) for a, b in pairs])


def join_kernel(one, two, low, high):
    even = lax.rem(lax.axis_index("gx"), 2) == 0
    low[...] = jnp.where(even, two[...], one[...])
    high[...] = jnp.where(even, one[...], two[...])


def exchange(one, two):
    two = swapped(two, "gx", 1)
    one = swapped(one, "gx", 0)
    out = pl.pallas_call(
        join_kernel,
        out_shape=[pltpu.VMEM(one.shape, F32)] * 2,
        in_specs=[VM, VM],
        out_specs=[VM, VM],
        compiler_params=PARAMS,
        name="join",
    )(in_vmem(one), in_vmem(two))
    return tuple(in_vmem(x) for x in out)


def local(
    f_in,
    rotor_place,
    marker_cell,
    pitch_phase,
    blade_area,
    blade_twist,
    blade_speed,
    blade_angle,
    filt_in,
):
    sh = Shape(f_in, rotor_place, marker_cell, pitch_phase, filt_in)
    area, twist, speed, angle = [
        by_group(sh, x[0, 0]) for x in (blade_area, blade_twist, blade_speed, blade_angle)
    ]
    filt = by_group(sh, jnp.swapaxes(filt_in[0, 0], 0, 1))
    plan, blades, f = start(sh, rotor_place, pitch_phase, twist, angle, f_in)
    edges = ()
    for step in range(sh.steps):
        last = step == sh.steps - 1
        if step == 0:
            columns = make_columns(sh, plan, f, edges)
            sections = make_sections(sh, plan, f, edges, columns)
            tables = make_tables(sh, plan, marker_cell, in_vmem(sections[0]))
        else:
            sections = make_sections(sh, plan, f, edges, ())
            columns = make_columns(sh, plan, f, edges)
        sections = [sections[0]] + [
            shifted(sections[by], "gy", by) for by in range(1, sh.tiles)
        ]
        filt, loads, forces = do_markers(
            sh,
            step,
            plan,
            tables,
            (area, speed),
            blades,
            filt,
            columns,
            [in_vmem(section) for section in sections],
        )
        forces = [forces[0]] + [shifted(forces[by], "gy", by) for by in range(1, sh.tiles)]
        forces = [in_vmem(force) for force in forces]
        bulk = do_bulk(sh, last, plan, f, edges, loads, filt)
        if last:
            loads_out, filt_out = bulk[2:]
        planes = in_vmem(bulk[1])
        bulk = in_vmem(bulk[0])
        sent = make_edges(sh, plan, f, edges, forces, bulk)
        done = do_patch(sh, last, plan, planes, forces, bulk)
        edges = exchange(*sent)
        f = in_vmem(done[0])
    f = finish(sh, f, done[1], edges)
    loads_out, filt_out = [
        jnp.swapaxes(by_slot(sh, x), 0, 1)[None, None] for x in (loads_out, filt_out)
    ]
    return f, loads_out, filt_out


def solution(mesh):
    in_specs = (
        P(None, None, "gx", "gy"),
        P(),
        P(),
        P(),
        P("gx", "gy", None, None),
        P("gx", "gy", None, None),
        P("gx", "gy", None, None),
        P("gx", "gy", None, None),
        P("gx", "gy", None, None, None),
    )
    out_specs = (
        P(None, None, "gx", "gy"),
        P("gx", "gy", None, None, None),
        P("gx", "gy", None, None, None),
    )
    return jax.shard_map(local, mesh=mesh, in_specs=in_specs, out_specs=out_specs, check_vma=False)
```

```python
import math

import jax
import jax.numpy as jnp
from jax import lax
from jax.experimental import pallas as pl
from jax.experimental.pallas import tpu as pltpu
from jax.sharding import PartitionSpec as P

PHASES = 64
PAIRS = [
    (1, 0, 0),
    (0, 1, 0),
    (0, 0, 1),
    (1, 1, 0),
    (1, -1, 0),
    (1, 0, 1),
    (1, 0, -1),
    (0, 1, 1),
    (0, 1, -1),
]
DIRS = [(0, 0, 0)]
for along in PAIRS:
    DIRS.append(along)
    DIRS.append(tuple(-part for part in along))
OPPOSITE = [0] + [q + 1 if q % 2 else q - 1 for q in range(1, 19)]
PLUS = [q for q in range(19) if DIRS[q][0] == 1]
MINUS = [q for q in range(19) if DIRS[q][0] == -1]
SIDEWAYS = [q for q in range(19) if DIRS[q][1] != 0]
OMEGA = 1.0 / 0.6
KEEP = 1.0 - OMEGA
GUO = 1.0 - 0.5 * OMEGA
SPREAD = 0.01
MIX = 0.5
PITCH_AMP = 0.2
LANES = 128
F32 = jnp.float32
BF16 = jnp.bfloat16
VMEM_LIMIT = 8 * 1024 * 1024


def iota(shape, axis):
    return lax.broadcasted_iota(jnp.int32, shape, axis)


def aligned(value, by):
    return value if isinstance(value, int) else pl.multiple_of(value, by)


def wrapped(value):
    return value % LANES if isinstance(value, int) else lax.rem(value, LANES)


def moments(f):
    sums = [f[2 * k + 1] + f[2 * k + 2] for k in range(9)]
    gaps = [f[2 * k + 1] - f[2 * k + 2] for k in range(9)]
    density = f[0]
    for part in sums:
        density = density + part
    momentum = []
    for axis in range(3):
        total = None
        for k in range(9):
            sign = PAIRS[k][axis]
            if sign == 0:
                continue
            if total is None:
                total = gaps[k]
            else:
                total = total + gaps[k] if sign > 0 else total - gaps[k]
        momentum.append(total)
    return density, momentum


def collide(f, force, wanted):
    density, momentum = moments(f)
    inverse = 1.0 / density
    relaxed = OMEGA * density
    if force is None:
        v = [momentum[a] * inverse for a in range(3)]
        square = v[0] * v[0] + v[1] * v[1] + v[2] * v[2]
        base = relaxed * (1.0 - 1.5 * square)
        drive = [OMEGA * momentum[a] for a in range(3)]
        bend = [4.5 * part for part in drive]
    else:
        v = [(momentum[a] + 0.5 * force[a]) * inverse for a in range(3)]
        square = v[0] * v[0] + v[1] * v[1] + v[2] * v[2]
        work = v[0] * force[0] + v[1] * force[1] + v[2] * force[2]
        base = relaxed * (1.0 - 1.5 * square) - (3.0 * GUO) * work
        drive = [relaxed * v[a] + GUO * force[a] for a in range(3)]
        bend = [(4.5 * relaxed) * v[a] + (9.0 * GUO) * force[a] for a in range(3)]
    post = {}
    if 0 in wanted:
        post[0] = KEEP * f[0] + base * (1.0 / 3.0)
    scaled = {}
    for weight in (18.0, 36.0):
        scaled[weight] = (
            base * (1.0 / weight),
            [part * (3.0 / weight) for part in drive],
            [part * (1.0 / weight) for part in bend],
        )

    def along(k, parts):
        total = None
        for axis in range(3):
            sign = PAIRS[k][axis]
            if sign == 0:
                continue
            if total is None:
                total = parts[axis]
            else:
                total = total + parts[axis] if sign > 0 else total - parts[axis]
        return total

    for k in range(9):
        if 2 * k + 1 not in wanted and 2 * k + 2 not in wanted:
            continue
        level, drives, bends = scaled[18.0 if k < 3 else 36.0]
        even = level + along(k, v) * along(k, bends)
        odd = along(k, drives)
        if 2 * k + 1 in wanted:
            post[2 * k + 1] = KEEP * f[2 * k + 1] + (even + odd)
        if 2 * k + 2 in wanted:
            post[2 * k + 2] = KEEP * f[2 * k + 2] + (even - odd)
    return post


def outside(q, levels, rows):
    if DIRS[q][2] == 1:
        return rows == 0
    if DIRS[q][2] == -1:
        return rows == levels - 1
    return None


class Shape:
    def __init__(self, f_in, rotor_place, marker_cell, pitch_phase, filt_in):
        self.levels = f_in.shape[1]
        self.xs = f_in.shape[2]
        self.rotors = rotor_place.shape[0]
        self.steps = pitch_phase.shape[1]
        self.markers = marker_cell.shape[1]
        self.slots = filt_in.shape[2]
        self.tiles = lax.axis_size("gy")
        self.groups = self.markers // LANES
        self.section = self.slots * 3 * self.levels


def in_vmem(x):
    return pltpu.with_memory_space_constraint(x, pltpu.VMEM)


def in_hbm(x):
    return pltpu.with_memory_space_constraint(x, pltpu.HBM)


def in_smem(x):
    return pltpu.with_memory_space_constraint(x, pltpu.SMEM)


VM = pl.BlockSpec(memory_space=pltpu.VMEM)
SM = pl.BlockSpec(memory_space=pltpu.SMEM)
HB = pl.BlockSpec(memory_space=pl.ANY)
PARAMS = pltpu.CompilerParams(vmem_limit_bytes=VMEM_LIMIT)


def write_plan(sh, place, plan):
    row = lax.axis_index("gx")
    shape = (sh.tiles, sh.rotors)
    mine = jnp.logical_and(place[2:3, :] == iota(shape, 0), place[0:1, :] == row)
    keys = iota(shape, 1) * sh.xs + place[1:2, :]
    none = sh.rotors * sh.xs
    last = jnp.full((sh.tiles, 1), -1, jnp.int32)
    for slot in range(sh.slots):
        left = jnp.logical_and(mine, keys > last)
        last = jnp.min(jnp.where(left, keys, none), axis=1, keepdims=True)
        for owner in range(sh.tiles):
            key = last[owner, 0]
            plan[owner * sh.slots + slot] = jnp.where(key < none, key, -1)


def plane_at(sh, plan, owner, slot):
    key = plan[owner * sh.slots + slot]
    return jnp.where(key < 0, -1, lax.rem(key, sh.xs))


def rotor_at(sh, plan, slot):
    key = plan[lax.axis_index("gy") * sh.slots + slot]
    return jnp.where(key < 0, -1, lax.div(key, sh.xs))


def plane_of(sh, f, x, low, high):
    rows = iota((sh.levels, LANES), 0)
    planes = []
    for q in range(19):
        value = f[q, pl.ds(x, sh.levels, stride=sh.xs), :]
        if low is not None and DIRS[q][0] != 0:
            if DIRS[q][0] == 1:
                other, at = low[PLUS.index(q)], 0
            else:
                other, at = high[MINUS.index(q)], sh.xs - 1
            here = jnp.asarray(x == at)
            skip = outside(q, sh.levels, rows)
            use = here if skip is None else jnp.logical_and(here, jnp.logical_not(skip))
            value = jnp.where(use, other, value)
        planes.append(value)
    return planes


def write_sections(sh, plan, f, low, high, outs, held):
    me = lax.axis_index("gy")
    for shift in range(sh.tiles):
        owner = lax.rem(me + shift, sh.tiles)
        for slot in range(sh.slots):
            x = plane_at(sh, plan, owner, slot)

            @pl.when(x >= 0)
            def _():
                planes = plane_of(sh, f, x, low, high)
                for q, value in enumerate(planes):
                    held[owner * sh.slots + slot, q] = value
                density, momentum = moments(planes)
                inverse = 1.0 / density
                for axis in range(3):
                    at = (slot * 3 + axis) * sh.levels
                    outs[shift][at : at + sh.levels, :] = momentum[axis] * inverse

            @pl.when(x < 0)
            def _():
                at = slot * 3 * sh.levels
                outs[shift][at : at + 3 * sh.levels, :] = jnp.zeros((3 * sh.levels, LANES), F32)


def sincos(x):
    turns = jnp.floor(x * (2.0 / math.pi) + 0.5)
    r = x - turns * 1.5703125
    r = r - turns * 4.837512969970703125e-4
    r = r - turns * 7.549789954891882e-8
    r2 = r * r
    sin_r = r + r * r2 * (
        -1.0 / 6 + r2 * (1.0 / 120 + r2 * (-1.0 / 5040 + r2 * (1.0 / 362880)))
    )
    cos_r = (
        1.0
        - 0.5 * r2
        + r2
        * r2
        * (1.0 / 24 + r2 * (-1.0 / 720 + r2 * (1.0 / 40320 - r2 * (1.0 / 3628800))))
    )
    quarter = turns.astype(jnp.int32)
    swap = (quarter & 1) == 1
    sin_x = jnp.where(swap, cos_r, sin_r)
    cos_x = jnp.where(swap, sin_r, cos_r)
    sin_x = jnp.where((quarter & 2) == 2, -sin_x, sin_x)
    cos_x = jnp.where(((quarter + 1) & 2) == 2, -cos_x, cos_x)
    return sin_x, cos_x


def write_blades(sh, plan, phases, twist, angle, blades):
    blades[0], blades[1] = sincos(angle[...])
    sin_twist, cos_twist = sincos(twist[...])
    owner = iota((1, LANES), 1)
    rows = iota((sh.slots * sh.groups, LANES), 0) % sh.slots
    phase = jnp.zeros((1, LANES), F32)
    for step in range(sh.steps):
        for slot in range(sh.slots):
            rotor = jnp.maximum(rotor_at(sh, plan, slot), 0)
            here = owner == step * sh.slots + slot
            phase = jnp.where(here, phases[step, rotor].astype(F32), phase)
    pitch = PITCH_AMP * sincos((2.0 * math.pi / PHASES) * phase)[0]
    pitched = sincos(pitch)
    for step in range(sh.steps):
        parts = []
        for part in pitched:
            total = jnp.zeros((sh.slots * sh.groups, LANES), F32)
            for slot in range(sh.slots):
                lane = step * sh.slots + slot
                total = jnp.where(rows == slot, part[:, lane : lane + 1], total)
            parts.append(total)
        blades[2 + 2 * step] = sin_twist * parts[1] + cos_twist * parts[0]
        blades[3 + 2 * step] = cos_twist * parts[1] - sin_twist * parts[0]


def start_kernel(
    sh, place_in, phases_in, twist_in, angle_in, f_in, plan, blades, f, place, phases, twist, angle, sems
):
    pairs = ((place_in, place), (phases_in, phases), (angle_in, angle), (twist_in, twist))
    copies = [pltpu.make_async_copy(*pair, sems.at[k]) for k, pair in enumerate(pairs)]
    whole = pltpu.make_async_copy(f_in, f, sems.at[4])
    for copy in copies:
        copy.start()
    whole.start()
    for copy in copies:
        copy.wait()
    write_plan(sh, place, plan)
    write_blades(sh, plan, phases, twist, angle, blades)
    whole.wait()


def start(sh, rotor_place, phases, twist, angle, f_in):
    rows = sh.slots * sh.groups
    plan, blades, f = pl.pallas_call(
        lambda *refs: start_kernel(sh, *refs),
        out_shape=[
            pltpu.SMEM((sh.tiles * sh.slots,), jnp.int32),
            pltpu.VMEM((2 + 2 * sh.steps, rows, LANES), F32),
            pltpu.VMEM((19, sh.levels * sh.xs, LANES), F32),
        ],
        in_specs=[HB] * 5,
        out_specs=[SM, VM, VM],
        scratch_shapes=[
            pltpu.VMEM((3, sh.rotors), jnp.int32),
            pltpu.SMEM((sh.steps, sh.rotors), jnp.int32),
            pltpu.VMEM((rows, LANES), F32),
            pltpu.VMEM((rows, LANES), F32),
            pltpu.SemaphoreType.DMA((5,)),
        ],
        compiler_params=PARAMS,
        name="start",
    )(
        in_hbm(jnp.transpose(rotor_place)),
        in_hbm(jnp.transpose(phases)),
        in_hbm(twist),
        in_hbm(angle),
        in_hbm(f_in.reshape(19, sh.levels * sh.xs, LANES)),
    )
    return in_smem(plan), in_vmem(blades), in_vmem(f)


def section_kernel(sh, has_edges, plan, f, *refs):
    low, high = refs[:2] if has_edges else (None, None)
    write_sections(sh, plan, f, low, high, refs[-sh.tiles - 1 : -1], refs[-1])


def make_sections(sh, plan, f, edges, after):
    out = pl.pallas_call(
        lambda *refs: section_kernel(sh, bool(edges), *refs),
        out_shape=[pltpu.VMEM((sh.section, LANES), F32)] * sh.tiles
        + [pltpu.VMEM((sh.tiles * sh.slots, 19, sh.levels, LANES), F32)],
        in_specs=[SM] + [VM] * (1 + len(edges) + len(after)),
        out_specs=[VM] * (sh.tiles + 1),
        compiler_params=PARAMS,
        name="sections",
    )(plan, f, *edges, *after)
    return out[:-1], in_vmem(out[-1])


def column_kernel(sh, has_edges, *refs):
    f = refs[1]
    low, high = refs[2:4] if has_edges else (None, None)
    east, west = refs[-2:]
    packed = []
    pairs = iota((sh.xs, LANES), 1) // 2
    xrows = iota((sh.xs, LANES), 0)
    per = LANES // (2 * sh.levels)
    groups = (19 + per - 1) // per
    for group in range(groups):
        total = jnp.ones((sh.xs, LANES), F32)
        for q in range(group * per, min(19, (group + 1) * per)):
            for z in range(sh.levels):
                tile = f[q, z * sh.xs : (z + 1) * sh.xs, :]
                if has_edges and DIRS[q][0] != 0:
                    blocked = (DIRS[q][2] == 1 and z == 0) or (
                        DIRS[q][2] == -1 and z == sh.levels - 1
                    )
                    if not blocked:
                        if DIRS[q][0] == 1:
                            tile = jnp.where(xrows == 0, low[PLUS.index(q), z : z + 1, :], tile)
                        else:
                            tile = jnp.where(
                                xrows == sh.xs - 1, high[MINUS.index(q), z : z + 1, :], tile
                            )
                pair = (q % per) * sh.levels + z
                total = jnp.where(
                    pairs == pair, pltpu.roll(tile, (2 * pair + 1) % LANES, 1), total
                )
        packed.append(total)
    zpairs = iota((sh.levels, LANES), 1) // 2
    corners = jnp.ones((sh.levels, LANES), F32)
    for which, x in ((0, 0), (1, sh.xs - 1)):
        planes = plane_of(sh, f, x, low, high)
        for q in range(19):
            pair = 2 * q + which
            corners = jnp.where(zpairs == pair, pltpu.roll(planes[q], 2 * pair + 1, 1), corners)
    packed.append(corners)
    even = iota((sh.xs, LANES), 1) % 2 == 0
    for k in range(len(packed) // 2):
        first, second = packed[2 * k], packed[2 * k + 1]
        rows = slice(k * sh.xs, (k + 1) * sh.xs)
        east[rows, :] = jnp.where(even, first, pltpu.roll(second, 1, 1))
        west[rows, :] = jnp.where(even, pltpu.roll(first, LANES - 1, 1), second)


def packed_columns(sh):
    per = LANES // (2 * sh.levels)
    return (19 + per - 1) // per + 1


def unpack_columns(sh, left, right, first):
    even = iota((sh.xs, LANES), 1) % 2 == 0
    groups = []
    for k in range(packed_columns(sh) // 2):
        rows = pl.ds(first + k * sh.xs, sh.xs)
        a, b = left[rows, :], right[rows, :]
        groups.append(jnp.where(even, a, pltpu.roll(b, 1, 1)))
        groups.append(jnp.where(even, pltpu.roll(a, LANES - 1, 1), b))
    return groups


def make_columns(sh, plan, f, edges):
    shape = (packed_columns(sh) // 2 * sh.xs, LANES)
    out = pl.pallas_call(
        lambda *refs: column_kernel(sh, bool(edges), *refs),
        out_shape=[pltpu.VMEM(shape, F32)] * 2,
        in_specs=[SM] + [VM] * (1 + len(edges)),
        out_specs=[VM] * 2,
        compiler_params=PARAMS,
        name="columns",
    )(plan, f, *edges)
    return [in_vmem(x) for x in out]


def peskin(offsets):
    distance = jnp.abs(offsets)
    near_arg = jnp.maximum(1.0 + 4.0 * distance - 4.0 * distance * distance, 1.0)
    far_arg = jnp.maximum(-7.0 + 12.0 * distance - 4.0 * distance * distance, 1.0)
    near = distance <= 1.0
    root = jnp.sqrt(jnp.where(near, near_arg, far_arg))
    return (jnp.where(near, 3.0, 5.0) - 2.0 * distance + jnp.where(near, root, -root)) * 0.125


TABLE_CHUNK = 1024


def table_kernel(sh, plan, cells, after, across, upward, info, codes, lines, sem):
    del after
    ids = [rotor_at(sh, plan, slot) for slot in range(sh.slots)]
    copies = []
    for slot in range(sh.slots):
        first = pl.multiple_of(jnp.maximum(ids[slot], 0) // 8 * 8, 8)
        copy = pltpu.make_async_copy(cells.at[pl.ds(first, 8), :], codes.at[slot], sem.at[slot])
        copy.start()
        copies.append(copy)
    width = min(TABLE_CHUNK, sh.markers)
    part = iota((8, width), 0)
    spanwise = part < 4
    cell_bits = 6 + sh.levels.bit_length() - 1
    quarter = LANES // 4
    packed = 16
    ycells = [
        (iota((packed, LANES), 0) + first).astype(F32).astype(BF16)
        for first in range(0, quarter, packed)
    ]
    zcells = iota((sh.levels, LANES), 0)
    for slot in range(sh.slots):
        copies[slot].wait()

        @pl.when(ids[slot] >= 0)
        def _():
            line = ids[slot] % 8
            every = codes[slot, pl.ds(line, 1), :] >> cell_bits
            lowest = jnp.min(every)
            highest = jnp.max(every)
            narrow = highest - lowest + 4 <= LANES
            start = jnp.where(narrow, lowest, lowest // LANES * LANES)
            info[2 * slot] = start
            info[2 * slot + 1] = jnp.where(narrow, 1, 2)

            def chunk(window, at):
                code = codes[slot, pl.ds(line, 1), pl.ds(at, width)]
                cells = (code >> cell_bits) - (start + window * LANES)
                levels = (code >> 6) & (sh.levels - 1)
                eighths = jnp.where(spanwise, code >> 3, code) & 7
                corner = jnp.where(spanwise, (part - cells) & 3, part - 4)
                weights = peskin(corner.astype(F32) - 1.0 - eighths.astype(F32) * 0.125)
                places = ((cells + corner - part) >> 2).astype(F32)
                top = weights.astype(BF16).astype(F32)
                rest = weights - top
                lines[0] = places
                lines[1] = top
                lines[2] = rest
                lines[3] = weights
                for group in range(width // LANES):
                    lanes = slice(group * LANES, (group + 1) * LANES)
                    to = pl.ds(at + group * LANES, LANES)
                    tall = jnp.zeros((sh.levels, LANES), F32)
                    for j in range(4):
                        tall = jnp.where(
                            zcells == levels[:, lanes] + j, lines[3, 4 + j : 5 + j, lanes], tall
                        )
                    upward[slot, :, to] = tall

                    def spread_line(k, kind):
                        line = lines[k, kind : kind + 1, lanes]
                        return jnp.broadcast_to(line, (packed, LANES)).astype(BF16)

                    for kind in range(4):
                        spot, high, low = [spread_line(k, kind) for k in range(3)]
                        for k, cell in enumerate(ycells):
                            here = cell == spot
                            for half, source in ((0, high), (1, low)):
                                row = half * LANES + kind * quarter + k * packed
                                across[slot, window, row : row + packed, to] = jnp.where(
                                    here, source, jnp.zeros((), BF16)
                                )

            def sweep(window):
                def body(i, carry):
                    chunk(window, pl.multiple_of(i * width, width))
                    return carry

                lax.fori_loop(0, sh.markers // width, body, 0)

            sweep(0)

            @pl.when(jnp.logical_not(narrow))
            def _():
                sweep(1)


def make_tables(sh, plan, marker_cell, after):
    across, upward, info = pl.pallas_call(
        lambda *refs: table_kernel(sh, *refs),
        out_shape=[
            pltpu.VMEM((sh.slots, 2, 2 * LANES, sh.markers), BF16),
            pltpu.VMEM((sh.slots, sh.levels, sh.markers), F32),
            pltpu.SMEM((2 * sh.slots,), jnp.int32),
        ],
        in_specs=[SM, HB, VM],
        out_specs=[VM, VM, SM],
        scratch_shapes=[
            pltpu.VMEM((sh.slots, 8, sh.markers), jnp.int32),
            pltpu.VMEM((4, 8, min(TABLE_CHUNK, sh.markers)), F32),
            pltpu.SemaphoreType.DMA((sh.slots,)),
        ],
        compiler_params=PARAMS,
        name="tables",
    )(plan, marker_cell, after)
    return in_vmem(across), in_vmem(upward), in_smem(info)


GHOST_LANES = 32
SAMPLE_CHUNK = 8192
SPREAD_CHUNK = 8192


def split(value):
    top = value.astype(BF16)
    return top, (value - top.astype(F32)).astype(BF16)


def marker_kernel(
    sh, step, plan, info, across, upward, area, speed, blades, filt_old, east, west, *refs
):
    sections = refs[: sh.tiles]
    filt_new, loads = refs[sh.tiles : sh.tiles + 2]
    forces = refs[sh.tiles + 2 : 2 * sh.tiles + 2]
    around, sampled, weighted, spread, turning = refs[2 * sh.tiles + 2 :]
    me = lax.axis_index("gy")
    tall = 3 * sh.levels
    quarter = LANES // 4
    rows = iota((LANES, LANES), 0)
    kinds = iota((LANES, LANES), 1)
    by_class = (rows == kinds % quarter * 4 + kinds // quarter).astype(F32).astype(BF16)
    from_class = (kinds == rows % quarter * 4 + rows // quarter).astype(F32).astype(BF16)
    for shift in range(sh.tiles):
        around[lax.rem(me + sh.tiles - shift, sh.tiles)] = sections[shift][...]
    spread[...] = jnp.zeros(spread.shape, F32)

    def window_of(slot, window):
        start = info[2 * slot] + window * LANES
        tile = start // LANES
        return tile, jnp.minimum(tile + 1, sh.tiles - 1), start - tile * LANES

    def windows(slot, body):
        @pl.when(rotor_at(sh, plan, slot) >= 0)
        def _():
            body(0)

            @pl.when(info[2 * slot + 1] > 1)
            def _():
                body(1)

    for slot in range(sh.slots):
        rows = pl.ds(slot * tall, tall)

        def sample(window):
            tile, after, offset = window_of(slot, window)
            both = jnp.concatenate([around[tile, rows, :], around[after, rows, :]], axis=1)
            seen = pltpu.roll(both, lax.rem(2 * LANES - offset, 2 * LANES), 1)[:, :LANES]
            top, rest = split(seen)
            left = jnp.concatenate([top, rest], axis=0)
            left = jnp.dot(left, by_class, preferred_element_type=F32).astype(BF16)
            left = jnp.concatenate([left, left], axis=1)

            def chunk(i, carry):
                at = pl.multiple_of(i * SAMPLE_CHUNK, SAMPLE_CHUNK)
                value = jnp.dot(
                    left,
                    across[slot, window, :, pl.ds(at, SAMPLE_CHUNK)],
                    preferred_element_type=F32,
                )
                value = value[:tall] + value[tall:]
                heights = upward[slot, :, pl.ds(at, SAMPLE_CHUNK)]
                for axis in range(3):
                    part = jnp.sum(
                        value[axis * sh.levels : (axis + 1) * sh.levels] * heights,
                        axis=0,
                        keepdims=True,
                    )
                    for group in range(SAMPLE_CHUNK // LANES):
                        row = (i * (SAMPLE_CHUNK // LANES) + group) * sh.slots + slot
                        piece = part[:, group * LANES : (group + 1) * LANES]
                        if window:
                            piece = piece + sampled[axis, pl.ds(row, 1), :]
                        sampled[axis, pl.ds(row, 1), :] = piece
                return carry

            lax.fori_loop(0, sh.markers // SAMPLE_CHUNK, chunk, 0)

        windows(slot, sample)

    felt = []
    for axis in range(3):
        old = filt_old[axis]
        value = old + MIX * (sampled[axis] - old)
        filt_new[axis] = value
        felt.append(value)
    sin_t = blades[0]
    cos_t = blades[1]
    tangent = speed[...] + sin_t * felt[1] - cos_t * felt[2]
    square = felt[0] * felt[0] + tangent * tangent
    inverse = 1.0 / jnp.sqrt(square)
    sin_p = felt[0] * inverse
    cos_p = tangent * inverse
    sin_b = blades[2 + 2 * step]
    cos_b = blades[3 + 2 * step]
    sin_a = sin_p * cos_b - cos_p * sin_b
    cos_a = cos_p * cos_b + sin_p * sin_b
    lift = (2.0 * math.pi) * sin_a * cos_a
    drag = 0.02 + sin_a * sin_a
    dynamic = 0.5 * area[...] * square
    around_axis = dynamic * (lift * sin_p - drag * cos_p)
    loads[0] = dynamic * (lift * cos_p + drag * sin_p)
    loads[1] = -around_axis * sin_t
    loads[2] = around_axis * cos_t

    for slot in range(sh.slots):
        rows = pl.ds(slot * tall, tall)

        def spread_out(window):
            tile, after, offset = window_of(slot, window)

            def chunk(i, total):
                at = pl.multiple_of(i * SPREAD_CHUNK, SPREAD_CHUNK)
                for group in range(SPREAD_CHUNK // LANES):
                    heights = upward[slot, :, pl.ds(at + group * LANES, LANES)]
                    row = (i * (SPREAD_CHUNK // LANES) + group) * sh.slots + slot
                    parts = [heights * loads[axis, pl.ds(row, 1), :] for axis in range(3)]
                    top, rest = split(jnp.concatenate(parts, axis=0))
                    weighted[:tall, group * LANES : (group + 1) * LANES] = top
                    weighted[tall:, group * LANES : (group + 1) * LANES] = rest
                return total + lax.dot_general(
                    across[slot, window, :, pl.ds(at, SPREAD_CHUNK)],
                    weighted[...],
                    (((1,), (1,)), ((), ())),
                    preferred_element_type=F32,
                )

            total = lax.fori_loop(
                0,
                sh.markers // SPREAD_CHUNK,
                chunk,
                jnp.zeros((2 * LANES, 2 * tall), F32),
            )
            total = jnp.transpose(total)
            total = total[:tall] + total[tall:]
            total = -SPREAD * (total[:, :LANES] + total[:, LANES:])
            pieces = []
            for _ in range(3):
                pieces.append(total.astype(BF16))
                total = total - pieces[-1].astype(F32)
            pieces = jnp.dot(
                jnp.concatenate(pieces, axis=0), from_class, preferred_element_type=F32
            )
            total = pieces[:tall] + pieces[tall : 2 * tall] + pieces[2 * tall :]
            both = jnp.concatenate([total, jnp.zeros((tall, LANES), F32)], axis=1)
            both = pltpu.roll(both, offset, 1)
            spread[tile, rows, :] = spread[tile, rows, :] + both[:, :LANES]
            spread[after, rows, :] = spread[after, rows, :] + both[:, LANES:]

        windows(slot, spread_out)

    lanes = iota((sh.levels, LANES), 1)
    for shift in range(sh.tiles):
        tile = lax.rem(me + shift, sh.tiles)
        forces[shift][: sh.section, :] = spread[tile]
        before = lax.rem(tile + sh.tiles - 1, sh.tiles)
        after = lax.rem(tile + 1, sh.tiles)
        beyond = [jnp.zeros((sh.levels, LANES), F32)] * 2
        for k in range(3 * sh.slots):
            at = pl.ds(k * sh.levels, sh.levels)
            left = jnp.broadcast_to(spread[before, at, :][:, LANES - 1 :], (sh.levels, LANES))
            right = jnp.broadcast_to(spread[after, at, :][:, :1], (sh.levels, LANES))
            beyond[0] = jnp.where(lanes == k, left, beyond[0])
            beyond[1] = jnp.where(lanes == k, right, beyond[1])
        at = shift * GHOST_LANES
        for side in range(2):
            turning[pl.ds(at + side, sh.levels, stride=2), :] = beyond[side]
        forces[shift][sh.section + 8 : sh.section + 8 + sh.levels, :] = jnp.where(
            lanes < 8, beyond[0], pltpu.roll(beyond[1], 8, 1)
        )
    each = LANES // GHOST_LANES
    for first in range(0, sh.tiles, each):
        rows = jnp.transpose(turning[first * GHOST_LANES : (first + each) * GHOST_LANES, :])[:8]
        for k in range(each):
            forces[first + k][sh.section : sh.section + 8, :] = pltpu.roll(
                rows, (LANES - k * GHOST_LANES) % LANES, 1
            )
    forces[1][sh.section + 8 + sh.levels :, :] = east[...]
    forces[sh.tiles - 1][sh.section + 8 + sh.levels :, :] = west[...]


def do_markers(sh, step, plan, tables, fixed, blades, filt, columns, sections):
    across, upward, info = tables
    rows = sh.slots * sh.groups
    dense = pltpu.VMEM((3, rows, LANES), F32)
    plain = sh.section + 8 + sh.levels
    extra = columns[0].shape[0]
    forces = [
        pltpu.VMEM((plain + (extra if by in (1, sh.tiles - 1) else 0), LANES), F32)
        for by in range(sh.tiles)
    ]
    out = pl.pallas_call(
        lambda *refs: marker_kernel(sh, step, *refs),
        out_shape=[dense, dense] + forces,
        in_specs=[SM, SM] + [VM] * (8 + sh.tiles),
        out_specs=[VM] * (2 + sh.tiles),
        scratch_shapes=[
            pltpu.VMEM((sh.tiles, sh.section, LANES), F32),
            pltpu.VMEM((3, rows, LANES), F32),
            pltpu.VMEM((6 * sh.levels, SPREAD_CHUNK), BF16),
            pltpu.VMEM((sh.tiles, sh.section, LANES), F32),
            pltpu.VMEM((sh.tiles * GHOST_LANES, LANES), F32),
        ],
        compiler_params=PARAMS,
        name="markers",
    )(plan, info, across, upward, *fixed, blades, filt, *columns, *sections)
    return in_vmem(out[0]), in_vmem(out[1]), out[2:]


def edge_kernel(sh, has_edges, plan, f, *refs):
    low, high = refs[:2] if has_edges else (None, None)
    refs = refs[2 * has_edges :]
    forces = refs[: sh.tiles]
    outs = refs[sh.tiles + 1 :]
    me = lax.axis_index("gy")
    lanes = iota((sh.levels, LANES), 1)
    blank = jnp.zeros((sh.levels, LANES), F32)
    planes_at = (0, sh.xs - 1)
    even = lax.rem(lax.axis_index("gx"), 2) == 0
    beyond = unpack_columns(sh, forces[1], forces[sh.tiles - 1], sh.section + 8 + sh.levels)[-1]
    corner = [pltpu.roll(beyond, (LANES - 4 * q) % LANES, 1) for q in range(19)]
    corner_force = [blank, blank, blank]
    edge_force = [[blank, blank, blank], [blank, blank, blank]]
    for shift in range(sh.tiles):
        owner = lax.rem(me + sh.tiles - shift, sh.tiles)
        ghosts = forces[shift][sh.section + 8 : sh.section + 8 + sh.levels, :]
        for slot in range(sh.slots):
            x = plane_at(sh, plan, owner, slot)
            for axis in range(3):
                k = slot * 3 + axis
                piece = forces[shift][k * sh.levels : (k + 1) * sh.levels, :]
                for which in range(2):
                    here = jnp.asarray(x == planes_at[which])
                    edge_force[which][axis] = edge_force[which][axis] + jnp.where(here, piece, 0.0)
                    for side in range(2):
                        lane = 2 * which + side
                        moved = pltpu.roll(ghosts, (lane - side * 8 - k) % LANES, 1)
                        corner_force[axis] = corner_force[axis] + jnp.where(
                            jnp.logical_and(here, lanes == lane), moved, 0.0
                        )
    corner_post = collide(corner, corner_force, [q for q in PLUS + MINUS if DIRS[q][1]])
    leaving = ([], [])
    for which, wanted in ((1, PLUS), (0, MINUS)):
        planes = plane_of(sh, f, planes_at[which], low, high)
        post = collide(planes, edge_force[which], wanted)
        for k, q in enumerate(wanted):
            value = post[q]
            if DIRS[q][1] == 1:
                value = pltpu.roll(value, 1, 1)
                ghost = pltpu.roll(corner_post[q], (LANES - 2 * which) % LANES, 1)
                value = jnp.where(lanes == 0, ghost, value)
            elif DIRS[q][1] == -1:
                value = pltpu.roll(value, LANES - 1, 1)
                ghost = pltpu.roll(corner_post[q], LANES - 2 - 2 * which, 1)
                value = jnp.where(lanes == LANES - 1, ghost, value)
            if DIRS[q][2]:
                value = pltpu.roll(value, DIRS[q][2] % sh.levels, 0)
            leaving[which].append(value)
    for k, (down, up) in enumerate(zip(*leaving)):
        outs[0][k] = jnp.where(even, up, down)
        outs[1][k] = jnp.where(even, down, up)


def make_edges(sh, plan, f, edges, forces, after):
    return pl.pallas_call(
        lambda *refs: edge_kernel(sh, bool(edges), *refs),
        out_shape=[pltpu.VMEM((len(PLUS), sh.levels, LANES), F32)] * 2,
        in_specs=[SM] + [VM] * (2 + len(edges) + sh.tiles),
        out_specs=[VM] * 2,
        compiler_params=PARAMS,
        name="edges",
    )(plan, f, *edges, *forces, after)


def bulk_kernel(sh, has_edges, last, plan, f, *refs):
    low, high = refs[:2] if has_edges else (None, None)
    refs = refs[2 * has_edges :]
    loads, filt, out = refs[:3]
    xs = sh.xs
    xrows = iota((xs, LANES), 0)
    copies = []
    if last:
        masked, sems = refs[-2:]
        rows = iota((sh.slots * sh.groups, LANES), 0) % sh.slots
        used = jnp.zeros((sh.slots * sh.groups, LANES), jnp.int32)
        for slot in range(sh.slots):
            there = (rotor_at(sh, plan, slot) >= 0).astype(jnp.int32)
            used = jnp.where(rows == slot, there, used)
        for k, source in enumerate((loads, filt)):
            for axis in range(3):
                masked[k, axis] = jnp.where(used > 0, source[axis], 0.0)
            copy = pltpu.make_async_copy(masked.at[k], refs[3 + k], sems.at[k])
            copy.start()
            copies.append(copy)

    def level(z, bottom, top):
        at = aligned(z * xs, xs)
        here = []
        for q in range(19):
            tile = f[q, pl.ds(at, xs), :]
            if has_edges and DIRS[q][0] != 0:
                blocked = (DIRS[q][2] == 1 and bottom) or (DIRS[q][2] == -1 and top)
                if not blocked:
                    if DIRS[q][0] == 1:
                        tile = jnp.where(xrows == 0, low[PLUS.index(q), pl.ds(z, 1), :], tile)
                    else:
                        tile = jnp.where(
                            xrows == xs - 1, high[MINUS.index(q), pl.ds(z, 1), :], tile
                        )
            here.append(tile)
        post = collide(here, None, range(19))
        for q in range(19):
            dx, dy, dz = DIRS[q]
            value = post[q]
            if (dz == 1 and top) or (dz == -1 and bottom):
                to, target = OPPOSITE[q], z
            else:
                to, target = q, z + dz
                if dy:
                    value = pltpu.roll(value, dy % LANES, 1)
                if dx:
                    value = pltpu.roll(value, dx % xs, 0)
            out[to, pl.ds(aligned(target * xs, xs), xs), :] = value

    level(0, True, False)

    def middle(z, carry):
        level(z, False, False)
        return carry

    lax.fori_loop(1, sh.levels - 1, middle, 0)
    level(sh.levels - 1, False, True)
    for copy in copies:
        copy.wait()


def do_bulk(sh, last, plan, f, edges, loads, filt):
    out_shape = [pltpu.VMEM((19, sh.levels * sh.xs, LANES), F32)]
    scratch = []
    if last:
        out_shape += [jax.ShapeDtypeStruct(loads.shape, F32)] * 2
        scratch = [pltpu.VMEM((2, *loads.shape), F32), pltpu.SemaphoreType.DMA((2,))]
    return pl.pallas_call(
        lambda *refs: bulk_kernel(sh, bool(edges), last, *refs),
        out_shape=out_shape,
        in_specs=[SM] + [VM] * (3 + len(edges)),
        out_specs=[VM] + [HB] * (len(out_shape) - 1),
        scratch_shapes=scratch,
        compiler_params=PARAMS,
        name="bulk",
    )(plan, f, *edges, loads, filt)


def patch_kernel(sh, last, plan, planes, *refs):
    forces = refs[: sh.tiles]
    out = refs[sh.tiles + 1]
    sems = refs[-1]
    me = lax.axis_index("gy")
    xs = sh.xs
    lanes = iota((xs, LANES), 1)
    xrows = iota((xs, LANES), 0)
    per = LANES // (2 * sh.levels)
    copies = []

    def send(q):
        if last:
            copy = pltpu.make_async_copy(out.at[q], refs[sh.tiles + 2].at[q], sems.at[q])
            copy.start()
            copies.append(copy)

    rotors = []
    for shift in range(sh.tiles):
        owner = lax.rem(me + sh.tiles - shift, sh.tiles)
        for slot in range(sh.slots):
            rotors.append(
                (plane_at(sh, plan, owner, slot), forces[shift], slot * 3, owner * sh.slots + slot)
            )

    for x, _, _, index in rotors:

        @pl.when(x >= 0)
        def _():
            here = [planes[index, q] for q in range(19)]
            force = [jnp.zeros((sh.levels, LANES), F32)] * 3
            for other, source, first, _ in rotors:
                same = (other == x).astype(F32)
                for axis in range(3):
                    at = (first + axis) * sh.levels
                    force[axis] = force[axis] + same * source[at : at + sh.levels, :]
            post = collide(here, force, range(19))
            rows = sh.levels - 1
            for q in range(19):
                dx, dy, dz = DIRS[q]
                value = post[q]
                moved = pltpu.roll(value, dy % LANES, 1) if dy else value
                to = lax.rem(x + (dx + xs), xs) if dx else x
                if dz == 0:
                    out[q, pl.ds(to, sh.levels, stride=xs), :] = moved
                elif dz == 1:
                    out[q, pl.ds(to + xs, rows, stride=xs), :] = moved[:rows]
                else:
                    out[q, pl.ds(to, rows, stride=xs), :] = moved[1:]
                if dz == 1:
                    out[OPPOSITE[q], pl.ds(x + rows * xs, 1), :] = value[rows:]
                elif dz == -1:
                    out[OPPOSITE[q], pl.ds(x, 1), :] = value[:1]

    for q in range(19):
        if q not in SIDEWAYS:
            send(q)

    ghost_force = [jnp.zeros((xs, LANES), F32) for axis in range(3)]
    tall = 2 * sh.levels
    for x, source, first, _ in rotors:
        ghosts = source[sh.section : sh.section + 8, :]
        for axis in range(3):
            k = first + axis
            ghost_force[axis] = ghost_force[axis] + jnp.where(
                xrows == x, ghosts[k : k + 1, :], 0.0
            )
    beyond = unpack_columns(sh, forces[1], forces[sh.tiles - 1], sh.section + 8 + sh.levels)
    ghost = [
        pltpu.roll(beyond[q // per], (LANES - (q % per) * tall) % LANES, 1) for q in range(19)
    ]
    posted = collide(ghost, ghost_force, SIDEWAYS)
    for k, q in enumerate(SIDEWAYS):
        dx, dy, dz = DIRS[q]
        value = posted[q]
        if dx:
            value = pltpu.roll(value, dx % xs, 0)
        for z in range(sh.levels):
            if not 0 <= z - dz < sh.levels:
                continue
            at = pl.ds(z * xs, xs)
            here = out[q, at, :]
            if dy == 1:
                other = pltpu.roll(value, (LANES - 2 * (z - dz)) % LANES, 1)
                here = jnp.where(lanes == 0, other, here)
            else:
                other = pltpu.roll(value, LANES - 2 - 2 * (z - dz), 1)
                here = jnp.where(lanes == LANES - 1, other, here)
            out[q, at, :] = here
        send(q)
    for copy in copies:
        copy.wait()


def do_patch(sh, last, plan, planes, forces, bulk):
    out_shape = [pltpu.VMEM(bulk.shape, F32)]
    if last:
        out_shape.append(jax.ShapeDtypeStruct(bulk.shape, F32))
    return pl.pallas_call(
        lambda *refs: patch_kernel(sh, last, *refs),
        out_shape=out_shape,
        in_specs=[SM] + [VM] * (2 + sh.tiles),
        out_specs=[VM] + [HB] * last,
        scratch_shapes=[
            pltpu.SemaphoreType.DMA((19,)),
        ],
        input_output_aliases={2 + sh.tiles: 0},
        compiler_params=PARAMS,
        name="patch",
    )(plan, planes, *forces, bulk)


def finish_kernel(sh, held, low, high, f_old, f, merged, sem):
    del f_old
    rows = iota((8, LANES), 0)
    copies = []
    for side, dirs, edge in ((0, PLUS, low), (1, MINUS, high)):
        at_row = 0 if side == 0 else 7
        first = 0 if side == 0 else sh.xs - 8
        for k, q in enumerate(dirs):
            index = side * len(PLUS) + k
            for z in range(sh.levels):
                value = held[q, z * sh.xs + first : z * sh.xs + first + 8, :]
                blocked = (DIRS[q][2] == 1 and z == 0) or (
                    DIRS[q][2] == -1 and z == sh.levels - 1
                )
                if not blocked:
                    value = jnp.where(rows == at_row, edge[k, z : z + 1, :], value)
                merged[index, z] = value
            copy = pltpu.make_async_copy(
                merged.at[index], f.at[q, :, first : first + 8, :], sem.at[index]
            )
            copy.start()
            copies.append(copy)
    for copy in copies:
        copy.wait()


def finish(sh, held, f, edges):
    f = f.reshape(19, sh.levels, sh.xs, LANES)
    return pl.pallas_call(
        lambda *refs: finish_kernel(sh, *refs),
        out_shape=jax.ShapeDtypeStruct(f.shape, F32),
        in_specs=[VM, VM, VM, HB],
        out_specs=HB,
        scratch_shapes=[
            pltpu.VMEM((2 * len(PLUS), sh.levels, 8, LANES), F32),
            pltpu.SemaphoreType.DMA((2 * len(PLUS),)),
        ],
        input_output_aliases={3: 0},
        compiler_params=PARAMS,
        name="finish",
    )(held, *edges, f)


def by_group(sh, x):
    head = x.shape[:-2]
    x = x.reshape(*head, sh.slots, sh.groups, LANES)
    return jnp.swapaxes(x, -3, -2).reshape(*head, sh.slots * sh.groups, LANES)


def by_slot(sh, x):
    head = x.shape[:-2]
    x = x.reshape(*head, sh.groups, sh.slots, LANES)
    return jnp.swapaxes(x, -3, -2).reshape(*head, sh.slots, sh.markers)


def shifted(x, axis, by):
    count = lax.axis_size(axis)
    return lax.ppermute(x, axis, [(i, (i + by) % count) for i in range(count)])


def swapped(x, axis, first):
    count = lax.axis_size(axis)
    pairs = [(i, (i + 1) % count) for i in range(first, count, 2)]
    return lax.ppermute(x, axis, pairs + [(b, a) for a, b in pairs])


def join_kernel(one, two, low, high):
    even = lax.rem(lax.axis_index("gx"), 2) == 0
    low[...] = jnp.where(even, two[...], one[...])
    high[...] = jnp.where(even, one[...], two[...])


def exchange(one, two):
    two = swapped(two, "gx", 1)
    one = swapped(one, "gx", 0)
    out = pl.pallas_call(
        join_kernel,
        out_shape=[pltpu.VMEM(one.shape, F32)] * 2,
        in_specs=[VM, VM],
        out_specs=[VM, VM],
        compiler_params=PARAMS,
        name="join",
    )(in_vmem(one), in_vmem(two))
    return tuple(in_vmem(x) for x in out)


def local(
    f_in,
    rotor_place,
    marker_cell,
    pitch_phase,
    blade_area,
    blade_twist,
    blade_speed,
    blade_angle,
    filt_in,
):
    sh = Shape(f_in, rotor_place, marker_cell, pitch_phase, filt_in)
    area, twist, speed, angle = [
        by_group(sh, x[0, 0]) for x in (blade_area, blade_twist, blade_speed, blade_angle)
    ]
    filt = by_group(sh, jnp.swapaxes(filt_in[0, 0], 0, 1))
    plan, blades, f = start(sh, rotor_place, pitch_phase, twist, angle, f_in)
    edges = ()
    for step in range(sh.steps):
        last = step == sh.steps - 1
        if step == 0:
            columns = make_columns(sh, plan, f, edges)
            sections, planes = make_sections(sh, plan, f, edges, columns)
            tables = make_tables(sh, plan, marker_cell, in_vmem(sections[0]))
        else:
            sections, planes = make_sections(sh, plan, f, edges, ())
            columns = make_columns(sh, plan, f, edges)
        sections = [sections[0]] + [
            shifted(sections[by], "gy", by) for by in range(1, sh.tiles)
        ]
        filt, loads, forces = do_markers(
            sh,
            step,
            plan,
            tables,
            (area, speed),
            blades,
            filt,
            columns,
            [in_vmem(section) for section in sections],
        )
        forces = [forces[0]] + [shifted(forces[by], "gy", by) for by in range(1, sh.tiles)]
        forces = [in_vmem(force) for force in forces]
        bulk = do_bulk(sh, last, plan, f, edges, loads, filt)
        if last:
            loads_out, filt_out = bulk[1:]
        bulk = in_vmem(bulk[0])
        sent = make_edges(sh, plan, f, edges, forces, bulk)
        done = do_patch(sh, last, plan, planes, forces, bulk)
        edges = exchange(*sent)
        f = in_vmem(done[0])
    f = finish(sh, f, done[1], edges)
    loads_out, filt_out = [
        jnp.swapaxes(by_slot(sh, x), 0, 1)[None, None] for x in (loads_out, filt_out)
    ]
    return f, loads_out, filt_out


def solution(mesh):
    in_specs = (
        P(None, None, "gx", "gy"),
        P(),
        P(),
        P(),
        P("gx", "gy", None, None),
        P("gx", "gy", None, None),
        P("gx", "gy", None, None),
        P("gx", "gy", None, None),
        P("gx", "gy", None, None, None),
    )
    out_specs = (
        P(None, None, "gx", "gy"),
        P("gx", "gy", None, None, None),
        P("gx", "gy", None, None, None),
    )
    return jax.shard_map(local, mesh=mesh, in_specs=in_specs, out_specs=out_specs, check_vma=False)
```

```python
import math

import jax
import jax.numpy as jnp
from jax import lax
from jax.experimental import pallas as pl
from jax.experimental.pallas import tpu as pltpu
from jax.sharding import PartitionSpec as P

PHASES = 64
PAIRS = [
    (1, 0, 0),
    (0, 1, 0),
    (0, 0, 1),
    (1, 1, 0),
    (1, -1, 0),
    (1, 0, 1),
    (1, 0, -1),
    (0, 1, 1),
    (0, 1, -1),
]
DIRS = [(0, 0, 0)]
for along in PAIRS:
    DIRS.append(along)
    DIRS.append(tuple(-part for part in along))
OPPOSITE = [0] + [q + 1 if q % 2 else q - 1 for q in range(1, 19)]
PLUS = [q for q in range(19) if DIRS[q][0] == 1]
MINUS = [q for q in range(19) if DIRS[q][0] == -1]
SIDEWAYS = [q for q in range(19) if DIRS[q][1] != 0]
OMEGA = 1.0 / 0.6
KEEP = 1.0 - OMEGA
GUO = 1.0 - 0.5 * OMEGA
SPREAD = 0.01
MIX = 0.5
PITCH_AMP = 0.2
LANES = 128
F32 = jnp.float32
BF16 = jnp.bfloat16
VMEM_LIMIT = 8 * 1024 * 1024


def iota(shape, axis):
    return lax.broadcasted_iota(jnp.int32, shape, axis)


def aligned(value, by):
    return value if isinstance(value, int) else pl.multiple_of(value, by)


def wrapped(value):
    return value % LANES if isinstance(value, int) else lax.rem(value, LANES)


def moments(f):
    sums = [f[2 * k + 1] + f[2 * k + 2] for k in range(9)]
    gaps = [f[2 * k + 1] - f[2 * k + 2] for k in range(9)]
    density = f[0]
    for part in sums:
        density = density + part
    momentum = []
    for axis in range(3):
        total = None
        for k in range(9):
            sign = PAIRS[k][axis]
            if sign == 0:
                continue
            if total is None:
                total = gaps[k]
            else:
                total = total + gaps[k] if sign > 0 else total - gaps[k]
        momentum.append(total)
    return density, momentum


def collide(f, force, wanted):
    density, momentum = moments(f)
    inverse = 1.0 / density
    relaxed = OMEGA * density
    if force is None:
        v = [momentum[a] * inverse for a in range(3)]
        square = v[0] * v[0] + v[1] * v[1] + v[2] * v[2]
        base = relaxed * (1.0 - 1.5 * square)
        drive = [OMEGA * momentum[a] for a in range(3)]
        bend = [4.5 * part for part in drive]
    else:
        v = [(momentum[a] + 0.5 * force[a]) * inverse for a in range(3)]
        square = v[0] * v[0] + v[1] * v[1] + v[2] * v[2]
        work = v[0] * force[0] + v[1] * force[1] + v[2] * force[2]
        base = relaxed * (1.0 - 1.5 * square) - (3.0 * GUO) * work
        drive = [relaxed * v[a] + GUO * force[a] for a in range(3)]
        bend = [(4.5 * relaxed) * v[a] + (9.0 * GUO) * force[a] for a in range(3)]
    post = {}
    if 0 in wanted:
        post[0] = KEEP * f[0] + base * (1.0 / 3.0)
    scaled = {}
    for weight in (18.0, 36.0):
        scaled[weight] = (
            base * (1.0 / weight),
            [part * (3.0 / weight) for part in drive],
            [part * (1.0 / weight) for part in bend],
        )

    def along(k, parts):
        total = None
        for axis in range(3):
            sign = PAIRS[k][axis]
            if sign == 0:
                continue
            if total is None:
                total = parts[axis]
            else:
                total = total + parts[axis] if sign > 0 else total - parts[axis]
        return total

    for k in range(9):
        if 2 * k + 1 not in wanted and 2 * k + 2 not in wanted:
            continue
        level, drives, bends = scaled[18.0 if k < 3 else 36.0]
        even = level + along(k, v) * along(k, bends)
        odd = along(k, drives)
        if 2 * k + 1 in wanted:
            post[2 * k + 1] = KEEP * f[2 * k + 1] + (even + odd)
        if 2 * k + 2 in wanted:
            post[2 * k + 2] = KEEP * f[2 * k + 2] + (even - odd)
    return post


def outside(q, levels, rows):
    if DIRS[q][2] == 1:
        return rows == 0
    if DIRS[q][2] == -1:
        return rows == levels - 1
    return None


class Shape:
    def __init__(self, f_in, rotor_place, marker_cell, pitch_phase, filt_in):
        self.levels = f_in.shape[1]
        self.xs = f_in.shape[2]
        self.rotors = rotor_place.shape[0]
        self.steps = pitch_phase.shape[1]
        self.markers = marker_cell.shape[1]
        self.slots = filt_in.shape[2]
        self.tiles = lax.axis_size("gy")
        self.groups = self.markers // LANES
        self.section = self.slots * 3 * self.levels


def in_vmem(x):
    return pltpu.with_memory_space_constraint(x, pltpu.VMEM)


def in_hbm(x):
    return pltpu.with_memory_space_constraint(x, pltpu.HBM)


def in_smem(x):
    return pltpu.with_memory_space_constraint(x, pltpu.SMEM)


VM = pl.BlockSpec(memory_space=pltpu.VMEM)
SM = pl.BlockSpec(memory_space=pltpu.SMEM)
HB = pl.BlockSpec(memory_space=pl.ANY)
PARAMS = pltpu.CompilerParams(vmem_limit_bytes=VMEM_LIMIT)


def write_plan(sh, place, plan):
    row = lax.axis_index("gx")
    shape = (sh.tiles, sh.rotors)
    mine = jnp.logical_and(place[2:3, :] == iota(shape, 0), place[0:1, :] == row)
    keys = iota(shape, 1) * sh.xs + place[1:2, :]
    none = sh.rotors * sh.xs
    last = jnp.full((sh.tiles, 1), -1, jnp.int32)
    for slot in range(sh.slots):
        left = jnp.logical_and(mine, keys > last)
        last = jnp.min(jnp.where(left, keys, none), axis=1, keepdims=True)
        for owner in range(sh.tiles):
            key = last[owner, 0]
            plan[owner * sh.slots + slot] = jnp.where(key < none, key, -1)


def plane_at(sh, plan, owner, slot):
    key = plan[owner * sh.slots + slot]
    return jnp.where(key < 0, -1, lax.rem(key, sh.xs))


def rotor_at(sh, plan, slot):
    key = plan[lax.axis_index("gy") * sh.slots + slot]
    return jnp.where(key < 0, -1, lax.div(key, sh.xs))


def plane_of(sh, f, x, low, high):
    rows = iota((sh.levels, LANES), 0)
    planes = []
    for q in range(19):
        value = f[q, pl.ds(x, sh.levels, stride=sh.xs), :]
        if low is not None and DIRS[q][0] != 0:
            if DIRS[q][0] == 1:
                other, at = low[PLUS.index(q)], 0
            else:
                other, at = high[MINUS.index(q)], sh.xs - 1
            here = jnp.asarray(x == at)
            skip = outside(q, sh.levels, rows)
            use = here if skip is None else jnp.logical_and(here, jnp.logical_not(skip))
            value = jnp.where(use, other, value)
        planes.append(value)
    return planes


def write_sections(sh, plan, f, low, high, outs, held):
    me = lax.axis_index("gy")
    for shift in range(sh.tiles):
        owner = lax.rem(me + shift, sh.tiles)
        for slot in range(sh.slots):
            x = plane_at(sh, plan, owner, slot)

            @pl.when(x >= 0)
            def _():
                planes = plane_of(sh, f, x, low, high)
                for q, value in enumerate(planes):
                    held[owner * sh.slots + slot, q] = value
                density, momentum = moments(planes)
                inverse = 1.0 / density
                for axis in range(3):
                    at = (slot * 3 + axis) * sh.levels
                    outs[shift][at : at + sh.levels, :] = momentum[axis] * inverse

            @pl.when(x < 0)
            def _():
                at = slot * 3 * sh.levels
                outs[shift][at : at + 3 * sh.levels, :] = jnp.zeros((3 * sh.levels, LANES), F32)


def sincos(x):
    turns = jnp.floor(x * (2.0 / math.pi) + 0.5)
    r = x - turns * 1.5703125
    r = r - turns * 4.837512969970703125e-4
    r = r - turns * 7.549789954891882e-8
    r2 = r * r
    sin_r = r + r * r2 * (
        -1.0 / 6 + r2 * (1.0 / 120 + r2 * (-1.0 / 5040 + r2 * (1.0 / 362880)))
    )
    cos_r = (
        1.0
        - 0.5 * r2
        + r2
        * r2
        * (1.0 / 24 + r2 * (-1.0 / 720 + r2 * (1.0 / 40320 - r2 * (1.0 / 3628800))))
    )
    quarter = turns.astype(jnp.int32)
    swap = (quarter & 1) == 1
    sin_x = jnp.where(swap, cos_r, sin_r)
    cos_x = jnp.where(swap, sin_r, cos_r)
    sin_x = jnp.where((quarter & 2) == 2, -sin_x, sin_x)
    cos_x = jnp.where(((quarter + 1) & 2) == 2, -cos_x, cos_x)
    return sin_x, cos_x


def write_blades(sh, plan, phases, twist, angle, blades):
    blades[0], blades[1] = sincos(angle[...])
    sin_twist, cos_twist = sincos(twist[...])
    owner = iota((1, LANES), 1)
    rows = iota((sh.slots * sh.groups, LANES), 0) % sh.slots
    phase = jnp.zeros((1, LANES), F32)
    for step in range(sh.steps):
        for slot in range(sh.slots):
            rotor = jnp.maximum(rotor_at(sh, plan, slot), 0)
            here = owner == step * sh.slots + slot
            phase = jnp.where(here, phases[step, rotor].astype(F32), phase)
    pitch = PITCH_AMP * sincos((2.0 * math.pi / PHASES) * phase)[0]
    pitched = sincos(pitch)
    for step in range(sh.steps):
        parts = []
        for part in pitched:
            total = jnp.zeros((sh.slots * sh.groups, LANES), F32)
            for slot in range(sh.slots):
                lane = step * sh.slots + slot
                total = jnp.where(rows == slot, part[:, lane : lane + 1], total)
            parts.append(total)
        blades[2 + 2 * step] = sin_twist * parts[1] + cos_twist * parts[0]
        blades[3 + 2 * step] = cos_twist * parts[1] - sin_twist * parts[0]


def start_kernel(
    sh, place_in, phases_in, twist_in, angle_in, f_in, plan, blades, f, place, phases, twist, angle, sems
):
    pairs = ((place_in, place), (phases_in, phases), (angle_in, angle), (twist_in, twist))
    copies = [pltpu.make_async_copy(*pair, sems.at[k]) for k, pair in enumerate(pairs)]
    whole = pltpu.make_async_copy(f_in, f, sems.at[4])
    for copy in copies:
        copy.start()
    whole.start()
    for copy in copies:
        copy.wait()
    write_plan(sh, place, plan)
    write_blades(sh, plan, phases, twist, angle, blades)
    whole.wait()


def start(sh, rotor_place, phases, twist, angle, f_in):
    rows = sh.slots * sh.groups
    plan, blades, f = pl.pallas_call(
        lambda *refs: start_kernel(sh, *refs),
        out_shape=[
            pltpu.SMEM((sh.tiles * sh.slots,), jnp.int32),
            pltpu.VMEM((2 + 2 * sh.steps, rows, LANES), F32),
            pltpu.VMEM((19, sh.levels * sh.xs, LANES), F32),
        ],
        in_specs=[HB] * 5,
        out_specs=[SM, VM, VM],
        scratch_shapes=[
            pltpu.VMEM((3, sh.rotors), jnp.int32),
            pltpu.SMEM((sh.steps, sh.rotors), jnp.int32),
            pltpu.VMEM((rows, LANES), F32),
            pltpu.VMEM((rows, LANES), F32),
            pltpu.SemaphoreType.DMA((5,)),
        ],
        compiler_params=PARAMS,
        name="start",
    )(
        in_hbm(jnp.transpose(rotor_place)),
        in_hbm(jnp.transpose(phases)),
        in_hbm(twist),
        in_hbm(angle),
        in_hbm(f_in.reshape(19, sh.levels * sh.xs, LANES)),
    )
    return in_smem(plan), in_vmem(blades), in_vmem(f)


def section_kernel(sh, has_edges, plan, f, *refs):
    low, high = refs[:2] if has_edges else (None, None)
    write_sections(sh, plan, f, low, high, refs[-sh.tiles - 1 : -1], refs[-1])


def make_sections(sh, plan, f, edges, after):
    out = pl.pallas_call(
        lambda *refs: section_kernel(sh, bool(edges), *refs),
        out_shape=[pltpu.VMEM((sh.section, LANES), F32)] * sh.tiles
        + [pltpu.VMEM((sh.tiles * sh.slots, 19, sh.levels, LANES), F32)],
        in_specs=[SM] + [VM] * (1 + len(edges) + len(after)),
        out_specs=[VM] * (sh.tiles + 1),
        compiler_params=PARAMS,
        name="sections",
    )(plan, f, *edges, *after)
    return out[:-1], in_vmem(out[-1])


def column_kernel(sh, has_edges, *refs):
    f = refs[1]
    low, high = refs[2:4] if has_edges else (None, None)
    east, west = refs[-2:]
    packed = []
    pairs = iota((sh.xs, LANES), 1) // 2
    xrows = iota((sh.xs, LANES), 0)
    per = LANES // (2 * sh.levels)
    groups = (19 + per - 1) // per
    for group in range(groups):
        total = jnp.ones((sh.xs, LANES), F32)
        for q in range(group * per, min(19, (group + 1) * per)):
            for z in range(sh.levels):
                tile = f[q, z * sh.xs : (z + 1) * sh.xs, :]
                if has_edges and DIRS[q][0] != 0:
                    blocked = (DIRS[q][2] == 1 and z == 0) or (
                        DIRS[q][2] == -1 and z == sh.levels - 1
                    )
                    if not blocked:
                        if DIRS[q][0] == 1:
                            tile = jnp.where(xrows == 0, low[PLUS.index(q), z : z + 1, :], tile)
                        else:
                            tile = jnp.where(
                                xrows == sh.xs - 1, high[MINUS.index(q), z : z + 1, :], tile
                            )
                pair = (q % per) * sh.levels + z
                total = jnp.where(
                    pairs == pair, pltpu.roll(tile, (2 * pair + 1) % LANES, 1), total
                )
        packed.append(total)
    zpairs = iota((sh.levels, LANES), 1) // 2
    corners = jnp.ones((sh.levels, LANES), F32)
    for which, x in ((0, 0), (1, sh.xs - 1)):
        planes = plane_of(sh, f, x, low, high)
        for q in range(19):
            pair = 2 * q + which
            corners = jnp.where(zpairs == pair, pltpu.roll(planes[q], 2 * pair + 1, 1), corners)
    packed.append(corners)
    even = iota((sh.xs, LANES), 1) % 2 == 0
    for k in range(len(packed) // 2):
        first, second = packed[2 * k], packed[2 * k + 1]
        rows = slice(k * sh.xs, (k + 1) * sh.xs)
        east[rows, :] = jnp.where(even, first, pltpu.roll(second, 1, 1))
        west[rows, :] = jnp.where(even, pltpu.roll(first, LANES - 1, 1), second)


def packed_columns(sh):
    per = LANES // (2 * sh.levels)
    return (19 + per - 1) // per + 1


def unpack_columns(sh, left, right, first):
    even = iota((sh.xs, LANES), 1) % 2 == 0
    groups = []
    for k in range(packed_columns(sh) // 2):
        rows = pl.ds(first + k * sh.xs, sh.xs)
        a, b = left[rows, :], right[rows, :]
        groups.append(jnp.where(even, a, pltpu.roll(b, 1, 1)))
        groups.append(jnp.where(even, pltpu.roll(a, LANES - 1, 1), b))
    return groups


def make_columns(sh, plan, f, edges):
    shape = (packed_columns(sh) // 2 * sh.xs, LANES)
    out = pl.pallas_call(
        lambda *refs: column_kernel(sh, bool(edges), *refs),
        out_shape=[pltpu.VMEM(shape, F32)] * 2,
        in_specs=[SM] + [VM] * (1 + len(edges)),
        out_specs=[VM] * 2,
        compiler_params=PARAMS,
        name="columns",
    )(plan, f, *edges)
    return [in_vmem(x) for x in out]


def peskin(offsets):
    distance = jnp.abs(offsets)
    near_arg = jnp.maximum(1.0 + 4.0 * distance - 4.0 * distance * distance, 1.0)
    far_arg = jnp.maximum(-7.0 + 12.0 * distance - 4.0 * distance * distance, 1.0)
    near = distance <= 1.0
    root = jnp.sqrt(jnp.where(near, near_arg, far_arg))
    return (jnp.where(near, 3.0, 5.0) - 2.0 * distance + jnp.where(near, root, -root)) * 0.125


TABLE_CHUNK = 1024


def table_kernel(sh, plan, cells, after, across, upward, info, codes, lines, sem):
    del after
    ids = [rotor_at(sh, plan, slot) for slot in range(sh.slots)]
    copies = []
    for slot in range(sh.slots):
        first = pl.multiple_of(jnp.maximum(ids[slot], 0) // 8 * 8, 8)
        copy = pltpu.make_async_copy(cells.at[pl.ds(first, 8), :], codes.at[slot], sem.at[slot])
        copy.start()
        copies.append(copy)
    width = min(TABLE_CHUNK, sh.markers)
    part = iota((8, width), 0)
    spanwise = part < 4
    cell_bits = 6 + sh.levels.bit_length() - 1
    quarter = LANES // 4
    packed = 16
    ycells = [
        (iota((packed, LANES), 0) + first).astype(F32).astype(BF16)
        for first in range(0, quarter, packed)
    ]
    zcells = iota((sh.levels, LANES), 0)
    for slot in range(sh.slots):
        copies[slot].wait()

        @pl.when(ids[slot] >= 0)
        def _():
            line = ids[slot] % 8
            every = codes[slot, pl.ds(line, 1), :] >> cell_bits
            lowest = jnp.min(every)
            highest = jnp.max(every)
            narrow = highest - lowest + 4 <= LANES
            start = jnp.where(narrow, lowest, lowest // LANES * LANES)
            info[2 * slot] = start
            info[2 * slot + 1] = jnp.where(narrow, 1, 2)

            def chunk(window, at):
                code = codes[slot, pl.ds(line, 1), pl.ds(at, width)]
                cells = (code >> cell_bits) - (start + window * LANES)
                levels = (code >> 6) & (sh.levels - 1)
                eighths = jnp.where(spanwise, code >> 3, code) & 7
                corner = jnp.where(spanwise, (part - cells) & 3, part - 4)
                weights = peskin(corner.astype(F32) - 1.0 - eighths.astype(F32) * 0.125)
                places = ((cells + corner - part) >> 2).astype(F32)
                top = weights.astype(BF16).astype(F32)
                rest = weights - top
                lines[0] = places
                lines[1] = top
                lines[2] = rest
                lines[3] = weights
                for group in range(width // LANES):
                    lanes = slice(group * LANES, (group + 1) * LANES)
                    to = pl.ds(at + group * LANES, LANES)
                    tall = jnp.zeros((sh.levels, LANES), F32)
                    for j in range(4):
                        tall = jnp.where(
                            zcells == levels[:, lanes] + j, lines[3, 4 + j : 5 + j, lanes], tall
                        )
                    upward[slot, :, to] = tall

                    def spread_line(k, kind):
                        line = lines[k, kind : kind + 1, lanes]
                        return jnp.broadcast_to(line, (packed, LANES)).astype(BF16)

                    for kind in range(4):
                        spot, high, low = [spread_line(k, kind) for k in range(3)]
                        for k, cell in enumerate(ycells):
                            here = cell == spot
                            for half, source in ((0, high), (1, low)):
                                row = half * LANES + kind * quarter + k * packed
                                across[slot, window, row : row + packed, to] = jnp.where(
                                    here, source, jnp.zeros((), BF16)
                                )

            def sweep(window):
                def body(i, carry):
                    chunk(window, pl.multiple_of(i * width, width))
                    return carry

                lax.fori_loop(0, sh.markers // width, body, 0)

            sweep(0)

            @pl.when(jnp.logical_not(narrow))
            def _():
                sweep(1)


def make_tables(sh, plan, marker_cell, after):
    across, upward, info = pl.pallas_call(
        lambda *refs: table_kernel(sh, *refs),
        out_shape=[
            pltpu.VMEM((sh.slots, 2, 2 * LANES, sh.markers), BF16),
            pltpu.VMEM((sh.slots, sh.levels, sh.markers), F32),
            pltpu.SMEM((2 * sh.slots,), jnp.int32),
        ],
        in_specs=[SM, HB, VM],
        out_specs=[VM, VM, SM],
        scratch_shapes=[
            pltpu.VMEM((sh.slots, 8, sh.markers), jnp.int32),
            pltpu.VMEM((4, 8, min(TABLE_CHUNK, sh.markers)), F32),
            pltpu.SemaphoreType.DMA((sh.slots,)),
        ],
        compiler_params=PARAMS,
        name="tables",
    )(plan, marker_cell, after)
    return in_vmem(across), in_vmem(upward), in_smem(info)


GHOST_LANES = 32
SAMPLE_CHUNK = 8192
SPREAD_CHUNK = 8192


def split(value):
    top = value.astype(BF16)
    return top, (value - top.astype(F32)).astype(BF16)


def marker_kernel(
    sh, step, plan, info, across, upward, area, speed, blades, filt_old, east, west, *refs
):
    sections = refs[: sh.tiles]
    filt_new, loads = refs[sh.tiles : sh.tiles + 2]
    forces = refs[sh.tiles + 2 : 2 * sh.tiles + 2]
    around, sampled, weighted, spread, turning = refs[2 * sh.tiles + 2 :]
    me = lax.axis_index("gy")
    tall = 3 * sh.levels
    quarter = LANES // 4
    rows = iota((LANES, LANES), 0)
    kinds = iota((LANES, LANES), 1)
    by_class = (rows == kinds % quarter * 4 + kinds // quarter).astype(F32).astype(BF16)
    from_class = (kinds == rows % quarter * 4 + rows // quarter).astype(F32).astype(BF16)
    for shift in range(sh.tiles):
        around[lax.rem(me + sh.tiles - shift, sh.tiles)] = sections[shift][...]
    spread[...] = jnp.zeros(spread.shape, F32)

    def window_of(slot, window):
        start = info[2 * slot] + window * LANES
        tile = start // LANES
        return tile, jnp.minimum(tile + 1, sh.tiles - 1), start - tile * LANES

    def windows(slot, body):
        @pl.when(rotor_at(sh, plan, slot) >= 0)
        def _():
            body(0)

            @pl.when(info[2 * slot + 1] > 1)
            def _():
                body(1)

    for slot in range(sh.slots):
        rows = pl.ds(slot * tall, tall)

        def sample(window):
            tile, after, offset = window_of(slot, window)
            both = jnp.concatenate([around[tile, rows, :], around[after, rows, :]], axis=1)
            seen = pltpu.roll(both, lax.rem(2 * LANES - offset, 2 * LANES), 1)[:, :LANES]
            top, rest = split(seen)
            left = jnp.concatenate([top, rest], axis=0)
            left = jnp.dot(left, by_class, preferred_element_type=F32).astype(BF16)
            left = jnp.concatenate([left, left], axis=1)

            def chunk(i, carry):
                at = pl.multiple_of(i * SAMPLE_CHUNK, SAMPLE_CHUNK)
                value = jnp.dot(
                    left,
                    across[slot, window, :, pl.ds(at, SAMPLE_CHUNK)],
                    preferred_element_type=F32,
                )
                value = value[:tall] + value[tall:]
                heights = upward[slot, :, pl.ds(at, SAMPLE_CHUNK)]
                for axis in range(3):
                    part = jnp.sum(
                        value[axis * sh.levels : (axis + 1) * sh.levels] * heights,
                        axis=0,
                        keepdims=True,
                    )
                    for group in range(SAMPLE_CHUNK // LANES):
                        row = (i * (SAMPLE_CHUNK // LANES) + group) * sh.slots + slot
                        piece = part[:, group * LANES : (group + 1) * LANES]
                        if window:
                            piece = piece + sampled[axis, pl.ds(row, 1), :]
                        sampled[axis, pl.ds(row, 1), :] = piece
                return carry

            lax.fori_loop(0, sh.markers // SAMPLE_CHUNK, chunk, 0)

        windows(slot, sample)

    felt = []
    for axis in range(3):
        old = filt_old[axis]
        value = old + MIX * (sampled[axis] - old)
        filt_new[axis] = value
        felt.append(value)
    sin_t = blades[0]
    cos_t = blades[1]
    tangent = speed[...] + sin_t * felt[1] - cos_t * felt[2]
    square = felt[0] * felt[0] + tangent * tangent
    inverse = 1.0 / jnp.sqrt(square)
    sin_p = felt[0] * inverse
    cos_p = tangent * inverse
    sin_b = blades[2 + 2 * step]
    cos_b = blades[3 + 2 * step]
    sin_a = sin_p * cos_b - cos_p * sin_b
    cos_a = cos_p * cos_b + sin_p * sin_b
    lift = (2.0 * math.pi) * sin_a * cos_a
    drag = 0.02 + sin_a * sin_a
    dynamic = 0.5 * area[...] * square
    around_axis = dynamic * (lift * sin_p - drag * cos_p)
    loads[0] = dynamic * (lift * cos_p + drag * sin_p)
    loads[1] = -around_axis * sin_t
    loads[2] = around_axis * cos_t

    for slot in range(sh.slots):
        rows = pl.ds(slot * tall, tall)

        def spread_out(window):
            tile, after, offset = window_of(slot, window)

            def chunk(i, total):
                at = pl.multiple_of(i * SPREAD_CHUNK, SPREAD_CHUNK)
                for group in range(SPREAD_CHUNK // LANES):
                    heights = upward[slot, :, pl.ds(at + group * LANES, LANES)]
                    row = (i * (SPREAD_CHUNK // LANES) + group) * sh.slots + slot
                    parts = [heights * loads[axis, pl.ds(row, 1), :] for axis in range(3)]
                    top, rest = split(jnp.concatenate(parts, axis=0))
                    weighted[:tall, group * LANES : (group + 1) * LANES] = top
                    weighted[tall:, group * LANES : (group + 1) * LANES] = rest
                return total + lax.dot_general(
                    across[slot, window, :, pl.ds(at, SPREAD_CHUNK)],
                    weighted[...],
                    (((1,), (1,)), ((), ())),
                    preferred_element_type=F32,
                )

            total = lax.fori_loop(
                0,
                sh.markers // SPREAD_CHUNK,
                chunk,
                jnp.zeros((2 * LANES, 2 * tall), F32),
            )
            total = jnp.transpose(total)
            total = total[:tall] + total[tall:]
            total = -SPREAD * (total[:, :LANES] + total[:, LANES:])
            pieces = []
            for _ in range(3):
                pieces.append(total.astype(BF16))
                total = total - pieces[-1].astype(F32)
            pieces = jnp.dot(
                jnp.concatenate(pieces, axis=0), from_class, preferred_element_type=F32
            )
            total = pieces[:tall] + pieces[tall : 2 * tall] + pieces[2 * tall :]
            both = jnp.concatenate([total, jnp.zeros((tall, LANES), F32)], axis=1)
            both = pltpu.roll(both, offset, 1)
            spread[tile, rows, :] = spread[tile, rows, :] + both[:, :LANES]
            spread[after, rows, :] = spread[after, rows, :] + both[:, LANES:]

        windows(slot, spread_out)

    lanes = iota((sh.levels, LANES), 1)
    for shift in range(sh.tiles):
        tile = lax.rem(me + shift, sh.tiles)
        forces[shift][: sh.section, :] = spread[tile]
        before = lax.rem(tile + sh.tiles - 1, sh.tiles)
        after = lax.rem(tile + 1, sh.tiles)
        beyond = [jnp.zeros((sh.levels, LANES), F32)] * 2
        for k in range(3 * sh.slots):
            at = pl.ds(k * sh.levels, sh.levels)
            left = jnp.broadcast_to(spread[before, at, :][:, LANES - 1 :], (sh.levels, LANES))
            right = jnp.broadcast_to(spread[after, at, :][:, :1], (sh.levels, LANES))
            beyond[0] = jnp.where(lanes == k, left, beyond[0])
            beyond[1] = jnp.where(lanes == k, right, beyond[1])
        at = shift * GHOST_LANES
        for side in range(2):
            turning[pl.ds(at + side, sh.levels, stride=2), :] = beyond[side]
        forces[shift][sh.section + 8 : sh.section + 8 + sh.levels, :] = jnp.where(
            lanes < 8, beyond[0], pltpu.roll(beyond[1], 8, 1)
        )
    each = LANES // GHOST_LANES
    for first in range(0, sh.tiles, each):
        rows = jnp.transpose(turning[first * GHOST_LANES : (first + each) * GHOST_LANES, :])[:8]
        for k in range(each):
            forces[first + k][sh.section : sh.section + 8, :] = pltpu.roll(
                rows, (LANES - k * GHOST_LANES) % LANES, 1
            )
    forces[1][sh.section + 8 + sh.levels :, :] = east[...]
    forces[sh.tiles - 1][sh.section + 8 + sh.levels :, :] = west[...]


def do_markers(sh, step, plan, tables, fixed, blades, filt, columns, sections):
    across, upward, info = tables
    rows = sh.slots * sh.groups
    dense = pltpu.VMEM((3, rows, LANES), F32)
    plain = sh.section + 8 + sh.levels
    extra = columns[0].shape[0]
    forces = [
        pltpu.VMEM((plain + (extra if by in (1, sh.tiles - 1) else 0), LANES), F32)
        for by in range(sh.tiles)
    ]
    out = pl.pallas_call(
        lambda *refs: marker_kernel(sh, step, *refs),
        out_shape=[dense, dense] + forces,
        in_specs=[SM, SM] + [VM] * (8 + sh.tiles),
        out_specs=[VM] * (2 + sh.tiles),
        scratch_shapes=[
            pltpu.VMEM((sh.tiles, sh.section, LANES), F32),
            pltpu.VMEM((3, rows, LANES), F32),
            pltpu.VMEM((6 * sh.levels, SPREAD_CHUNK), BF16),
            pltpu.VMEM((sh.tiles, sh.section, LANES), F32),
            pltpu.VMEM((sh.tiles * GHOST_LANES, LANES), F32),
        ],
        compiler_params=PARAMS,
        name="markers",
    )(plan, info, across, upward, *fixed, blades, filt, *columns, *sections)
    return in_vmem(out[0]), in_vmem(out[1]), out[2:]


def edge_kernel(sh, has_edges, plan, f, *refs):
    low, high = refs[:2] if has_edges else (None, None)
    refs = refs[2 * has_edges :]
    forces = refs[: sh.tiles]
    outs = refs[sh.tiles + 1 :]
    me = lax.axis_index("gy")
    lanes = iota((sh.levels, LANES), 1)
    blank = jnp.zeros((sh.levels, LANES), F32)
    planes_at = (0, sh.xs - 1)
    beyond = unpack_columns(sh, forces[1], forces[sh.tiles - 1], sh.section + 8 + sh.levels)[-1]
    corner = [pltpu.roll(beyond, (LANES - 4 * q) % LANES, 1) for q in range(19)]
    corner_force = [blank, blank, blank]
    edge_force = [[blank, blank, blank], [blank, blank, blank]]
    for shift in range(sh.tiles):
        owner = lax.rem(me + sh.tiles - shift, sh.tiles)
        ghosts = forces[shift][sh.section + 8 : sh.section + 8 + sh.levels, :]
        for slot in range(sh.slots):
            x = plane_at(sh, plan, owner, slot)
            for axis in range(3):
                k = slot * 3 + axis
                piece = forces[shift][k * sh.levels : (k + 1) * sh.levels, :]
                for which in range(2):
                    here = jnp.asarray(x == planes_at[which])
                    edge_force[which][axis] = edge_force[which][axis] + jnp.where(here, piece, 0.0)
                    for side in range(2):
                        lane = 2 * which + side
                        moved = pltpu.roll(ghosts, (lane - side * 8 - k) % LANES, 1)
                        corner_force[axis] = corner_force[axis] + jnp.where(
                            jnp.logical_and(here, lanes == lane), moved, 0.0
                        )
    corner_post = collide(corner, corner_force, [q for q in PLUS + MINUS if DIRS[q][1]])
    leaving = ([], [])
    for which, wanted in ((1, PLUS), (0, MINUS)):
        planes = plane_of(sh, f, planes_at[which], low, high)
        post = collide(planes, edge_force[which], wanted)
        for k, q in enumerate(wanted):
            value = post[q]
            if DIRS[q][1] == 1:
                value = pltpu.roll(value, 1, 1)
                ghost = pltpu.roll(corner_post[q], (LANES - 2 * which) % LANES, 1)
                value = jnp.where(lanes == 0, ghost, value)
            elif DIRS[q][1] == -1:
                value = pltpu.roll(value, LANES - 1, 1)
                ghost = pltpu.roll(corner_post[q], LANES - 2 - 2 * which, 1)
                value = jnp.where(lanes == LANES - 1, ghost, value)
            if DIRS[q][2]:
                value = pltpu.roll(value, DIRS[q][2] % sh.levels, 0)
            leaving[which].append(value)
    for k, (down, up) in enumerate(zip(*leaving)):
        outs[0][k] = up
        outs[1][k] = down


def make_edges(sh, plan, f, edges, forces, after):
    return pl.pallas_call(
        lambda *refs: edge_kernel(sh, bool(edges), *refs),
        out_shape=[pltpu.VMEM((len(PLUS), sh.levels, LANES), F32)] * 2,
        in_specs=[SM] + [VM] * (2 + len(edges) + sh.tiles),
        out_specs=[VM] * 2,
        compiler_params=PARAMS,
        name="edges",
    )(plan, f, *edges, *forces, after)


def bulk_kernel(sh, has_edges, last, plan, f, *refs):
    low, high = refs[:2] if has_edges else (None, None)
    refs = refs[2 * has_edges :]
    loads, filt, out = refs[:3]
    xs = sh.xs
    xrows = iota((xs, LANES), 0)
    copies = []
    if last:
        masked, sems = refs[-2:]
        rows = iota((sh.slots * sh.groups, LANES), 0) % sh.slots
        used = jnp.zeros((sh.slots * sh.groups, LANES), jnp.int32)
        for slot in range(sh.slots):
            there = (rotor_at(sh, plan, slot) >= 0).astype(jnp.int32)
            used = jnp.where(rows == slot, there, used)
        for k, source in enumerate((loads, filt)):
            for axis in range(3):
                masked[k, axis] = jnp.where(used > 0, source[axis], 0.0)
            copy = pltpu.make_async_copy(masked.at[k], refs[3 + k], sems.at[k])
            copy.start()
            copies.append(copy)

    def level(z, bottom, top):
        at = aligned(z * xs, xs)
        here = []
        for q in range(19):
            tile = f[q, pl.ds(at, xs), :]
            if has_edges and DIRS[q][0] != 0:
                blocked = (DIRS[q][2] == 1 and bottom) or (DIRS[q][2] == -1 and top)
                if not blocked:
                    if DIRS[q][0] == 1:
                        tile = jnp.where(xrows == 0, low[PLUS.index(q), pl.ds(z, 1), :], tile)
                    else:
                        tile = jnp.where(
                            xrows == xs - 1, high[MINUS.index(q), pl.ds(z, 1), :], tile
                        )
            here.append(tile)
        post = collide(here, None, range(19))
        for q in range(19):
            dx, dy, dz = DIRS[q]
            value = post[q]
            if (dz == 1 and top) or (dz == -1 and bottom):
                to, target = OPPOSITE[q], z
            else:
                to, target = q, z + dz
                if dy:
                    value = pltpu.roll(value, dy % LANES, 1)
                if dx:
                    value = pltpu.roll(value, dx % xs, 0)
            out[to, pl.ds(aligned(target * xs, xs), xs), :] = value

    level(0, True, False)

    def middle(z, carry):
        level(z, False, False)
        return carry

    lax.fori_loop(1, sh.levels - 1, middle, 0)
    level(sh.levels - 1, False, True)
    for copy in copies:
        copy.wait()


def do_bulk(sh, last, plan, f, edges, loads, filt):
    out_shape = [pltpu.VMEM((19, sh.levels * sh.xs, LANES), F32)]
    scratch = []
    if last:
        out_shape += [jax.ShapeDtypeStruct(loads.shape, F32)] * 2
        scratch = [pltpu.VMEM((2, *loads.shape), F32), pltpu.SemaphoreType.DMA((2,))]
    return pl.pallas_call(
        lambda *refs: bulk_kernel(sh, bool(edges), last, *refs),
        out_shape=out_shape,
        in_specs=[SM] + [VM] * (3 + len(edges)),
        out_specs=[VM] + [HB] * (len(out_shape) - 1),
        scratch_shapes=scratch,
        compiler_params=PARAMS,
        name="bulk",
    )(plan, f, *edges, loads, filt)


def patch_kernel(sh, last, plan, planes, *refs):
    forces = refs[: sh.tiles]
    out = refs[sh.tiles + 1]
    sems = refs[-1]
    me = lax.axis_index("gy")
    xs = sh.xs
    lanes = iota((xs, LANES), 1)
    xrows = iota((xs, LANES), 0)
    per = LANES // (2 * sh.levels)
    copies = []

    def send(q):
        if last:
            copy = pltpu.make_async_copy(out.at[q], refs[sh.tiles + 2].at[q], sems.at[q])
            copy.start()
            copies.append(copy)

    rotors = []
    for shift in range(sh.tiles):
        owner = lax.rem(me + sh.tiles - shift, sh.tiles)
        for slot in range(sh.slots):
            rotors.append(
                (plane_at(sh, plan, owner, slot), forces[shift], slot * 3, owner * sh.slots + slot)
            )

    for x, _, _, index in rotors:

        @pl.when(x >= 0)
        def _():
            here = [planes[index, q] for q in range(19)]
            force = [jnp.zeros((sh.levels, LANES), F32)] * 3
            for other, source, first, _ in rotors:
                same = (other == x).astype(F32)
                for axis in range(3):
                    at = (first + axis) * sh.levels
                    force[axis] = force[axis] + same * source[at : at + sh.levels, :]
            post = collide(here, force, range(19))
            rows = sh.levels - 1
            for q in range(19):
                dx, dy, dz = DIRS[q]
                value = post[q]
                moved = pltpu.roll(value, dy % LANES, 1) if dy else value
                to = lax.rem(x + (dx + xs), xs) if dx else x
                if dz == 0:
                    out[q, pl.ds(to, sh.levels, stride=xs), :] = moved
                elif dz == 1:
                    out[q, pl.ds(to + xs, rows, stride=xs), :] = moved[:rows]
                else:
                    out[q, pl.ds(to, rows, stride=xs), :] = moved[1:]
                if dz == 1:
                    out[OPPOSITE[q], pl.ds(x + rows * xs, 1), :] = value[rows:]
                elif dz == -1:
                    out[OPPOSITE[q], pl.ds(x, 1), :] = value[:1]

    for q in range(19):
        if q not in SIDEWAYS:
            send(q)

    ghost_force = [jnp.zeros((xs, LANES), F32) for axis in range(3)]
    tall = 2 * sh.levels
    for x, source, first, _ in rotors:
        ghosts = source[sh.section : sh.section + 8, :]
        for axis in range(3):
            k = first + axis
            ghost_force[axis] = ghost_force[axis] + jnp.where(
                xrows == x, ghosts[k : k + 1, :], 0.0
            )
    beyond = unpack_columns(sh, forces[1], forces[sh.tiles - 1], sh.section + 8 + sh.levels)
    ghost = [
        pltpu.roll(beyond[q // per], (LANES - (q % per) * tall) % LANES, 1) for q in range(19)
    ]
    posted = collide(ghost, ghost_force, SIDEWAYS)
    for k, q in enumerate(SIDEWAYS):
        dx, dy, dz = DIRS[q]
        value = posted[q]
        if dx:
            value = pltpu.roll(value, dx % xs, 0)
        for z in range(sh.levels):
            if not 0 <= z - dz < sh.levels:
                continue
            at = pl.ds(z * xs, xs)
            here = out[q, at, :]
            if dy == 1:
                other = pltpu.roll(value, (LANES - 2 * (z - dz)) % LANES, 1)
                here = jnp.where(lanes == 0, other, here)
            else:
                other = pltpu.roll(value, LANES - 2 - 2 * (z - dz), 1)
                here = jnp.where(lanes == LANES - 1, other, here)
            out[q, at, :] = here
        send(q)
    for copy in copies:
        copy.wait()


def do_patch(sh, last, plan, planes, forces, bulk):
    out_shape = [pltpu.VMEM(bulk.shape, F32)]
    if last:
        out_shape.append(jax.ShapeDtypeStruct(bulk.shape, F32))
    return pl.pallas_call(
        lambda *refs: patch_kernel(sh, last, *refs),
        out_shape=out_shape,
        in_specs=[SM] + [VM] * (2 + sh.tiles),
        out_specs=[VM] + [HB] * last,
        scratch_shapes=[
            pltpu.SemaphoreType.DMA((19,)),
        ],
        input_output_aliases={2 + sh.tiles: 0},
        compiler_params=PARAMS,
        name="patch",
    )(plan, planes, *forces, bulk)


def finish_kernel(sh, held, low, high, f_old, f, merged, sem):
    del f_old
    rows = iota((8, LANES), 0)
    copies = []
    for side, dirs, edge in ((0, PLUS, low), (1, MINUS, high)):
        at_row = 0 if side == 0 else 7
        first = 0 if side == 0 else sh.xs - 8
        for k, q in enumerate(dirs):
            index = side * len(PLUS) + k
            for z in range(sh.levels):
                value = held[q, z * sh.xs + first : z * sh.xs + first + 8, :]
                blocked = (DIRS[q][2] == 1 and z == 0) or (
                    DIRS[q][2] == -1 and z == sh.levels - 1
                )
                if not blocked:
                    value = jnp.where(rows == at_row, edge[k, z : z + 1, :], value)
                merged[index, z] = value
            copy = pltpu.make_async_copy(
                merged.at[index], f.at[q, :, first : first + 8, :], sem.at[index]
            )
            copy.start()
            copies.append(copy)
    for copy in copies:
        copy.wait()


def finish(sh, held, f, edges):
    f = f.reshape(19, sh.levels, sh.xs, LANES)
    return pl.pallas_call(
        lambda *refs: finish_kernel(sh, *refs),
        out_shape=jax.ShapeDtypeStruct(f.shape, F32),
        in_specs=[VM, VM, VM, HB],
        out_specs=HB,
        scratch_shapes=[
            pltpu.VMEM((2 * len(PLUS), sh.levels, 8, LANES), F32),
            pltpu.SemaphoreType.DMA((2 * len(PLUS),)),
        ],
        input_output_aliases={3: 0},
        compiler_params=PARAMS,
        name="finish",
    )(held, *edges, f)


def by_group(sh, x):
    head = x.shape[:-2]
    x = x.reshape(*head, sh.slots, sh.groups, LANES)
    return jnp.swapaxes(x, -3, -2).reshape(*head, sh.slots * sh.groups, LANES)


def by_slot(sh, x):
    head = x.shape[:-2]
    x = x.reshape(*head, sh.groups, sh.slots, LANES)
    return jnp.swapaxes(x, -3, -2).reshape(*head, sh.slots, sh.markers)


def shifted(x, axis, by):
    count = lax.axis_size(axis)
    return lax.ppermute(x, axis, [(i, (i + by) % count) for i in range(count)])


def local(
    f_in,
    rotor_place,
    marker_cell,
    pitch_phase,
    blade_area,
    blade_twist,
    blade_speed,
    blade_angle,
    filt_in,
):
    sh = Shape(f_in, rotor_place, marker_cell, pitch_phase, filt_in)
    area, twist, speed, angle = [
        by_group(sh, x[0, 0]) for x in (blade_area, blade_twist, blade_speed, blade_angle)
    ]
    filt = by_group(sh, jnp.swapaxes(filt_in[0, 0], 0, 1))
    plan, blades, f = start(sh, rotor_place, pitch_phase, twist, angle, f_in)
    edges = ()
    for step in range(sh.steps):
        last = step == sh.steps - 1
        if step == 0:
            columns = make_columns(sh, plan, f, edges)
            sections, planes = make_sections(sh, plan, f, edges, columns)
            tables = make_tables(sh, plan, marker_cell, in_vmem(sections[0]))
        else:
            sections, planes = make_sections(sh, plan, f, edges, ())
            columns = make_columns(sh, plan, f, edges)
        sections = [sections[0]] + [
            shifted(sections[by], "gy", by) for by in range(1, sh.tiles)
        ]
        filt, loads, forces = do_markers(
            sh,
            step,
            plan,
            tables,
            (area, speed),
            blades,
            filt,
            columns,
            [in_vmem(section) for section in sections],
        )
        forces = [forces[0]] + [shifted(forces[by], "gy", by) for by in range(1, sh.tiles)]
        forces = [in_vmem(force) for force in forces]
        bulk = do_bulk(sh, last, plan, f, edges, loads, filt)
        if last:
            loads_out, filt_out = bulk[1:]
        bulk = in_vmem(bulk[0])
        sent = make_edges(sh, plan, f, edges, forces, bulk)
        done = do_patch(sh, last, plan, planes, forces, bulk)
        edges = (in_vmem(shifted(sent[0], "gx", 1)), in_vmem(shifted(sent[1], "gx", -1)))
        f = in_vmem(done[0])
    f = finish(sh, f, done[1], edges)
    loads_out, filt_out = [
        jnp.swapaxes(by_slot(sh, x), 0, 1)[None, None] for x in (loads_out, filt_out)
    ]
    return f, loads_out, filt_out


def solution(mesh):
    in_specs = (
        P(None, None, "gx", "gy"),
        P(),
        P(),
        P(),
        P("gx", "gy", None, None),
        P("gx", "gy", None, None),
        P("gx", "gy", None, None),
        P("gx", "gy", None, None),
        P("gx", "gy", None, None, None),
    )
    out_specs = (
        P(None, None, "gx", "gy"),
        P("gx", "gy", None, None, None),
        P("gx", "gy", None, None, None),
    )
    return jax.shard_map(local, mesh=mesh, in_specs=in_specs, out_specs=out_specs, check_vma=False)
```
